32 devices in a mesh: leaf: 8 (over z, y), sep: 4 (over x, core).
Axes of the slice: x: 2, y: 2, z: 4, core: 2. Of those that a mesh axis runs over, the one named last changes fastest.
Arguments:
- leaf_source: float32 [8, 640, 256], P('leaf', 'sep'), may hold values from -6 to 6
- leaf_inverse: float32 [8, 640, 640], P('leaf', 'sep'), as said below
- leaf_update: float32 [8, 384, 640], P('leaf', None, 'sep'), as said below
- row_lists: int32 [8, 384], P('leaf'), may hold values from 0 to 255
- row_counts: int32 [8, 3], P('leaf'), may hold values from 1 to 128, as said below
- separator_source: float32 [8, 256, 256], P('leaf', 'sep'), may hold values from -6 to 6
- separator_inverse: float32 [8, 256, 256], P('leaf'), as said below
- separator_coupling: float32 [8, 256, 256], P('leaf'), may hold values from -0.1875 to 0.1875
Outputs:
- leaf_solution: float32 [8, 640, 256], P('leaf', 'sep')
- separator_solution: float32 [8, 256, 256], P('leaf', 'sep')
The draws below stay inside these ranges and needn't reach their ends.
Inputs may be any that keep to these rules, and one draw needn't show every extreme that they name: `leaf_inverse`: each leaf's block is lower triangular, zero above the diagonal, with diagonal entries between 0.6 and 1.4. `separator_inverse`: each block is lower triangular, zero above the diagonal, with diagonal entries between 0.6 and 1.4. `leaf_update`: row r of a leaf's block belongs to the leaf's ancestor of level 1 + r // 128. `row_lists`: entry r names a row of the leaf's ancestor of level 1 + r // 128. `row_counts`: at every level some leaf has 128 live rows.
All inputs are finite; a program needn't handle non-finite values.
Results may differ from the reference program's by a relative error of at most 0.00011.
Values sent between devices are 32-bit elements; how exact they have to be, the bound alone decides.
No kernel may reach another device: no remote copies, remote signals or barrier semaphores. Data moves between devices by JAX's collectives and lax.ppermute only.
A program may use at most 64 MiB of HBM per device.

```python
import jax
import jax.numpy as jnp
import numpy as np
from jax import lax

NRHS = 256
LR = 640
W = 256
P_SIZE = 128
NLEAF = 8
LEV = 3
UROWS = 384


def triangle(key, order, spread):
    entries = jax.random.normal(key, (NLEAF, order, order), jnp.float32) * spread
    diagonal = jax.random.uniform(jax.random.fold_in(key, 11), (NLEAF, order, 1), jnp.float32, 0.6, 1.4)
    row_ids = lax.broadcasted_iota(jnp.int32, (order, order), 0)
    col_ids = lax.broadcasted_iota(jnp.int32, (order, order), 1)
    return jnp.where(row_ids > col_ids, entries, jnp.where(row_ids == col_ids, diagonal, 0.0))


def draw_leaf_inverse(key, part):
    return triangle(key, LR, LR ** (-0.5))


def draw_separator_inverse(key, part):
    return triangle(key, W, (0.5 / W) ** 0.5)


def draw_leaf_update(key, part):
    entries = jax.random.normal(key, (NLEAF, UROWS, LR), jnp.float32)
    height_index = (lax.broadcasted_iota(jnp.int32, (UROWS, 1), 0) // P_SIZE).astype(jnp.float32)
    return entries * jnp.exp2(-0.5 * height_index) * LR ** (-0.5)


def draw_row_counts(key, part):
    counts = jax.random.randint(key, (NLEAF, LEV), 1, P_SIZE + 1)
    chosen = jax.random.randint(jax.random.fold_in(key, 7), (LEV,), 0, NLEAF)
    return jnp.where(jnp.arange(NLEAF)[:, None] == chosen[None, :], P_SIZE, counts).astype(jnp.int32)


def plant(result, key, low, top_value):
    dims = result.shape
    place = [jax.random.randint(jax.random.fold_in(key, axis), (), 0, dims[axis]) for axis in range(len(dims))]
    result = result.at[tuple(place)].set(low)
    longest = dims.index(max(dims))
    place[longest] = (place[longest] + 1) % dims[longest]
    return result.at[tuple(place)].set(top_value)


def level_of(stream_key, shape, cuts, low, top_value):
    def one(position, blocks):
        draws = jax.random.uniform(jax.random.fold_in(jax.random.fold_in(stream_key, 6), position), (blocks,), jnp.float32, low / len(cuts), top_value / len(cuts))
        return jnp.repeat(jnp.exp(draws), shape[position] // blocks).reshape((-1,) + (1,) * (len(shape) - position - 1))

    level = one(*cuts[0])
    for cut in cuts[1:]:
        level = level * one(*cut)
    return level


def centred(own_key, dims, width, limit, split=(), held_as=jnp.bfloat16):
    array = width * jax.random.normal(own_key, dims, jnp.float32)
    if split:
        array = array * level_of(own_key, dims, split, -0.22, 0.18)
    return jnp.clip(array, -limit, limit).astype(held_as)


def setup_inputs(seed: int = 0) -> dict:
    streams_of = jax.random.split(jax.random.key(seed), 9)
    leaf_source = centred(streams_of[0], (NLEAF, LR, NRHS), 1.0, 6.0, ((0, 8), (1, 4)), jnp.float32)
    leaf_inverse = draw_leaf_inverse(jax.random.fold_in(streams_of[8], 71), 0)
    leaf_update = draw_leaf_update(jax.random.fold_in(streams_of[8], 71), 0)
    row_lists = plant(jax.random.randint(streams_of[3], (NLEAF, UROWS), 0, W), jax.random.fold_in(streams_of[3], 1), 0, W - 1).astype(jnp.int32)
    row_counts = draw_row_counts(jax.random.fold_in(streams_of[8], 71), 0)
    separator_source = centred(streams_of[5], (NLEAF, W, NRHS), 1.0, 6.0, ((0, 8), (1, 4)), jnp.float32)
    separator_inverse = draw_separator_inverse(jax.random.fold_in(streams_of[8], 71), 0)
    separator_coupling = centred(streams_of[7], (NLEAF, W, W), (4 * W) ** -0.5, 0.1875, ((0, 8),), jnp.float32)
    return {"leaf_source": leaf_source, "leaf_inverse": leaf_inverse, "leaf_update": leaf_update, "row_lists": row_lists, "row_counts": row_counts, "separator_source": separator_source, "separator_inverse": separator_inverse, "separator_coupling": separator_coupling}


highest = lax.Precision.HIGHEST


def reference(leaf_source, leaf_inverse, leaf_update, row_lists, row_counts, separator_source, separator_inverse, separator_coupling):
    leaf_y = jnp.einsum("lij,ljn->lin", leaf_inverse, leaf_source, precision=highest)
    slot_index = np.arange(UROWS) % P_SIZE
    block_index = np.arange(UROWS) // P_SIZE
    live_rows = slot_index[None, :] < row_counts[:, block_index]
    update_terms = jnp.einsum("lrj,ljn->lrn", leaf_update, leaf_y, precision=highest)
    update_terms = jnp.where(live_rows[:, :, None], update_terms, 0.0)
    targets = row_lists.reshape(NLEAF, LEV, P_SIZE)
    picker = (jnp.arange(W, dtype=jnp.int32)[None, None, :, None] == targets[:, :, None, :]).astype(jnp.float32)
    densified = jnp.einsum("lkwp,lkpn->lkwn", picker, update_terms.reshape(NLEAF, LEV, P_SIZE, NRHS), precision=highest)
    solved_levels = []
    previous_owners = None
    for height in range(1, LEV + 1):
        groups = NLEAF >> height
        owners = np.arange(groups) * 2 ** height + 2 ** (height - 1)
        gathered = densified[:, height - 1].reshape(groups, 2 ** height, W, NRHS).sum(axis=1)
        residual = separator_source[owners] - gathered
        if height > 1:
            pushed = jnp.einsum("gvw,gwn->gvn", separator_coupling[previous_owners], solved_levels[-1], precision=highest)
            residual = residual - pushed.reshape(groups, 2, W, NRHS).sum(axis=1)
        solved_levels.append(jnp.einsum("gvw,gwn->gvn", separator_inverse[owners], residual, precision=highest))
        previous_owners = owners
    separator_solution = jnp.zeros((NLEAF, W, NRHS), jnp.float32)
    solution_levels = [None] * LEV
    above_x = None
    for height in range(LEV, 0, -1):
        owners = np.arange(NLEAF >> height) * 2 ** height + 2 ** (height - 1)
        target = solved_levels[height - 1]
        if height < LEV:
            parents = jnp.repeat(above_x, 2, axis=0)
            target = target - jnp.einsum("gvw,gvn->gwn", separator_coupling[owners], parents, precision=highest)
        above_x = jnp.einsum("gvw,gvn->gwn", separator_inverse[owners], target, precision=highest)
        solution_levels[height - 1] = above_x
        separator_solution = separator_solution.at[owners].set(above_x)
    ancestors = jnp.stack([solution_levels[height - 1][np.arange(NLEAF) >> height] for height in range(1, LEV + 1)], axis=1)
    picked = jnp.einsum("lkwp,lkwn->lkpn", picker, ancestors, precision=highest).reshape(NLEAF, UROWS, NRHS)
    picked = jnp.where(live_rows[:, :, None], picked, 0.0)
    leaf_w = leaf_y - jnp.einsum("lrj,lrn->ljn", leaf_update, picked, precision=highest)
    leaf_solution = jnp.einsum("lij,lin->ljn", leaf_inverse, leaf_w, precision=highest)
    return leaf_solution, separator_solution
```

```python
import jax
import jax.numpy as jnp
from jax import lax
from jax.sharding import PartitionSpec as P

precise = lax.Precision.HIGH
axes = ("leaf", "sep")


def contract(left, right, left_dim, right_dim):
    return lax.dot_general(
        left,
        right,
        (((left_dim,), (right_dim,)), ((), ())),
        precision=precise,
        preferred_element_type=jnp.float32,
    )


def swap(payload, leaf_flip, sep_flip):
    leaves, seps = lax.axis_size("leaf"), lax.axis_size("sep")
    pairs = [
        (leaf * seps + sep, (leaf ^ leaf_flip) * seps + (sep ^ sep_flip))
        for leaf in range(leaves)
        for sep in range(seps)
    ]
    return lax.ppermute(payload, axes, pairs)


def pick(array, index):
    return lax.dynamic_index_in_dim(array, index, 0, keepdims=False)


def per_device(
    leaf_source,
    leaf_inverse,
    leaf_update,
    row_lists,
    row_counts,
    separator_source,
    separator_inverse,
    separator_coupling,
):
    depth = row_counts.shape[1]
    leaf = lax.axis_index("leaf")
    sep = lax.axis_index("sep")
    odd = leaf % 2
    far_bit = sep // 2
    near_bit = sep % 2
    source = leaf_source[0]
    inverse = leaf_inverse[0]
    update = leaf_update[0]
    rows, columns = source.shape
    updates = update.shape[0]
    capacity = updates // depth
    order = separator_inverse.shape[1]
    quarter = separator_source.shape[1]
    block = columns // 8

    own_inverse = separator_inverse[0]
    down = contract(separator_coupling[0], own_inverse, 1, 0)
    square = contract(own_inverse, own_inverse, 0, 0)

    far = swap(source, 0, 2)
    near = swap(source, 0, 1)
    far_near = swap(far, 0, 1)

    def inverse_part(flip):
        return lax.dynamic_slice_in_dim(inverse, (sep ^ flip) * rows, rows, 1)

    leaf_y = contract(inverse_part(0), source, 1, 0) + contract(inverse_part(1), near, 1, 0)
    leaf_y = leaf_y + contract(inverse_part(2), far, 1, 0)
    leaf_y = leaf_y + contract(inverse_part(3), far_near, 1, 0)

    slot_index = jnp.arange(updates) % capacity
    live = slot_index < jnp.repeat(row_counts[0], capacity)
    listed = jnp.where(live, row_lists[0], -1).astype(jnp.float32)
    list_rows = -(-updates // (8 * order)) * 8
    listed_block = jnp.pad(listed, (0, list_rows * order - updates)).reshape(list_rows, order)
    carry = jnp.where(near_bit == 0, down, square)
    received = swap(jnp.concatenate([carry, listed_block], 0), 1, 0)
    listed_other = received[order:].reshape(-1)[:updates]
    received = received[:order]
    halves = [jnp.where(odd == 1, carry, received)]
    carry = jnp.where(odd == 1, received, carry)
    for level in range(2, depth + 1):
        received = swap(carry, 2 ** (level - 1), 0)
        upper = leaf // 2 ** (level - 1) % 2 == 1
        halves.append(jnp.where(upper, carry, received))
        carry = jnp.where(upper, received, carry)
    downs, squares = [], []
    for half in halves:
        other = swap(half, 0, 1)
        downs.append(jnp.where(near_bit == 0, half, other))
        squares.append(jnp.where(near_bit == 0, other, half))

    level_base = jnp.repeat(jnp.arange(depth) * order, capacity)
    place = jnp.arange(depth * order)[:, None]

    def one_hot(lists):
        target = jnp.where(lists >= 0, lists.astype(jnp.int32) + level_base, -1)
        return (place == target[None, :]).astype(jnp.float32)

    hot = one_hot(listed)
    hot_other = one_hot(listed_other)

    own_rows = jnp.transpose(separator_source[0]).reshape(2, columns // 2, quarter)
    kept = pick(own_rows, near_bit)
    passed = swap(pick(own_rows, 1 - near_bit), 0, 1)
    own_pair = jnp.where(
        near_bit == 0,
        jnp.concatenate([kept, passed], 1),
        jnp.concatenate([passed, kept], 1),
    )

    terms = contract(leaf_y, update, 0, 1).reshape(2, columns // 2, updates)
    terms = pick(terms, near_bit) + swap(pick(terms, 1 - near_bit), 0, 1)
    message = jnp.concatenate([terms, own_pair], 1).reshape(4, block, updates + 2 * quarter)
    here = 2 * odd + far_bit
    by_both = swap(pick(message, here ^ 3), 1, 2)
    by_far = swap(pick(message, here ^ 1), 0, 2)
    by_odd = swap(pick(message, here ^ 2), 1, 0)
    mine = pick(message, here)

    def joined(first, second):
        total = first[:, :updates] + second[:, :updates]
        one, two = first[:, updates:], second[:, updates:]
        ordered = jnp.where(
            far_bit == 0, jnp.concatenate([one, two], 1), jnp.concatenate([two, one], 1)
        )
        return total, ordered

    total, own_source = joined(mine, by_far)
    total_other, other_source = joined(by_odd, by_both)
    gathered = contract(total, hot, 1, 1) + contract(total_other, hot_other, 1, 1)
    odd_source = jnp.where(odd == 1, own_source, other_source)
    even_source = jnp.where(odd == 1, other_source, own_source)
    even_leaf = leaf - odd

    def is_level(index, level):
        return index % 2**level == 2 ** (level - 1)

    slots = [odd_source - gathered[:, :order]]
    for level in range(2, depth + 1):
        piece = gathered[:, (level - 1) * order : level * order]
        slots.append(jnp.where(is_level(even_leaf, level), even_source, 0.0) - piece)

    partial = []
    for level in range(1, depth + 1):
        if level > 1:
            stacked = jnp.concatenate(slots[level - 1 :], 1)
            stacked = stacked + swap(stacked, 2 ** (level - 1), 0)
            for upper in range(level, depth + 1):
                start = (upper - level) * order
                slots[upper - 1] = stacked[:, start : start + order]
        residual = slots[level - 1]
        partial.append(contract(residual, squares[level - 1], 1, 0))
        if level < depth:
            slots[level] = slots[level] - contract(residual, downs[level - 1], 1, 1)

    solved = [None] * depth
    solved[depth - 1] = partial[depth - 1]
    for level in range(depth - 1, 0, -1):
        solved[level - 1] = partial[level - 1] - contract(solved[level], downs[level - 1], 1, 0)
    every = jnp.concatenate(solved, 1)
    even_solved = jnp.zeros_like(solved[0])
    for level in range(2, depth + 1):
        even_solved = jnp.where(is_level(even_leaf, level), solved[level - 1], even_solved)
    own_solved = jnp.where(odd == 1, solved[0], even_solved).reshape(block, 2, 2 * quarter)
    other_solved = jnp.where(odd == 1, even_solved, solved[0]).reshape(block, 2, 2 * quarter)

    def rows_of(array, bit):
        return lax.dynamic_index_in_dim(array, bit, 1, keepdims=False)

    picked = contract(every, hot, 1, 0)
    picked_other = contract(every, hot_other, 1, 0)
    to_both = jnp.concatenate([picked_other, rows_of(other_solved, 1 - far_bit)], 1)
    to_far = jnp.concatenate([picked, rows_of(own_solved, 1 - far_bit)], 1)
    to_odd = jnp.concatenate([picked_other, rows_of(other_solved, far_bit)], 1)
    stay = jnp.concatenate([picked, rows_of(own_solved, far_bit)], 1)
    both = swap(to_both, 1, 2)
    beyond = swap(to_far, 0, 2)
    beside = swap(to_odd, 1, 0)
    group = jnp.stack([stay, beyond, beside, both])
    group = jnp.where(far_bit == 0, group, group[jnp.array([1, 0, 3, 2])])
    group = jnp.where(odd == 0, group, group[jnp.array([2, 3, 0, 1])])
    group = group.reshape(columns // 2, updates + 2 * quarter)
    group_other = swap(group, 0, 1)

    parts = jnp.concatenate(
        [contract(inverse, update, 0, 1), contract(inverse, leaf_y, 0, 0)], 1
    ).reshape(2, 2, rows, updates + columns)
    parts = lax.dynamic_index_in_dim(parts, near_bit, 1, keepdims=False) + swap(
        lax.dynamic_index_in_dim(parts, 1 - near_bit, 1, keepdims=False), 0, 1
    )
    parts = pick(parts, far_bit) + swap(pick(parts, 1 - far_bit), 0, 2)
    base = parts[:, updates:]
    last = jnp.concatenate(
        [
            jnp.pad(-parts[:, :updates], ((0, 0), (0, 2 * quarter))),
            (
                jnp.arange(updates + 2 * quarter)[None, :]
                == updates + near_bit * quarter + jnp.arange(quarter)[:, None]
            ).astype(jnp.float32),
        ],
        0,
    )
    ours = contract(last, group, 1, 1)
    theirs = contract(last, group_other, 1, 1)
    out = jnp.where(
        near_bit == 0,
        jnp.concatenate([ours, theirs], 1),
        jnp.concatenate([theirs, ours], 1),
    )
    return ((base + out[:rows])[None], out[rows:][None])


def solution(mesh):
    placed = (
        P("leaf", "sep", None),
        P("leaf", "sep", None),
        P("leaf", None, "sep"),
        P("leaf", None),
        P("leaf", None),
        P("leaf", "sep", None),
        P("leaf", None, None),
        P("leaf", None, None),
    )
    return jax.shard_map(
        per_device,
        mesh=mesh,
        in_specs=placed,
        out_specs=(P("leaf", "sep", None), P("leaf", "sep", None)),
        check_vma=False,
    )
```

```python
import functools

import jax
import jax.numpy as jnp
from jax import lax
from jax.experimental import pallas as pl
from jax.experimental.pallas import tpu as pltpu
from jax.sharding import PartitionSpec as P

axes = ("leaf", "sep")
f32 = jnp.float32


def swap(payload, leaf_flip, sep_flip, senders=None):
    leaves, seps = lax.axis_size("leaf"), lax.axis_size("sep")
    pairs = [
        (leaf * seps + sep, (leaf ^ leaf_flip) * seps + (sep ^ sep_flip))
        for leaf in range(leaves)
        for sep in range(seps)
        if senders is None or senders(leaf, sep)
    ]
    return lax.ppermute(payload, axes, pairs)


def after(*arrays):
    return lax.optimization_barrier(arrays)


def dot(left, right, left_dim=1, right_dim=0):
    return lax.dot_general(
        left,
        right,
        (((left_dim,), (right_dim,)), ((), ())),
        precision=lax.Precision.HIGHEST,
        preferred_element_type=f32,
    )


def hot_dot(left, right, right_dim):
    high = left.astype(jnp.bfloat16)
    rest = left - high.astype(f32)
    middle = rest.astype(jnp.bfloat16)
    low = (rest - middle.astype(f32)).astype(jnp.bfloat16)
    pieces = jnp.concatenate([high, middle, low], 0)
    out = lax.dot_general(
        pieces, right, (((1,), (right_dim,)), ((), ())), preferred_element_type=f32
    )
    size = left.shape[0]
    return out[:size] + (out[size : 2 * size] + out[2 * size :])


def stage(body, shapes, *operands, scratch=()):
    vmem = pl.BlockSpec(memory_space=pltpu.VMEM)
    return pl.pallas_call(
        body,
        out_shape=[
            jax.ShapeDtypeStruct(shape, f32) if isinstance(shape, tuple) else shape
            for shape in shapes
        ],
        in_specs=[vmem] * len(operands),
        out_specs=[vmem] * len(shapes),
        scratch_shapes=[pltpu.VMEM(shape, f32) for shape in scratch],
        compiler_params=pltpu.CompilerParams(vmem_limit_bytes=16 * 2**20),
        cost_estimate=pl.CostEstimate(flops=1000, bytes_accessed=1000, transcendentals=0),
    )(*operands)


def place():
    leaf, sep = lax.axis_index("leaf"), lax.axis_index("sep")
    return leaf, sep, lax.rem(leaf, 2), sep // 2, lax.rem(sep, 2)


def per_device(
    leaf_source,
    leaf_inverse,
    leaf_update,
    row_lists,
    row_counts,
    separator_source,
    separator_inverse,
    separator_coupling,
):
    depth = row_counts.shape[1]
    source = leaf_source[0]
    inverse = leaf_inverse[0]
    update = leaf_update[0]
    rows, columns = source.shape
    updates = update.shape[0]
    capacity = updates // depth
    order = separator_inverse.shape[1]
    quarter = separator_source.shape[1]
    half = columns // 2
    block = columns // 8
    width = updates + 2 * quarter
    list_rows = -(-depth // 8) * 8
    leaves = lax.axis_size("leaf")

    def at(index, size):
        return pl.ds(pl.multiple_of(index * size, size), size)

    far = swap(source, 0, 2)
    near = swap(source, 0, 1)

    def operators(coupling_ref, inverse_ref, lists_ref, counts_ref, out_ref):
        near_bit = place()[4]

        @pl.when(near_bit == 0)
        def _():
            out_ref[:order] = dot(coupling_ref[...], inverse_ref[...])

        @pl.when(near_bit == 1)
        def _():
            out_ref[:order] = dot(inverse_ref[...], inverse_ref[...], 0, 0)

        out_ref[order:] = jnp.zeros((list_rows, order), f32)
        slot = lax.broadcasted_iota(jnp.int32, (1, capacity), 1)
        for level in range(depth):
            lists = lists_ref[:, level * capacity : (level + 1) * capacity]
            live = slot < counts_ref[:, level : level + 1]
            out_ref[order + level : order + level + 1, :capacity] = jnp.where(
                live, lists, -1
            ).astype(f32)

    (payload,) = stage(
        operators,
        [(order + list_rows, order)],
        separator_coupling[0],
        separator_inverse[0],
        row_lists,
        row_counts,
    )
    received = swap(payload, 1, 0)

    def own_part(inverse_ref, source_ref, near_ref, rows_ref, y_ref, far_ref, keep_ref, pass_ref, full):
        _, sep, _, far_bit, near_bit = place()
        full[at(near_bit, rows)] = source_ref[...]
        full[at(1 - near_bit, rows)] = near_ref[...]
        first, second = inverse_ref[:, : 2 * rows], inverse_ref[:, 2 * rows :]
        y_ref[...] = dot(jnp.where(far_bit == 0, first, second), full[...])
        far_ref[...] = jnp.where(far_bit == 0, second, first)
        turned = jnp.transpose(rows_ref[...])
        keep_ref[...] = jnp.where(near_bit == 0, turned[:half], turned[half:])
        pass_ref[...] = jnp.where(near_bit == 0, turned[half:], turned[:half])

    payload, near = after(payload, near)
    own_y, inverse_far, rows_keep, rows_pass = stage(
        own_part,
        [(rows, columns), (rows, 2 * rows), (half, quarter), (half, quarter)],
        inverse,
        source,
        near,
        separator_source[0],
        scratch=[(2 * rows, columns)],
    )
    rows_near = swap(rows_pass, 0, 1)

    far, own_y = after(far, own_y)
    far_near = swap(far, 0, 1)

    def leaf_part(own_ref, inverse_ref, far_ref, far_near_ref, update_ref, y_ref, keep_ref, pass_ref, full):
        near_bit = place()[4]
        full[at(near_bit, rows)] = far_ref[...]
        full[at(1 - near_bit, rows)] = far_near_ref[...]
        leaf_y = own_ref[...] + dot(inverse_ref[...], full[...])
        y_ref[...] = leaf_y
        keep = jnp.where(near_bit == 0, leaf_y[:, :half], leaf_y[:, half:])
        passed = jnp.where(near_bit == 0, leaf_y[:, half:], leaf_y[:, :half])
        pass_ref[...] = dot(passed, update_ref[...], 0, 1)
        keep_ref[...] = dot(keep, update_ref[...], 0, 1)

    leaf_y, terms_keep, terms_pass = stage(
        leaf_part,
        [(rows, columns), (half, updates), (half, updates)],
        own_y,
        inverse_far,
        far,
        far_near,
        update,
        scratch=[(2 * rows, columns)],
    )
    terms_near = swap(terms_pass, 0, 1)

    def forward(level):
        def body(carry_ref, received_ref, half_ref, next_ref):
            upper = lax.rem(place()[0] // 2 ** (level - 1), 2) == 1
            carry, received = carry_ref[:order], received_ref[:order]
            half_ref[...] = jnp.where(upper, carry, received)
            next_ref[...] = jnp.where(upper, received, carry)

        return body

    received, terms_keep, rows_near = after(received, terms_keep, rows_near)
    halves, halves_near = [], []
    new_half, carry = stage(forward(1), [(order, order)] * 2, payload, received)
    halves.append(new_half)
    reached = swap(carry, 2, 0)
    halves_near.append(swap(new_half, 0, 1))

    def messages(keep_ref, near_ref, rows_keep_ref, rows_near_ref, *out_refs):
        _, _, odd, far_bit, near_bit = place()
        for flip, out_ref in enumerate(out_refs):
            part = at((2 * odd + far_bit) ^ flip, block)
            out_ref[:, :updates] = keep_ref[part] + near_ref[part]
            kept, passed = rows_keep_ref[part], rows_near_ref[part]
            out_ref[:, updates:] = jnp.where(
                near_bit == 0,
                jnp.concatenate([kept, passed], 1),
                jnp.concatenate([passed, kept], 1),
            )

    mine, to_far, to_odd, to_both = stage(
        messages, [(block, width)] * 4, terms_keep, terms_near, rows_keep, rows_near
    )
    by_both = swap(to_both, 1, 2)
    by_far = swap(to_far, 0, 2)
    by_odd = swap(to_odd, 1, 0)

    def one_hots(own_ref, other_ref, hot_ref):
        rows_of_node = lax.broadcasted_iota(jnp.int32, (order, capacity), 0)
        for level in range(depth):
            for index, ref in enumerate((own_ref, other_ref)):
                lists = ref[order + level : order + level + 1, :capacity].astype(jnp.int32)
                hot = jnp.where(rows_of_node == lists, 1.0, 0.0).astype(jnp.bfloat16)
                hot_ref[level, :, index * capacity : (index + 1) * capacity] = hot

    payload, received, mine = after(payload, received, mine)
    (hots,) = stage(
        one_hots,
        [jax.ShapeDtypeStruct((depth, order, 2 * capacity), jnp.bfloat16)],
        payload,
        received,
    )

    def transposed(inverse_ref, update_ref, y_ref, self_ref, near_ref, work):
        sep = place()[1]
        work[:, :updates] = dot(inverse_ref[...], update_ref[...], 0, 1)
        work[:, updates:] = dot(inverse_ref[...], y_ref[...], 0, 0)
        self_ref[:rows] = work[at(sep, rows)]
        self_ref[rows:] = work[at(sep ^ 2, rows)]
        near_ref[:rows] = work[at(sep ^ 1, rows)]
        near_ref[rows:] = work[at(sep ^ 3, rows)]

    inverse_again, hots = after(inverse, hots)
    self_part, near_part = stage(
        transposed,
        [(2 * rows, updates + columns)] * 2,
        inverse_again,
        update,
        leaf_y,
        scratch=[(inverse.shape[1], updates + columns)],
    )
    near_sum = swap(near_part, 0, 1)

    def root_sent(carry):
        start, size = leaves // 2, leaves // 4
        return [
            swap(carry, flip, 0, lambda leaf, sep: leaf // size == 2 and sep % 2 == 1)
            for flip in (start, start + size)
        ]

    if depth == 3:
        by_root = root_sent(carry)

    by_both, by_far, by_odd, self_part, halves_near[0] = after(
        by_both, by_far, by_odd, self_part, halves_near[0]
    )

    def first_level(mine_ref, far_ref, odd_ref, both_ref, hot_ref, half_ref, other_ref, residual_ref, up_ref):
        leaf, _, odd, far_bit, near_bit = place()

        def joined(one, two):
            first, second = one[:, updates:], two[:, updates:]
            ordered = jnp.where(
                far_bit == 0,
                jnp.concatenate([first, second], 1),
                jnp.concatenate([second, first], 1),
            )
            return one[:, :updates] + two[:, :updates], ordered

        total, own_source = joined(mine_ref[...], far_ref[...])
        total_other, other_source = joined(odd_ref[...], both_ref[...])
        odd_source = jnp.where(odd == 1, own_source, other_source)
        even_source = jnp.where(odd == 1, other_source, own_source)
        even_leaf = leaf - odd

        def gathered(level):
            part = slice((level - 1) * capacity, level * capacity)
            both = jnp.concatenate([total[:, part], total_other[:, part]], 1)
            return hot_dot(both, hot_ref[level - 1], 1)

        down = jnp.where(near_bit == 0, half_ref[...], other_ref[...])
        residual = odd_source - gathered(1)
        residual_ref[...] = residual
        for level in range(2, depth + 1):
            here = lax.rem(even_leaf, 2**level) == 2 ** (level - 1)
            slot = jnp.where(here, even_source, 0.0) - gathered(level)
            if level == 2:
                slot = slot - dot(residual, down, 1, 1)
            up_ref[:, (level - 2) * order : (level - 1) * order] = slot

    residual, going_up = stage(
        first_level,
        [(block, order), (block, (depth - 1) * order)],
        mine,
        by_far,
        by_odd,
        by_both,
        hots,
        halves[0],
        halves_near[0],
    )
    residuals = [residual]

    def next_level(level):
        def body(up_ref, partner_ref, half_ref, other_ref, residual_ref, next_ref):
            near_bit = place()[4]
            total = up_ref[...] + partner_ref[...]
            residual = total[:, :order]
            residual_ref[...] = residual
            down = jnp.where(near_bit == 0, half_ref[...], other_ref[...])
            next_ref[:, :order] = total[:, order : 2 * order] - dot(residual, down, 1, 1)
            if level + 1 < depth:
                next_ref[:, order:] = total[:, 2 * order :]

        return body

    for level in range(2, depth):
        partner = swap(going_up, 2 ** (level - 1), 0)
        reached, going_up, self_part = after(reached, going_up, self_part)
        new_half, carry = stage(forward(level), [(order, order)] * 2, carry, reached)
        halves.append(new_half)
        halves_near.append(swap(new_half, 0, 1))
        if level + 1 < depth:
            reached = swap(carry, 2**level, 0)
        if level == depth - 2:
            by_root = root_sent(carry)
        if level == 2:

            def summed(self_ref, near_ref, own_ref, far_ref):
                own_ref[...] = self_ref[:rows] + near_ref[:rows]
                far_ref[...] = self_ref[rows:] + near_ref[rows:]

            own_sum, far_sum = stage(
                summed, [(rows, updates + columns)] * 2, self_part, near_sum
            )
            from_far = swap(far_sum, 0, 2)
        partner, halves_near[-1], own_sum = after(partner, halves_near[-1], own_sum)
        residual, going_up = stage(
            next_level(level),
            [(block, order), (block, (depth - level) * order)],
            going_up,
            partner,
            halves[-1],
            halves_near[-1],
        )
        residuals.append(residual)
    partner = swap(going_up, 2 ** (depth - 1), 0)

    def beside(*refs):
        near_bit = place()[4]
        out_ref, refs = refs[-1], refs[:-1]
        count = depth - 1
        for level in range(count):
            square = jnp.where(near_bit == 0, refs[2 * count + level][...], refs[count + level][...])
            out_ref[:, level * order : (level + 1) * order] = dot(refs[level][...], square)

    residuals[0], going_up, carry = after(residuals[0], going_up, carry)
    (partial,) = stage(
        beside, [(block, (depth - 1) * order)], *residuals, *halves, *halves_near
    )

    def root_square(carry_ref, *refs):
        leaf = place()[0]
        refs, out_ref = refs[:-1], refs[-1]
        part = leaf // (leaves // 4)
        out_ref[...] = carry_ref[...]
        for index, ref in enumerate(refs):
            @pl.when(part == index)
            def _(ref=ref):
                out_ref[...] = ref[...]

    by_root[0], partial = after(by_root[0], partial)
    (root,) = stage(root_square, [(order, order)], carry, *by_root)
    root_near = swap(root, 0, 1)
    partner, root_near, from_far = after(partner, root_near, from_far)

    def way_down(*refs):
        leaf, _, odd, far_bit, near_bit = place()
        up_ref, partner_ref, partial_ref, hot_ref, root_ref, root_near_ref = refs[:6]
        down_refs, out_refs = refs[6 : 6 + 2 * (depth - 1)], refs[6 + 2 * (depth - 1) :]
        square = jnp.where(near_bit == 1, root_ref[...], root_near_ref[...])
        solved = [None] * depth
        solved[-1] = dot(up_ref[...] + partner_ref[...], square)
        for level in range(depth - 1, 0, -1):
            down = jnp.where(
                near_bit == 0, down_refs[level - 1][...], down_refs[depth - 1 + level - 1][...]
            )
            solved[level - 1] = partial_ref[:, (level - 1) * order : level * order] - dot(
                solved[level], down
            )
        even_leaf = leaf - odd
        even_solved = jnp.zeros_like(solved[0])
        for level in range(2, depth + 1):
            here = lax.rem(even_leaf, 2**level) == 2 ** (level - 1)
            even_solved = jnp.where(here, solved[level - 1], even_solved)
        own_solved = jnp.where(odd == 1, solved[0], even_solved)
        other_solved = jnp.where(odd == 1, even_solved, solved[0])
        for flip, out_ref in enumerate(out_refs):
            rows_of = other_solved if flip >= 2 else own_solved
            bit = far_bit ^ (flip % 2)
            out_ref[:, updates:] = jnp.where(
                bit == 0, rows_of[:, : 2 * quarter], rows_of[:, 2 * quarter :]
            )
        for level in range(depth):
            picked = hot_dot(solved[level], hot_ref[level], 0)
            for flip, out_ref in enumerate(out_refs):
                side = flip // 2
                out_ref[:, level * capacity : (level + 1) * capacity] = picked[
                    :, side * capacity : (side + 1) * capacity
                ]

    stay, to_far, to_odd, to_both = stage(
        way_down,
        [(block, width)] * 4,
        going_up,
        partner,
        partial,
        hots,
        root,
        root_near,
        *halves,
        *halves_near,
    )
    both = swap(to_both, 1, 2)
    beyond = swap(to_far, 0, 2)
    side = swap(to_odd, 1, 0)

    def last_left(own_ref, far_ref, base_ref, left_ref):
        near_bit = place()[4]
        base_ref[...] = own_ref[:, updates:] + far_ref[:, updates:]
        left_ref[:rows, :updates] = -(own_ref[:, :updates] + far_ref[:, :updates])
        left_ref[:rows, updates:] = jnp.zeros((rows, 2 * quarter), f32)
        row = lax.broadcasted_iota(jnp.int32, (quarter, width), 0)
        lane = lax.broadcasted_iota(jnp.int32, (quarter, width), 1)
        left_ref[rows:] = jnp.where(lane == updates + near_bit * quarter + row, 1.0, 0.0)

    own_sum, stay = after(own_sum, stay)
    base, left = stage(last_left, [(rows, columns), (rows + quarter, width)], own_sum, from_far)
    both, beyond, side, left = after(both, beyond, side, left)

    def grouped(*refs):
        _, _, odd, far_bit, _ = place()
        out_ref = refs[-1]
        for flip, ref in enumerate(refs[:-1]):
            out_ref[at((2 * odd + far_bit) ^ flip, block)] = ref[...]

    (group,) = stage(grouped, [(half, width)], stay, beyond, side, both)
    group_near = swap(group, 0, 1)

    def own_columns(left_ref, group_ref, out_ref):
        out_ref[...] = dot(left_ref[...], group_ref[...], 1, 1)

    (ours,) = stage(own_columns, [(rows + quarter, half)], left, group)
    group_near, ours = after(group_near, ours)

    def finish(left_ref, group_ref, ours_ref, base_ref, leaf_ref, rows_ref):
        near_bit = place()[4]
        ours = ours_ref[...]
        theirs = dot(left_ref[...], group_ref[...], 1, 1)
        first = jnp.where(near_bit == 0, ours, theirs)
        second = jnp.where(near_bit == 0, theirs, ours)
        leaf_ref[:, :half] = base_ref[:, :half] + first[:rows]
        leaf_ref[:, half:] = base_ref[:, half:] + second[:rows]
        rows_ref[:, :half] = first[rows:]
        rows_ref[:, half:] = second[rows:]

    leaf_x, separator_rows = stage(
        finish, [(rows, columns), (quarter, columns)], left, group_near, ours, base
    )
    return (leaf_x[None], separator_rows[None])


def solution(mesh):
    placed = (
        P("leaf", "sep", None),
        P("leaf", "sep", None),
        P("leaf", None, "sep"),
        P("leaf", None),
        P("leaf", None),
        P("leaf", "sep", None),
        P("leaf", None, None),
        P("leaf", None, None),
    )
    return jax.shard_map(
        per_device,
        mesh=mesh,
        in_specs=placed,
        out_specs=(P("leaf", "sep", None), P("leaf", "sep", None)),
        check_vma=False,
    )
```

```python
import jax
import jax.numpy as jnp
from jax import lax
from jax.experimental import pallas as pl
from jax.experimental.pallas import tpu as pltpu
from jax.sharding import PartitionSpec as P

axes = ("leaf", "sep")
f32 = jnp.float32
bf16 = jnp.bfloat16
brief, medium, long = 0, 10**9, 10**11


def swap(payload, leaf_flip, sep_flip, senders=None):
    leaves, seps = lax.axis_size("leaf"), lax.axis_size("sep")
    pairs = [
        (leaf * seps + sep, (leaf ^ leaf_flip) * seps + (sep ^ sep_flip))
        for leaf in range(leaves)
        for sep in range(seps)
        if senders is None or senders(leaf, sep)
    ]
    return lax.ppermute(payload, axes, pairs)


def quarter_swap(payload, moves):
    leaves, seps = lax.axis_size("leaf"), lax.axis_size("sep")
    size = leaves // 4
    pairs = [
        ((start * size + leaf) * seps + sep, (end * size + leaf) * seps + sep)
        for start, end in moves
        for leaf in range(size)
        for sep in range(seps)
    ]
    return lax.ppermute(payload, axes, pairs)


def after(*arrays):
    return lax.optimization_barrier(arrays)


def product(left, right, left_dim, right_dim, precision=None):
    return lax.dot_general(
        left,
        right,
        (((left_dim,), (right_dim,)), ((), ())),
        precision=precision,
        preferred_element_type=f32,
    )


def dot(left, right, left_dim=1, right_dim=0):
    return product(left, right, left_dim, right_dim, lax.Precision.HIGHEST)


def pieces_of(array):
    high = array.astype(bf16)
    return high, (array - high.astype(f32)).astype(bf16)


def dot3(left, right, left_dim=1, right_dim=0):
    left_high, left_low = pieces_of(left)
    right_high, right_low = pieces_of(right)
    small = product(left_high, right_low, left_dim, right_dim)
    small = small + product(left_low, right_high, left_dim, right_dim)
    return product(left_high, right_high, left_dim, right_dim) + small


def hot_dot(left, right, right_dim):
    high = left.astype(bf16)
    rest = left - high.astype(f32)
    middle = rest.astype(bf16)
    low = (rest - middle.astype(f32)).astype(bf16)
    out = product(jnp.concatenate([high, middle, low], 0), right, 1, right_dim)
    size = left.shape[0]
    return out[:size] + (out[size : 2 * size] + out[2 * size :])


def stage(body, shapes, *operands, scratch=(), space=pltpu.VMEM, cost=brief):
    return pl.pallas_call(
        body,
        out_shape=[
            jax.ShapeDtypeStruct(shape, f32) if isinstance(shape, tuple) else shape
            for shape in shapes
        ],
        in_specs=[pl.BlockSpec(memory_space=space)] * len(operands),
        out_specs=[pl.BlockSpec(memory_space=pltpu.VMEM)] * len(shapes),
        scratch_shapes=[
            pltpu.VMEM(shape, f32) if isinstance(shape, tuple) else shape for shape in scratch
        ],
        compiler_params=pltpu.CompilerParams(vmem_limit_bytes=16 * 2**20),
        cost_estimate=pl.CostEstimate(flops=cost, bytes_accessed=0, transcendentals=0),
    )(*operands)


def place():
    leaf, sep = lax.axis_index("leaf"), lax.axis_index("sep")
    return leaf, sep, lax.rem(leaf, 2), sep // 2, lax.rem(sep, 2)


def at(index, size):
    return pl.ds(pl.multiple_of(index * size, size), size)


def by_bit(bit, zero, one):
    return jnp.where(bit == 0, zero, one)


def per_device(
    leaf_source,
    leaf_inverse,
    leaf_update,
    row_lists,
    row_counts,
    separator_source,
    separator_inverse,
    separator_coupling,
):
    depth = row_counts.shape[1]
    source = leaf_source[0]
    inverse = leaf_inverse[0]
    update = jnp.swapaxes(leaf_update, 1, 2)[0]
    rows_source = separator_source[0]
    rows, columns = source.shape
    size = inverse.shape[1]
    updates = update.shape[1]
    capacity = updates // depth
    order = separator_inverse.shape[1]
    middle = order // 2
    packed_rows = middle // 2 + 8
    carried = middle + packed_rows
    list_rows = -(-depth // 8) * 8
    quarter = rows_source.shape[0]
    half = columns // 2
    block = columns // 8
    width = updates + 2 * quarter
    leaves = lax.axis_size("leaf")

    near = swap(source, 0, 1)
    update_near = swap(update, 0, 1)
    inverse_near = swap(inverse, 0, 1)
    rows_near = swap(rows_source, 0, 1)

    def chip_source(source_ref, near_ref, out_ref):
        near_bit = place()[4]
        own, other = source_ref[...], near_ref[...]
        out_ref[at(near_bit, rows)] = by_bit(near_bit, own[:, :half], own[:, half:])
        out_ref[at(1 - near_bit, rows)] = by_bit(near_bit, other[:, :half], other[:, half:])

    (chip,) = stage(chip_source, [(2 * rows, half)], source, near)
    far = swap(chip, 0, 2)

    def operators(coupling_ref, inverse_ref, lists_ref, counts_ref, out_ref, coupling, inverse, lists, counts, packed, sems):
        near_bit = place()[4]
        pairs = ((coupling_ref.at[at(near_bit, middle)], coupling), (inverse_ref, inverse), (lists_ref, lists), (counts_ref, counts))
        copies = [pltpu.make_async_copy(src, dst, sems.at[index]) for index, (src, dst) in enumerate(pairs)]
        for copy in copies:
            copy.start()
        for copy in copies:
            copy.wait()
        out_ref[:middle] = dot(coupling[...], inverse[...])
        row = lax.broadcasted_iota(jnp.int32, (middle, middle), 0)
        lane = lax.broadcasted_iota(jnp.int32, (middle, middle), 1)
        last = inverse[middle:, middle:]
        packed[:middle, :middle] = jnp.where(row >= lane, inverse[:middle, :middle], jnp.transpose(last))
        packed[:middle, middle:] = inverse[middle:, :middle]
        packed[middle:] = jnp.zeros((2 * packed_rows - middle, order), f32)
        packed[middle : middle + 1, :middle] = jnp.sum(jnp.where(row == lane, last, 0.0), 0, keepdims=True)
        out_ref[middle:carried] = packed[at(near_bit, packed_rows)]
        out_ref[carried:] = jnp.full((list_rows, order), -1.0, f32)
        slot = lax.broadcasted_iota(jnp.int32, (1, capacity), 1)
        for level in range(depth):
            names = lists[:, level * capacity : (level + 1) * capacity]
            live = slot < counts[:, level : level + 1]
            out_ref[carried + level : carried + level + 1, :capacity] = jnp.where(live, names, -1).astype(f32)

    chip, coupling, own_inverse = after(chip, separator_coupling[0], separator_inverse[0])
    (payload,) = stage(
        operators,
        [(carried + list_rows, order)],
        coupling,
        own_inverse,
        row_lists,
        row_counts,
        scratch=[
            (middle, order),
            (order, order),
            pltpu.VMEM(row_lists.shape, jnp.int32),
            pltpu.VMEM(row_counts.shape, jnp.int32),
            (2 * packed_rows, order),
            pltpu.SemaphoreType.DMA((4,)),
        ],
        space=pltpu.HBM,
    )

    def own_part(inverse_ref, inverse_near_ref, update_ref, update_near_ref, rows_ref, rows_near_ref, chip_ref, y_ref, all_ref, far_ref, mine_ref, update_out_ref, turned_ref):
        _, _, _, far_bit, near_bit = place()
        own, other = at(near_bit, rows), at(1 - near_bit, rows)
        all_ref[own] = inverse_ref[...]
        all_ref[other] = inverse_near_ref[...]
        update_out_ref[own] = update_ref[...]
        update_out_ref[other] = update_near_ref[...]
        whole = all_ref[...]
        first, second = whole[:, : 2 * rows], whole[:, 2 * rows :]
        far_ref[...] = by_bit(far_bit, second, first)
        y_ref[...] = dot3(by_bit(far_bit, first, second), chip_ref[...])
        mine_ref[:, :rows] = by_bit(near_bit, first[:, :rows], first[:, rows:])
        mine_ref[:, rows:] = by_bit(near_bit, second[:, :rows], second[:, rows:])
        turned, turned_near = jnp.transpose(rows_ref[...]), jnp.transpose(rows_near_ref[...])
        turned = by_bit(near_bit, turned[:half], turned[half:])
        turned_near = by_bit(near_bit, turned_near[:half], turned_near[half:])
        turned_ref[...] = by_bit(
            near_bit,
            jnp.concatenate([turned, turned_near], 1),
            jnp.concatenate([turned_near, turned], 1),
        )

    received = swap(payload, 1, 0)
    inverse_near, payload = after(inverse_near, payload)
    own_y, inverse_all, inverse_far, inverse_mine, update_all, turned = stage(
        own_part,
        [(2 * rows, half), (2 * rows, size), (2 * rows, 2 * rows), (2 * rows, 2 * rows), (2 * rows, updates), (half, 2 * quarter)],
        inverse,
        inverse_near,
        update,
        update_near,
        rows_source,
        rows_near,
        chip,
    )
    far, own_y = after(far, own_y)

    def leaf_part(own_ref, inverse_ref, far_ref, update_ref, turned_ref, y_ref, *refs):
        _, _, odd, far_bit, _ = place()
        out_refs, terms = refs[:-1], refs[-1]
        leaf_y = own_ref[...] + dot3(inverse_ref[...], far_ref[...])
        y_ref[...] = leaf_y
        terms[...] = dot3(leaf_y, update_ref[...], 0, 0)
        for flip, out_ref in enumerate(out_refs):
            part = at((2 * odd + far_bit) ^ flip, block)
            out_ref[:, :updates] = terms[part]
            out_ref[:, updates:] = turned_ref[part]

    leaf_y, mine, to_far, to_odd, to_both = stage(
        leaf_part,
        [(2 * rows, half)] + [(block, width)] * 4,
        own_y,
        inverse_far,
        far,
        update_all,
        turned,
        scratch=[(half, updates)],
    )
    by_both = swap(to_both, 1, 2)
    by_far = swap(to_far, 0, 2)
    by_odd = swap(to_odd, 1, 0)

    def forward(level):
        def body(carry_ref, received_ref, half_ref, next_ref):
            upper = lax.rem(place()[0] // 2 ** (level - 1), 2) == 1
            carry, received = carry_ref[:carried], received_ref[:carried]
            half_ref[...] = jnp.where(upper, carry, received)
            next_ref[...] = jnp.where(upper, received, carry)

        return body

    def last_forward(carry_ref, received_ref, half_ref, root_ref):
        part = place()[0] // (leaves // 4)
        carry, received = carry_ref[...], received_ref[...]
        half_ref[...] = jnp.where(lax.rem(part, 2) == 1, carry, received)
        root_ref[...] = jnp.where(part == 1, received[middle:], carry[middle:])

    def root_half(root_ref, received_ref, out_ref):
        part = place()[0] // (leaves // 4)
        inner = jnp.logical_or(part == 1, part == 2)
        out_ref[...] = jnp.where(inner, root_ref[...], received_ref[...])

    received, mine = after(received, mine)
    new_half, carry = stage(forward(1), [(carried, order)] * 2, payload, received)
    halves, halves_near = [new_half], [swap(new_half, 0, 1)]
    for level in range(2, depth - 1):
        reached = swap(carry, 2 ** (level - 1), 0)
        new_half, carry = stage(forward(level), [(carried, order)] * 2, carry, reached)
        halves.append(new_half)
        halves_near.append(swap(new_half, 0, 1))
    reached = quarter_swap(carry, ((1, 0), (3, 2), (2, 1)))

    def one_hots(own_ref, other_ref, hot_ref):
        rows_of_node = lax.broadcasted_iota(jnp.int32, (order, capacity), 0)
        for level in range(depth):
            for index, ref in enumerate((own_ref, other_ref)):
                names = ref[carried + level : carried + level + 1, :capacity].astype(jnp.int32)
                hot = jnp.where(rows_of_node == names, 1.0, 0.0).astype(bf16)
                hot_ref[level, :, index * capacity : (index + 1) * capacity] = hot

    carry, payload = after(carry, payload)
    (hots,) = stage(
        one_hots, [jax.ShapeDtypeStruct((depth, order, 2 * capacity), bf16)], payload, received
    )

    def transposed(all_ref, mine_ref, update_ref, y_ref, own_ref, far_ref, work):
        far_bit = place()[3]
        work[:, :half] = dot3(all_ref[...], y_ref[...], 0, 0)
        both = dot3(mine_ref[...], update_ref[...], 0, 0)
        own_ref[:, :updates] = by_bit(far_bit, both[:rows], both[rows:])
        far_ref[:, :updates] = by_bit(far_bit, both[rows:], both[:rows])
        for index in range(2):
            part = slice(updates + index * half, updates + (index + 1) * half)
            own_ref[:, part] = work[at(2 * far_bit + index, rows)]
            far_ref[:, part] = work[at(2 - 2 * far_bit + index, rows)]

    leaf_y, hots = after(leaf_y, hots)
    own_sum, far_sum = stage(
        transposed,
        [(rows, updates + columns)] * 2,
        inverse_all,
        inverse_mine,
        update_all,
        leaf_y,
        scratch=[(size, half)],
    )
    by_both, by_far, by_odd, own_sum = after(by_both, by_far, by_odd, own_sum)

    def gathered_part(mine_ref, far_ref, odd_ref, both_ref, hot_ref, residual_ref, up_ref):
        leaf, _, odd, far_bit, _ = place()

        def joined(one, two):
            first, second = one[:, updates:], two[:, updates:]
            ordered = by_bit(
                far_bit,
                jnp.concatenate([first, second], 1),
                jnp.concatenate([second, first], 1),
            )
            return one[:, :updates] + two[:, :updates], ordered

        total, own_source = joined(mine_ref[...], far_ref[...])
        total_other, other_source = joined(odd_ref[...], both_ref[...])
        odd_source = by_bit(odd, other_source, own_source)
        even_source = by_bit(odd, own_source, other_source)
        for level in range(1, depth + 1):
            part = slice((level - 1) * capacity, level * capacity)
            both = jnp.concatenate([total[:, part], total_other[:, part]], 1)
            gathered = hot_dot(both, hot_ref[level - 1], 1)
            if level == 1:
                residual_ref[...] = odd_source - gathered
            else:
                here = lax.rem(leaf - odd, 2**level) == 2 ** (level - 1)
                slot = jnp.where(here, even_source, 0.0) - gathered
                up_ref[:, (level - 2) * order : (level - 1) * order] = slot

    residual, slots = stage(
        gathered_part,
        [(block, order), (block, (depth - 1) * order)],
        mine,
        by_far,
        by_odd,
        by_both,
        hots,
        cost=3*medium,
    )
    residuals = [residual]

    def operator_of(half_ref, near_ref):
        near_bit = place()[4]
        own, other = half_ref[:middle], near_ref[:middle]
        return jnp.concatenate([by_bit(near_bit, own, other), by_bit(near_bit, other, own)], 0)

    def push(slots_ref, residual_ref, half_ref, near_ref, out_ref):
        taken = dot(residual_ref[...], operator_of(half_ref, near_ref), 1, 1)
        out_ref[:, :order] = slots_ref[:, :order] - taken
        if out_ref.shape[1] > order:
            out_ref[:, order:] = slots_ref[:, order:]

    def inverse_of(own, other, out_ref):
        near_bit = place()[4]
        row = lax.broadcasted_iota(jnp.int32, (middle, middle), 0)
        lane = lax.broadcasted_iota(jnp.int32, (middle, middle), 1)
        packed = jnp.concatenate([by_bit(near_bit, own, other), by_bit(near_bit, other, own)], 0)
        both = packed[:middle, :middle]
        last = jnp.where(row > lane, jnp.transpose(both), 0.0)
        out_ref[:middle, :middle] = jnp.where(row >= lane, both, 0.0)
        out_ref[:middle, middle:] = jnp.zeros((middle, middle), f32)
        out_ref[middle:, :middle] = packed[:middle, middle:]
        out_ref[middle:, middle:] = jnp.where(row == lane, packed[middle : middle + 1, :middle], last)

    def alone(residual_ref, half_ref, near_ref, out_ref, work):
        inverse_of(half_ref[middle:], near_ref[middle:], work)
        out_ref[...] = dot(dot(residual_ref[...], work[...], 1, 1), work[...])

    def level_sum(up_ref, partner_ref, residual_ref, rest_ref):
        total = up_ref[...] + partner_ref[...]
        residual_ref[...] = total[:, :order]
        rest_ref[...] = total[:, order:]

    partials = []
    halves_near[0], residual, slots = after(halves_near[0], residual, slots)
    (going_up,) = stage(
        push, [(block, (depth - 1) * order)], slots, residual, halves[0], halves_near[0]
    )
    for level in range(2, depth):
        partner = swap(going_up, 2 ** (level - 1), 0)
        if level == depth - 1:
            reached, going_up, far_sum = after(reached, going_up, far_sum)
            new_half, root = stage(
                last_forward, [(carried, order), (packed_rows, order)], carry, reached
            )
            halves.append(new_half)
            from_far = swap(far_sum, 0, 2, lambda leaf, sep: sep // 2 == 1)
            halves_near.append(swap(new_half, 0, 1))
            by_root = quarter_swap(root, ((2, 3), (1, 0)))
        residuals[-1], going_up, new_half = after(residuals[-1], going_up, halves[-1])
        (partial,) = stage(
            alone,
            [(block, order)],
            residuals[-1],
            halves[level - 2],
            halves_near[level - 2],
            scratch=[(order, order)],
        )
        partials.append(partial)
        partner, partial = after(partner, partial)
        residual, slots = stage(
            level_sum,
            [(block, order), (block, (depth - level) * order)],
            going_up,
            partner,
            cost=long,
        )
        residuals.append(residual)
        halves_near[level - 1], residual, slots = after(halves_near[level - 1], residual, slots)
        (going_up,) = stage(
            push,
            [(block, (depth - level) * order)],
            slots,
            residual,
            halves[level - 1],
            halves_near[level - 1],
        )
    partner = swap(going_up, 2 ** (depth - 1), 0)

    residuals[-1], going_up = after(residuals[-1], going_up)
    (partial,) = stage(
        alone,
        [(block, order)],
        residuals[-1],
        halves[-1],
        halves_near[-1],
        scratch=[(order, order)],
    )
    partials.append(partial)
    by_root, partial = after(by_root, partial)
    (root,) = stage(root_half, [(packed_rows, order)], root, by_root)
    root_near = swap(root, 0, 1)
    partner, root = after(partner, root)

    def root_sum(up_ref, partner_ref, out_ref):
        out_ref[...] = up_ref[...] + partner_ref[...]

    (residual,) = stage(root_sum, [(block, order)], going_up, partner, cost=medium)
    root_near, residual = after(root_near, residual)

    def way_down(residual_ref, root_ref, root_near_ref, hot_ref, *refs):
        leaf, _, odd, far_bit, _ = place()
        partial_refs, half_refs = refs[: depth - 1], refs[depth - 1 : 2 * depth - 2]
        near_refs, out_refs, work = refs[2 * depth - 2 : 3 * depth - 3], refs[3 * depth - 3 : -1], refs[-1]
        inverse_of(root_ref[...], root_near_ref[...], work)
        solved = [None] * depth
        solved[-1] = dot(dot(residual_ref[...], work[...], 1, 1), work[...])
        for level in range(depth - 1, 0, -1):
            down = operator_of(half_refs[level - 1], near_refs[level - 1])
            solved[level - 1] = partial_refs[level - 1][...] - dot(solved[level], down)
        even_solved = jnp.zeros_like(solved[0])
        for level in range(2, depth + 1):
            here = lax.rem(leaf - odd, 2**level) == 2 ** (level - 1)
            even_solved = jnp.where(here, solved[level - 1], even_solved)
        own_solved = by_bit(odd, even_solved, solved[0])
        other_solved = by_bit(odd, solved[0], even_solved)
        for flip, out_ref in enumerate(out_refs):
            rows_of = other_solved if flip >= 2 else own_solved
            out_ref[:, updates:] = by_bit(
                far_bit ^ (flip % 2), rows_of[:, : 2 * quarter], rows_of[:, 2 * quarter :]
            )
        for level in range(depth):
            picked = hot_dot(solved[level], hot_ref[level], 0)
            for flip, out_ref in enumerate(out_refs):
                side = flip // 2
                out_ref[:, level * capacity : (level + 1) * capacity] = picked[
                    :, side * capacity : (side + 1) * capacity
                ]

    stay, to_far, to_odd, to_both = stage(
        way_down,
        [(block, width)] * 4,
        residual,
        root,
        root_near,
        hots,
        *partials,
        *halves,
        *halves_near,
        scratch=[(order, order)],
    )
    both = swap(to_both, 1, 2)
    beyond = swap(to_far, 0, 2)
    side = swap(to_odd, 1, 0)

    def last_left(own_ref, far_ref, left_ref, keep_ref, pass_ref):
        near_bit = place()[4]
        total = own_ref[...] + far_ref[...]
        left_ref[:rows, :updates] = -total[:, :updates]
        left_ref[:rows, updates:] = jnp.zeros((rows, 2 * quarter), f32)
        row = lax.broadcasted_iota(jnp.int32, (quarter, width), 0)
        lane = lax.broadcasted_iota(jnp.int32, (quarter, width), 1)
        left_ref[rows:] = jnp.where(lane == updates + near_bit * quarter + row, 1.0, 0.0)
        first, second = total[:, updates : updates + half], total[:, updates + half :]
        keep_ref[...] = by_bit(near_bit, first, second)
        pass_ref[...] = by_bit(near_bit, second, first)

    from_far, stay = after(from_far, stay)
    left, base_keep, base_pass = stage(
        last_left, [(rows + quarter, width), (rows, half), (rows, half)], own_sum, from_far
    )
    both, beyond, side, left = after(both, beyond, side, left)

    def grouped(*refs):
        _, _, odd, far_bit, _ = place()
        out_ref = refs[-1]
        for flip, ref in enumerate(refs[:-1]):
            out_ref[at((2 * odd + far_bit) ^ flip, block)] = ref[...]

    (group,) = stage(grouped, [(half, width)], stay, beyond, side, both)
    base_near = swap(base_pass, 0, 1)
    group_near = swap(group, 0, 1)

    def own_columns(left_ref, group_ref, out_ref):
        out_ref[...] = dot3(left_ref[...], group_ref[...], 1, 1)

    (ours,) = stage(own_columns, [(rows + quarter, half)], left, group)
    group_near, ours = after(group_near, ours)

    def finish(left_ref, group_ref, ours_ref, base_ref, base_near_ref, leaf_ref, rows_ref):
        near_bit = place()[4]
        ours = ours_ref[...]
        theirs = dot3(left_ref[...], group_ref[...], 1, 1)
        ours_x, theirs_x = base_ref[...] + ours[:rows], base_near_ref[...] + theirs[:rows]
        leaf_ref[:, :half] = by_bit(near_bit, ours_x, theirs_x)
        leaf_ref[:, half:] = by_bit(near_bit, theirs_x, ours_x)
        rows_ref[:, :half] = by_bit(near_bit, ours[rows:], theirs[rows:])
        rows_ref[:, half:] = by_bit(near_bit, theirs[rows:], ours[rows:])

    leaf_x, separator_rows = stage(
        finish,
        [(rows, columns), (quarter, columns)],
        left,
        group_near,
        ours,
        base_keep,
        base_near,
    )
    return (leaf_x[None], separator_rows[None])


def solution(mesh):
    placed = (
        P("leaf", "sep", None),
        P("leaf", "sep", None),
        P("leaf", None, "sep"),
        P("leaf", None),
        P("leaf", None),
        P("leaf", "sep", None),
        P("leaf", None, None),
        P("leaf", None, None),
    )
    return jax.shard_map(
        per_device,
        mesh=mesh,
        in_specs=placed,
        out_specs=(P("leaf", "sep", None), P("leaf", "sep", None)),
        check_vma=False,
    )
```

```python
import jax
import jax.numpy as jnp
from jax import lax
from jax.experimental import pallas as pl
from jax.experimental.pallas import tpu as pltpu
from jax.sharding import PartitionSpec as P

axes = ("leaf", "sep")
f32 = jnp.float32
bf16 = jnp.bfloat16
brief, medium, long = 0, 10**9, 10**11


def swap(payload, leaf_flip, sep_flip, senders=None):
    leaves, seps = lax.axis_size("leaf"), lax.axis_size("sep")
    pairs = [
        (leaf * seps + sep, (leaf ^ leaf_flip) * seps + (sep ^ sep_flip))
        for leaf in range(leaves)
        for sep in range(seps)
        if senders is None or senders(leaf, sep)
    ]
    return lax.ppermute(payload, axes, pairs)


def quarter_swap(payload, moves):
    leaves, seps = lax.axis_size("leaf"), lax.axis_size("sep")
    size = leaves // 4
    pairs = [
        ((start * size + leaf) * seps + sep, (end * size + leaf) * seps + sep)
        for start, end in moves
        for leaf in range(size)
        for sep in range(seps)
    ]
    return lax.ppermute(payload, axes, pairs)


def after(*arrays):
    return lax.optimization_barrier(arrays)


def product(left, right, left_dim, right_dim, precision=None):
    return lax.dot_general(
        left,
        right,
        (((left_dim,), (right_dim,)), ((), ())),
        precision=precision,
        preferred_element_type=f32,
    )


def dot(left, right, left_dim=1, right_dim=0):
    return product(left, right, left_dim, right_dim, lax.Precision.HIGHEST)


def pieces_of(array):
    high = array.astype(bf16)
    return high, (array - high.astype(f32)).astype(bf16)


def dot3(left, right, left_dim=1, right_dim=0):
    left_high, left_low = pieces_of(left)
    right_high, right_low = pieces_of(right)
    small = product(left_high, right_low, left_dim, right_dim)
    small = small + product(left_low, right_high, left_dim, right_dim)
    return product(left_high, right_high, left_dim, right_dim) + small


def hot_dot(left, right, right_dim):
    high = left.astype(bf16)
    rest = left - high.astype(f32)
    middle = rest.astype(bf16)
    low = (rest - middle.astype(f32)).astype(bf16)
    out = product(jnp.concatenate([high, middle, low], 0), right, 1, right_dim)
    size = left.shape[0]
    return out[:size] + (out[size : 2 * size] + out[2 * size :])


def stage(body, shapes, *operands, scratch=(), space=pltpu.VMEM, cost=brief):
    return pl.pallas_call(
        body,
        out_shape=[
            jax.ShapeDtypeStruct(shape, f32) if isinstance(shape, tuple) else shape
            for shape in shapes
        ],
        in_specs=[pl.BlockSpec(memory_space=space)] * len(operands),
        out_specs=[pl.BlockSpec(memory_space=pltpu.VMEM)] * len(shapes),
        scratch_shapes=[
            pltpu.VMEM(shape, f32) if isinstance(shape, tuple) else shape for shape in scratch
        ],
        compiler_params=pltpu.CompilerParams(vmem_limit_bytes=16 * 2**20),
        cost_estimate=pl.CostEstimate(flops=cost, bytes_accessed=0, transcendentals=0),
    )(*operands)


def place():
    leaf, sep = lax.axis_index("leaf"), lax.axis_index("sep")
    return leaf, sep, lax.rem(leaf, 2), sep // 2, lax.rem(sep, 2)


def at(index, size):
    return pl.ds(pl.multiple_of(index * size, size), size)


def by_bit(bit, zero, one):
    return jnp.where(bit == 0, zero, one)


def per_device(
    leaf_source,
    leaf_inverse,
    leaf_update,
    row_lists,
    row_counts,
    separator_source,
    separator_inverse,
    separator_coupling,
):
    depth = row_counts.shape[1]
    source = leaf_source[0]
    inverse = leaf_inverse[0]
    update = jnp.swapaxes(leaf_update, 1, 2)[0]
    rows_source = separator_source[0]
    rows, columns = source.shape
    size = inverse.shape[1]
    updates = update.shape[1]
    capacity = updates // depth
    order = separator_inverse.shape[1]
    middle = order // 2
    packed_rows = middle // 2 + 8
    carried = middle + packed_rows
    list_rows = -(-depth // 8) * 8
    quarter = rows_source.shape[0]
    half = columns // 2
    block = columns // 8
    width = updates + 2 * quarter
    leaves = lax.axis_size("leaf")

    near = swap(source, 0, 1)
    update_near = swap(update, 0, 1)
    inverse_near = swap(inverse, 0, 1)
    rows_near = swap(rows_source, 0, 1)

    def own_columns_of(source_ref, out_ref):
        near_bit = place()[4]
        out_ref[...] = by_bit(near_bit, source_ref[:, :half], source_ref[:, half:])

    def chip_source(own_ref, near_ref, out_ref):
        near_bit = place()[4]
        out_ref[at(near_bit, rows)] = own_ref[...]
        out_ref[at(1 - near_bit, rows)] = by_bit(near_bit, near_ref[:, :half], near_ref[:, half:])

    (own_source,) = stage(own_columns_of, [(rows, half)], source)
    near, rows_near, own_source = after(near, rows_near, own_source)
    (chip,) = stage(chip_source, [(2 * rows, half)], own_source, near)
    far = swap(chip, 0, 2)

    def operators(coupling_ref, inverse_ref, lists_ref, counts_ref, out_ref, coupling, inverse, lists, counts, packed, sems):
        near_bit = place()[4]
        pairs = ((coupling_ref.at[at(near_bit, middle)], coupling), (inverse_ref, inverse), (lists_ref, lists), (counts_ref, counts))
        copies = [pltpu.make_async_copy(src, dst, sems.at[index]) for index, (src, dst) in enumerate(pairs)]
        for copy in copies:
            copy.start()
        for copy in copies:
            copy.wait()
        out_ref[:middle] = dot(coupling[...], inverse[...])
        row = lax.broadcasted_iota(jnp.int32, (middle, middle), 0)
        lane = lax.broadcasted_iota(jnp.int32, (middle, middle), 1)
        last = inverse[middle:, middle:]
        packed[:middle, :middle] = jnp.where(row >= lane, inverse[:middle, :middle], jnp.transpose(last))
        packed[:middle, middle:] = inverse[middle:, :middle]
        packed[middle:] = jnp.zeros((2 * packed_rows - middle, order), f32)
        packed[middle : middle + 1, :middle] = jnp.sum(jnp.where(row == lane, last, 0.0), 0, keepdims=True)
        out_ref[middle:carried] = packed[at(near_bit, packed_rows)]
        out_ref[carried:] = jnp.full((list_rows, order), -1.0, f32)
        slot = lax.broadcasted_iota(jnp.int32, (1, capacity), 1)
        for level in range(depth):
            names = lists[:, level * capacity : (level + 1) * capacity]
            live = slot < counts[:, level : level + 1]
            out_ref[carried + level : carried + level + 1, :capacity] = jnp.where(live, names, -1).astype(f32)

    chip, coupling, own_inverse = after(chip, separator_coupling[0], separator_inverse[0])
    (payload,) = stage(
        operators,
        [(carried + list_rows, order)],
        coupling,
        own_inverse,
        row_lists,
        row_counts,
        scratch=[
            (middle, order),
            (order, order),
            pltpu.VMEM(row_lists.shape, jnp.int32),
            pltpu.VMEM(row_counts.shape, jnp.int32),
            (2 * packed_rows, order),
            pltpu.SemaphoreType.DMA((4,)),
        ],
        space=pltpu.HBM,
    )

    def own_part(inverse_ref, inverse_near_ref, update_ref, update_near_ref, rows_ref, rows_near_ref, chip_ref, y_ref, all_ref, far_ref, mine_ref, update_out_ref, turned_ref):
        _, _, _, far_bit, near_bit = place()
        own, other = at(near_bit, rows), at(1 - near_bit, rows)
        all_ref[own] = inverse_ref[...]
        all_ref[other] = inverse_near_ref[...]
        update_out_ref[own] = update_ref[...]
        update_out_ref[other] = update_near_ref[...]
        whole = all_ref[...]
        first, second = whole[:, : 2 * rows], whole[:, 2 * rows :]
        far_ref[...] = by_bit(far_bit, second, first)
        y_ref[...] = dot3(by_bit(far_bit, first, second), chip_ref[...])
        mine_ref[:, :rows] = by_bit(near_bit, first[:, :rows], first[:, rows:])
        mine_ref[:, rows:] = by_bit(near_bit, second[:, :rows], second[:, rows:])
        turned, turned_near = jnp.transpose(rows_ref[...]), jnp.transpose(rows_near_ref[...])
        turned = by_bit(near_bit, turned[:half], turned[half:])
        turned_near = by_bit(near_bit, turned_near[:half], turned_near[half:])
        turned_ref[...] = by_bit(
            near_bit,
            jnp.concatenate([turned, turned_near], 1),
            jnp.concatenate([turned_near, turned], 1),
        )

    received = swap(payload, 1, 0)
    inverse_near, payload = after(inverse_near, payload)
    own_y, inverse_all, inverse_far, inverse_mine, update_all, turned = stage(
        own_part,
        [(2 * rows, half), (2 * rows, size), (2 * rows, 2 * rows), (2 * rows, 2 * rows), (2 * rows, updates), (half, 2 * quarter)],
        inverse,
        inverse_near,
        update,
        update_near,
        rows_source,
        rows_near,
        chip,
    )
    far, own_y = after(far, own_y)

    def leaf_part(own_ref, inverse_ref, far_ref, update_ref, turned_ref, y_ref, *refs):
        _, _, odd, far_bit, _ = place()
        out_refs, terms = refs[:-1], refs[-1]
        leaf_y = own_ref[...] + dot3(inverse_ref[...], far_ref[...])
        y_ref[...] = leaf_y
        terms[...] = dot3(leaf_y, update_ref[...], 0, 0)
        for flip, out_ref in enumerate(out_refs):
            part = at((2 * odd + far_bit) ^ flip, block)
            out_ref[:, :updates] = terms[part]
            out_ref[:, updates:] = turned_ref[part]

    leaf_y, mine, to_far, to_odd, to_both = stage(
        leaf_part,
        [(2 * rows, half)] + [(block, width)] * 4,
        own_y,
        inverse_far,
        far,
        update_all,
        turned,
        scratch=[(half, updates)],
    )
    by_both = swap(to_both, 1, 2)
    by_far = swap(to_far, 0, 2)
    by_odd = swap(to_odd, 1, 0)

    def forward(level):
        def body(carry_ref, received_ref, half_ref, next_ref):
            upper = lax.rem(place()[0] // 2 ** (level - 1), 2) == 1
            carry, received = carry_ref[:carried], received_ref[:carried]
            half_ref[...] = jnp.where(upper, carry, received)
            next_ref[...] = jnp.where(upper, received, carry)

        return body

    def last_forward(carry_ref, received_ref, half_ref, root_ref):
        part = place()[0] // (leaves // 4)
        carry, received = carry_ref[...], received_ref[...]
        half_ref[...] = jnp.where(lax.rem(part, 2) == 1, carry, received)
        root_ref[...] = jnp.where(part == 1, received[middle:], carry[middle:])

    def root_half(root_ref, received_ref, out_ref):
        part = place()[0] // (leaves // 4)
        inner = jnp.logical_or(part == 1, part == 2)
        out_ref[...] = jnp.where(inner, root_ref[...], received_ref[...])

    received, mine = after(received, mine)
    new_half, carry = stage(forward(1), [(carried, order)] * 2, payload, received)
    halves, halves_near = [new_half], [swap(new_half, 0, 1)]
    for level in range(2, depth - 1):
        reached = swap(carry, 2 ** (level - 1), 0)
        new_half, carry = stage(forward(level), [(carried, order)] * 2, carry, reached)
        halves.append(new_half)
        halves_near.append(swap(new_half, 0, 1))
    reached = quarter_swap(carry, ((1, 0), (3, 2), (2, 1)))

    def one_hots(own_ref, other_ref, hot_ref):
        rows_of_node = lax.broadcasted_iota(jnp.int32, (order, capacity), 0)
        for level in range(depth):
            for index, ref in enumerate((own_ref, other_ref)):
                names = ref[carried + level : carried + level + 1, :capacity].astype(jnp.int32)
                hot = jnp.where(rows_of_node == names, 1.0, 0.0).astype(bf16)
                hot_ref[level, :, index * capacity : (index + 1) * capacity] = hot

    carry, payload = after(carry, payload)
    (hots,) = stage(
        one_hots, [jax.ShapeDtypeStruct((depth, order, 2 * capacity), bf16)], payload, received
    )

    def transposed(all_ref, mine_ref, update_ref, y_ref, own_ref, far_ref, work):
        far_bit = place()[3]
        work[:, :half] = dot3(all_ref[...], y_ref[...], 0, 0)
        both = dot3(mine_ref[...], update_ref[...], 0, 0)
        own_ref[:, :updates] = by_bit(far_bit, both[:rows], both[rows:])
        far_ref[:, :updates] = by_bit(far_bit, both[rows:], both[:rows])
        for index in range(2):
            part = slice(updates + index * half, updates + (index + 1) * half)
            own_ref[:, part] = work[at(2 * far_bit + index, rows)]
            far_ref[:, part] = work[at(2 - 2 * far_bit + index, rows)]

    leaf_y, hots = after(leaf_y, hots)
    own_sum, far_sum = stage(
        transposed,
        [(rows, updates + columns)] * 2,
        inverse_all,
        inverse_mine,
        update_all,
        leaf_y,
        scratch=[(size, half)],
    )
    by_both, by_far, by_odd, own_sum = after(by_both, by_far, by_odd, own_sum)

    def gathered_part(mine_ref, far_ref, odd_ref, both_ref, hot_ref, residual_ref, up_ref):
        leaf, _, odd, far_bit, _ = place()

        def joined(one, two):
            first, second = one[:, updates:], two[:, updates:]
            ordered = by_bit(
                far_bit,
                jnp.concatenate([first, second], 1),
                jnp.concatenate([second, first], 1),
            )
            return one[:, :updates] + two[:, :updates], ordered

        total, own_source = joined(mine_ref[...], far_ref[...])
        total_other, other_source = joined(odd_ref[...], both_ref[...])
        odd_source = by_bit(odd, other_source, own_source)
        even_source = by_bit(odd, own_source, other_source)
        for level in range(1, depth + 1):
            part = slice((level - 1) * capacity, level * capacity)
            both = jnp.concatenate([total[:, part], total_other[:, part]], 1)
            gathered = hot_dot(both, hot_ref[level - 1], 1)
            if level == 1:
                residual_ref[...] = odd_source - gathered
            else:
                here = lax.rem(leaf - odd, 2**level) == 2 ** (level - 1)
                slot = jnp.where(here, even_source, 0.0) - gathered
                up_ref[:, (level - 2) * order : (level - 1) * order] = slot

    residual, slots = stage(
        gathered_part,
        [(block, order), (block, (depth - 1) * order)],
        mine,
        by_far,
        by_odd,
        by_both,
        hots,
        cost=3*medium,
    )
    residuals = [residual]

    def operator_of(half_ref, near_ref):
        near_bit = place()[4]
        own, other = half_ref[:middle], near_ref[:middle]
        return jnp.concatenate([by_bit(near_bit, own, other), by_bit(near_bit, other, own)], 0)

    def push(slots_ref, residual_ref, half_ref, near_ref, out_ref):
        taken = dot(residual_ref[...], operator_of(half_ref, near_ref), 1, 1)
        out_ref[:, :order] = slots_ref[:, :order] - taken
        if out_ref.shape[1] > order:
            out_ref[:, order:] = slots_ref[:, order:]

    def blocks_of(own, other):
        near_bit = place()[4]
        row = lax.broadcasted_iota(jnp.int32, (middle, middle), 0)
        lane = lax.broadcasted_iota(jnp.int32, (middle, middle), 1)
        packed = jnp.concatenate([by_bit(near_bit, own, other), by_bit(near_bit, other, own)], 0)
        both = packed[:middle, :middle]
        last = jnp.where(row < lane, both, 0.0)
        last = jnp.where(row == lane, packed[middle : middle + 1, :middle], last)
        return jnp.where(row >= lane, both, 0.0), packed[:middle, middle:], last

    def alone(residual_ref, half_ref, near_ref, out_ref, down_ref):
        down_ref[...] = operator_of(half_ref, near_ref)
        first, below, last = blocks_of(half_ref[middle:], near_ref[middle:])
        one, two = residual_ref[:, :middle], residual_ref[:, middle:]
        upper, lower = dot3(one, first, 1, 1), dot3(one, below, 1, 1) + dot3(two, last)
        out_ref[:, :middle] = dot3(upper, first) + dot3(lower, below)
        out_ref[:, middle:] = dot3(lower, last, 1, 1)

    def level_sum(up_ref, partner_ref, residual_ref, rest_ref):
        total = up_ref[...] + partner_ref[...]
        residual_ref[...] = total[:, :order]
        rest_ref[...] = total[:, order:]

    partials, downs = [], []
    halves_near[0], residual, slots = after(halves_near[0], residual, slots)
    (going_up,) = stage(
        push, [(block, (depth - 1) * order)], slots, residual, halves[0], halves_near[0]
    )
    for level in range(2, depth):
        partner = swap(going_up, 2 ** (level - 1), 0)
        residuals[-1], going_up = after(residuals[-1], going_up)
        partial, down = stage(
            alone,
            [(block, order), (order, order)],
            residuals[-1],
            halves[level - 2],
            halves_near[level - 2],
        )
        if level == depth - 1:
            reached, partial = after(reached, partial)
            new_half, root = stage(
                last_forward, [(carried, order), (packed_rows, order)], carry, reached
            )
            halves.append(new_half)
            from_far = swap(far_sum, 0, 2, lambda leaf, sep: sep // 2 == 1)
            halves_near.append(swap(new_half, 0, 1))
            by_root = quarter_swap(root, ((2, 3), (1, 0)))
        downs.append(down)
        partials.append(partial)
        partner, partial = after(partner, partial)
        residual, slots = stage(
            level_sum,
            [(block, order), (block, (depth - level) * order)],
            going_up,
            partner,
            cost=3 * medium,
        )
        residuals.append(residual)
        halves_near[level - 1], residual, slots = after(halves_near[level - 1], residual, slots)
        (going_up,) = stage(
            push,
            [(block, (depth - level) * order)],
            slots,
            residual,
            halves[level - 1],
            halves_near[level - 1],
        )
    partner = swap(going_up, 2 ** (depth - 1), 0)

    residuals[-1], going_up = after(residuals[-1], going_up)
    partial, down = stage(
        alone,
        [(block, order), (order, order)],
        residuals[-1],
        halves[-1],
        halves_near[-1],
    )
    partials.append(partial)
    downs.append(down)
    by_root, partial = after(by_root, partial)
    (root,) = stage(root_half, [(packed_rows, order)], root, by_root)
    root_near = swap(root, 0, 1)
    partner, root = after(partner, root)

    def root_sum(up_ref, partner_ref, out_ref):
        out_ref[...] = up_ref[...] + partner_ref[...]

    (residual,) = stage(root_sum, [(block, order)], going_up, partner, cost=medium)
    root_near, residual = after(root_near, residual)

    def way_down(residual_ref, root_ref, root_near_ref, hot_ref, *refs):
        leaf, _, odd, far_bit, _ = place()
        partial_refs, down_refs = refs[: depth - 1], refs[depth - 1 : 2 * depth - 2]
        out_refs = refs[2 * depth - 2 :]
        first, below, last = blocks_of(root_ref[...], root_near_ref[...])
        one, two = residual_ref[:, :middle], residual_ref[:, middle:]
        upper, lower = dot3(one, first, 1, 1), dot3(one, below, 1, 1) + dot3(two, last)
        solved = [None] * depth
        solved[-1] = jnp.concatenate(
            [dot3(upper, first) + dot3(lower, below), dot3(lower, last, 1, 1)], 1
        )
        for level in range(depth - 1, 0, -1):
            solved[level - 1] = partial_refs[level - 1][...] - dot3(
                solved[level], down_refs[level - 1][...]
            )
        even_solved = jnp.zeros_like(solved[0])
        for level in range(2, depth + 1):
            here = lax.rem(leaf - odd, 2**level) == 2 ** (level - 1)
            even_solved = jnp.where(here, solved[level - 1], even_solved)
        own_solved = by_bit(odd, even_solved, solved[0])
        other_solved = by_bit(odd, solved[0], even_solved)
        for flip, out_ref in enumerate(out_refs):
            rows_of = other_solved if flip >= 2 else own_solved
            out_ref[:, updates:] = by_bit(
                far_bit ^ (flip % 2), rows_of[:, : 2 * quarter], rows_of[:, 2 * quarter :]
            )
        for level in range(depth):
            picked = hot_dot(solved[level], hot_ref[level], 0)
            for flip, out_ref in enumerate(out_refs):
                side = flip // 2
                out_ref[:, level * capacity : (level + 1) * capacity] = picked[
                    :, side * capacity : (side + 1) * capacity
                ]

    stay, to_far, to_odd, to_both = stage(
        way_down,
        [(block, width)] * 4,
        residual,
        root,
        root_near,
        hots,
        *partials,
        *downs,
    )
    both = swap(to_both, 1, 2)
    beyond = swap(to_far, 0, 2)
    side = swap(to_odd, 1, 0)

    def last_left(own_ref, far_ref, left_ref, keep_ref, pass_ref):
        near_bit = place()[4]
        total = own_ref[...] + far_ref[...]
        left_ref[:rows, :updates] = -total[:, :updates]
        left_ref[:rows, updates:] = jnp.zeros((rows, 2 * quarter), f32)
        row = lax.broadcasted_iota(jnp.int32, (quarter, width), 0)
        lane = lax.broadcasted_iota(jnp.int32, (quarter, width), 1)
        left_ref[rows:] = jnp.where(lane == updates + near_bit * quarter + row, 1.0, 0.0)
        first, second = total[:, updates : updates + half], total[:, updates + half :]
        keep_ref[...] = by_bit(near_bit, first, second)
        pass_ref[...] = by_bit(near_bit, second, first)

    from_far, stay = after(from_far, stay)
    left, base_keep, base_pass = stage(
        last_left, [(rows + quarter, width), (rows, half), (rows, half)], own_sum, from_far
    )
    both, beyond, side, left = after(both, beyond, side, left)

    def grouped(*refs):
        _, _, odd, far_bit, _ = place()
        out_ref = refs[-1]
        for flip, ref in enumerate(refs[:-1]):
            out_ref[at((2 * odd + far_bit) ^ flip, block)] = ref[...]

    (group,) = stage(grouped, [(half, width)], stay, beyond, side, both)
    base_near = swap(base_pass, 0, 1)
    group_near = swap(group, 0, 1)

    def own_columns(left_ref, group_ref, out_ref):
        out_ref[...] = dot3(left_ref[...], group_ref[...], 1, 1)

    (ours,) = stage(own_columns, [(rows + quarter, half)], left, group)
    group_near, ours = after(group_near, ours)

    def finish(left_ref, group_ref, ours_ref, base_ref, base_near_ref, leaf_ref, rows_ref):
        near_bit = place()[4]
        ours = ours_ref[...]
        theirs = dot3(left_ref[...], group_ref[...], 1, 1)
        ours_x, theirs_x = base_ref[...] + ours[:rows], base_near_ref[...] + theirs[:rows]
        leaf_ref[:, :half] = by_bit(near_bit, ours_x, theirs_x)
        leaf_ref[:, half:] = by_bit(near_bit, theirs_x, ours_x)
        rows_ref[:, :half] = by_bit(near_bit, ours[rows:], theirs[rows:])
        rows_ref[:, half:] = by_bit(near_bit, theirs[rows:], ours[rows:])

    leaf_x, separator_rows = stage(
        finish,
        [(rows, columns), (quarter, columns)],
        left,
        group_near,
        ours,
        base_keep,
        base_near,
    )
    return (leaf_x[None], separator_rows[None])


def solution(mesh):
    placed = (
        P("leaf", "sep", None),
        P("leaf", "sep", None),
        P("leaf", None, "sep"),
        P("leaf", None),
        P("leaf", None),
        P("leaf", "sep", None),
        P("leaf", None, None),
        P("leaf", None, None),
    )
    return jax.shard_map(
        per_device,
        mesh=mesh,
        in_specs=placed,
        out_specs=(P("leaf", "sep", None), P("leaf", "sep", None)),
        check_vma=False,
    )
```

```python
import jax
import jax.numpy as jnp
from jax import lax
from jax.experimental import pallas as pl
from jax.experimental.pallas import tpu as pltpu
from jax.sharding import PartitionSpec as P

axes = ("leaf", "sep")
f32 = jnp.float32
bf16 = jnp.bfloat16
brief, medium, long = 0, 10**9, 10**11


def swap(payload, leaf_flip, sep_flip, senders=None):
    leaves, seps = lax.axis_size("leaf"), lax.axis_size("sep")
    pairs = [
        (leaf * seps + sep, (leaf ^ leaf_flip) * seps + (sep ^ sep_flip))
        for leaf in range(leaves)
        for sep in range(seps)
        if senders is None or senders(leaf, sep)
    ]
    return lax.ppermute(payload, axes, pairs)


def quarter_swap(payload, moves):
    leaves, seps = lax.axis_size("leaf"), lax.axis_size("sep")
    size = leaves // 4
    pairs = [
        ((start * size + leaf) * seps + sep, (end * size + leaf) * seps + sep)
        for start, end in moves
        for leaf in range(size)
        for sep in range(seps)
    ]
    return lax.ppermute(payload, axes, pairs)


def after(*arrays):
    return lax.optimization_barrier(arrays)


def product(left, right, left_dim, right_dim, precision=None):
    return lax.dot_general(
        left,
        right,
        (((left_dim,), (right_dim,)), ((), ())),
        precision=precision,
        preferred_element_type=f32,
    )


def dot(left, right, left_dim=1, right_dim=0):
    return product(left, right, left_dim, right_dim, lax.Precision.HIGHEST)


def pieces_of(array):
    high = array.astype(bf16)
    return high, (array - high.astype(f32)).astype(bf16)


def dot3(left, right, left_dim=1, right_dim=0):
    left_high, left_low = pieces_of(left)
    right_high, right_low = pieces_of(right)
    small = product(left_high, right_low, left_dim, right_dim)
    small = small + product(left_low, right_high, left_dim, right_dim)
    return product(left_high, right_high, left_dim, right_dim) + small


def hot_dot(left, right, right_dim):
    high = left.astype(bf16)
    rest = left - high.astype(f32)
    middle = rest.astype(bf16)
    low = (rest - middle.astype(f32)).astype(bf16)
    out = product(jnp.concatenate([high, middle, low], 0), right, 1, right_dim)
    size = left.shape[0]
    return out[:size] + (out[size : 2 * size] + out[2 * size :])


def stage(body, shapes, *operands, scratch=(), space=pltpu.VMEM, cost=brief):
    return pl.pallas_call(
        body,
        out_shape=[
            jax.ShapeDtypeStruct(shape, f32) if isinstance(shape, tuple) else shape
            for shape in shapes
        ],
        in_specs=[pl.BlockSpec(memory_space=space)] * len(operands),
        out_specs=[pl.BlockSpec(memory_space=pltpu.VMEM)] * len(shapes),
        scratch_shapes=[
            pltpu.VMEM(shape, f32) if isinstance(shape, tuple) else shape for shape in scratch
        ],
        compiler_params=pltpu.CompilerParams(vmem_limit_bytes=16 * 2**20),
        cost_estimate=pl.CostEstimate(flops=cost, bytes_accessed=0, transcendentals=0),
    )(*operands)


def place():
    leaf, sep = lax.axis_index("leaf"), lax.axis_index("sep")
    return leaf, sep, lax.rem(leaf, 2), sep // 2, lax.rem(sep, 2)


def at(index, size):
    return pl.ds(pl.multiple_of(index * size, size), size)


def by_bit(bit, zero, one):
    return jnp.where(bit == 0, zero, one)


def per_device(
    leaf_source,
    leaf_inverse,
    leaf_update,
    row_lists,
    row_counts,
    separator_source,
    separator_inverse,
    separator_coupling,
):
    depth = row_counts.shape[1]
    source = leaf_source[0]
    inverse = leaf_inverse[0]
    update = jnp.swapaxes(leaf_update, 1, 2)[0]
    rows_source = separator_source[0]
    rows, columns = source.shape
    size = inverse.shape[1]
    updates = update.shape[1]
    capacity = updates // depth
    order = separator_inverse.shape[1]
    middle = order // 2
    packed_rows = middle // 2 + 8
    carried = middle + packed_rows
    list_rows = -(-depth // 8) * 8
    quarter = rows_source.shape[0]
    half = columns // 2
    block = columns // 8
    width = updates + 2 * quarter
    leaves = lax.axis_size("leaf")

    near = swap(source, 0, 1)
    update_near = swap(update, 0, 1)
    inverse_near = swap(inverse, 0, 1)
    rows_near = swap(rows_source, 0, 1)

    def own_columns_of(source_ref, out_ref):
        near_bit = place()[4]
        out_ref[...] = by_bit(near_bit, source_ref[:, :half], source_ref[:, half:])

    def chip_source(own_ref, near_ref, out_ref):
        near_bit = place()[4]
        out_ref[at(near_bit, rows)] = own_ref[...]
        out_ref[at(1 - near_bit, rows)] = by_bit(near_bit, near_ref[:, :half], near_ref[:, half:])

    (own_source,) = stage(own_columns_of, [(rows, half)], source)
    near, own_source = after(near, own_source)
    (chip,) = stage(chip_source, [(2 * rows, half)], own_source, near)
    far = swap(chip, 0, 2)

    def operators(coupling_ref, inverse_ref, lists_ref, counts_ref, out_ref, coupling, inverse, lists, counts, packed, sems):
        near_bit = place()[4]
        pairs = ((coupling_ref.at[at(near_bit, middle)], coupling), (inverse_ref, inverse), (lists_ref, lists), (counts_ref, counts))
        copies = [pltpu.make_async_copy(src, dst, sems.at[index]) for index, (src, dst) in enumerate(pairs)]
        for copy in copies:
            copy.start()
        for copy in copies:
            copy.wait()
        out_ref[:middle] = dot(coupling[...], inverse[...])
        row = lax.broadcasted_iota(jnp.int32, (middle, middle), 0)
        lane = lax.broadcasted_iota(jnp.int32, (middle, middle), 1)
        last = inverse[middle:, middle:]
        packed[:middle, :middle] = jnp.where(row >= lane, inverse[:middle, :middle], jnp.transpose(last))
        packed[:middle, middle:] = inverse[middle:, :middle]
        packed[middle:] = jnp.zeros((2 * packed_rows - middle, order), f32)
        packed[middle : middle + 1, :middle] = jnp.sum(jnp.where(row == lane, last, 0.0), 0, keepdims=True)
        out_ref[middle:carried] = packed[at(near_bit, packed_rows)]
        out_ref[carried:] = jnp.full((list_rows, order), -1.0, f32)
        slot = lax.broadcasted_iota(jnp.int32, (1, capacity), 1)
        for level in range(depth):
            names = lists[:, level * capacity : (level + 1) * capacity]
            live = slot < counts[:, level : level + 1]
            out_ref[carried + level : carried + level + 1, :capacity] = jnp.where(live, names, -1).astype(f32)

    chip, coupling, own_inverse = after(chip, separator_coupling[0], separator_inverse[0])
    (payload,) = stage(
        operators,
        [(carried + list_rows, order)],
        coupling,
        own_inverse,
        row_lists,
        row_counts,
        scratch=[
            (middle, order),
            (order, order),
            pltpu.VMEM(row_lists.shape, jnp.int32),
            pltpu.VMEM(row_counts.shape, jnp.int32),
            (2 * packed_rows, order),
            pltpu.SemaphoreType.DMA((4,)),
        ],
        space=pltpu.HBM,
    )

    def own_part(inverse_ref, inverse_near_ref, update_ref, update_near_ref, rows_ref, rows_near_ref, chip_ref, y_ref, all_ref, far_ref, mine_ref, update_out_ref, turned_ref):
        _, _, _, far_bit, near_bit = place()
        own, other = at(near_bit, rows), at(1 - near_bit, rows)
        all_ref[own] = inverse_ref[...]
        all_ref[other] = inverse_near_ref[...]
        update_out_ref[own] = update_ref[...]
        update_out_ref[other] = update_near_ref[...]
        whole = all_ref[...]
        first, second = whole[:, : 2 * rows], whole[:, 2 * rows :]
        far_ref[...] = by_bit(far_bit, second, first)
        y_ref[...] = dot3(by_bit(far_bit, first, second), chip_ref[...])
        mine_ref[:, :rows] = by_bit(near_bit, first[:, :rows], first[:, rows:])
        mine_ref[:, rows:] = by_bit(near_bit, second[:, :rows], second[:, rows:])
        turned, turned_near = jnp.transpose(rows_ref[...]), jnp.transpose(rows_near_ref[...])
        turned = by_bit(near_bit, turned[:half], turned[half:])
        turned_near = by_bit(near_bit, turned_near[:half], turned_near[half:])
        turned_ref[...] = by_bit(
            near_bit,
            jnp.concatenate([turned, turned_near], 1),
            jnp.concatenate([turned_near, turned], 1),
        )

    received = swap(payload, 1, 0)
    inverse_near, rows_near, payload = after(inverse_near, rows_near, payload)
    own_y, inverse_all, inverse_far, inverse_mine, update_all, turned = stage(
        own_part,
        [(2 * rows, half), (2 * rows, size), (2 * rows, 2 * rows), (2 * rows, 2 * rows), (2 * rows, updates), (half, 2 * quarter)],
        inverse,
        inverse_near,
        update,
        update_near,
        rows_source,
        rows_near,
        chip,
    )
    far, own_y = after(far, own_y)

    def leaf_part(own_ref, inverse_ref, far_ref, update_ref, turned_ref, y_ref, *refs):
        _, _, odd, far_bit, _ = place()
        out_refs, terms = refs[:-1], refs[-1]
        leaf_y = own_ref[...] + dot3(inverse_ref[...], far_ref[...])
        y_ref[...] = leaf_y
        terms[...] = dot3(leaf_y, update_ref[...], 0, 0)
        for flip, out_ref in enumerate(out_refs):
            part = at((2 * odd + far_bit) ^ flip, block)
            out_ref[:, :updates] = terms[part]
            out_ref[:, updates:] = turned_ref[part]

    leaf_y, mine, to_far, to_odd, to_both = stage(
        leaf_part,
        [(2 * rows, half)] + [(block, width)] * 4,
        own_y,
        inverse_far,
        far,
        update_all,
        turned,
        scratch=[(half, updates)],
    )
    by_both = swap(to_both, 1, 2)
    by_far = swap(to_far, 0, 2)
    by_odd = swap(to_odd, 1, 0)

    def forward(level):
        def body(carry_ref, received_ref, half_ref, next_ref):
            upper = lax.rem(place()[0] // 2 ** (level - 1), 2) == 1
            carry, received = carry_ref[:carried], received_ref[:carried]
            half_ref[...] = jnp.where(upper, carry, received)
            next_ref[...] = jnp.where(upper, received, carry)

        return body

    def last_forward(carry_ref, received_ref, half_ref, root_ref):
        part = place()[0] // (leaves // 4)
        carry, received = carry_ref[...], received_ref[...]
        half_ref[...] = jnp.where(lax.rem(part, 2) == 1, carry, received)
        root_ref[...] = jnp.where(part == 1, received[middle:], carry[middle:])

    def root_half(root_ref, received_ref, out_ref):
        part = place()[0] // (leaves // 4)
        inner = jnp.logical_or(part == 1, part == 2)
        out_ref[...] = jnp.where(inner, root_ref[...], received_ref[...])

    received, mine = after(received, mine)
    new_half, carry = stage(forward(1), [(carried, order)] * 2, payload, received)
    halves, halves_near = [new_half], [swap(new_half, 0, 1)]
    for level in range(2, depth - 1):
        reached = swap(carry, 2 ** (level - 1), 0)
        new_half, carry = stage(forward(level), [(carried, order)] * 2, carry, reached)
        halves.append(new_half)
        halves_near.append(swap(new_half, 0, 1))
    reached = quarter_swap(carry, ((1, 0), (3, 2), (2, 1)))

    def one_hots(own_ref, other_ref, hot_ref):
        rows_of_node = lax.broadcasted_iota(jnp.int32, (order, capacity), 0)
        for level in range(depth):
            for index, ref in enumerate((own_ref, other_ref)):
                names = ref[carried + level : carried + level + 1, :capacity].astype(jnp.int32)
                hot = jnp.where(rows_of_node == names, 1.0, 0.0).astype(bf16)
                hot_ref[level, :, index * capacity : (index + 1) * capacity] = hot

    carry, payload = after(carry, payload)
    (hots,) = stage(
        one_hots, [jax.ShapeDtypeStruct((depth, order, 2 * capacity), bf16)], payload, received
    )

    def transposed(all_ref, mine_ref, update_ref, y_ref, own_ref, far_ref, work):
        far_bit = place()[3]
        work[:, :half] = dot3(all_ref[...], y_ref[...], 0, 0)
        both = dot3(mine_ref[...], update_ref[...], 0, 0)
        own_ref[:, :updates] = by_bit(far_bit, both[:rows], both[rows:])
        far_ref[:, :updates] = by_bit(far_bit, both[rows:], both[:rows])
        for index in range(2):
            part = slice(updates + index * half, updates + (index + 1) * half)
            own_ref[:, part] = work[at(2 * far_bit + index, rows)]
            far_ref[:, part] = work[at(2 - 2 * far_bit + index, rows)]

    leaf_y, hots = after(leaf_y, hots)
    own_sum, far_sum = stage(
        transposed,
        [(rows, updates + columns)] * 2,
        inverse_all,
        inverse_mine,
        update_all,
        leaf_y,
        scratch=[(size, half)],
    )
    by_both, by_far, by_odd, own_sum = after(by_both, by_far, by_odd, own_sum)

    def gathered_part(mine_ref, far_ref, odd_ref, both_ref, hot_ref, residual_ref, up_ref):
        leaf, _, odd, far_bit, _ = place()

        def joined(one, two):
            first, second = one[:, updates:], two[:, updates:]
            ordered = by_bit(
                far_bit,
                jnp.concatenate([first, second], 1),
                jnp.concatenate([second, first], 1),
            )
            return one[:, :updates] + two[:, :updates], ordered

        total, own_source = joined(mine_ref[...], far_ref[...])
        total_other, other_source = joined(odd_ref[...], both_ref[...])
        odd_source = by_bit(odd, other_source, own_source)
        even_source = by_bit(odd, own_source, other_source)
        for level in range(1, depth + 1):
            part = slice((level - 1) * capacity, level * capacity)
            both = jnp.concatenate([total[:, part], total_other[:, part]], 1)
            gathered = hot_dot(both, hot_ref[level - 1], 1)
            if level == 1:
                residual_ref[...] = odd_source - gathered
            else:
                here = lax.rem(leaf - odd, 2**level) == 2 ** (level - 1)
                slot = jnp.where(here, even_source, 0.0) - gathered
                up_ref[:, (level - 2) * order : (level - 1) * order] = slot

    residual, slots = stage(
        gathered_part,
        [(block, order), (block, (depth - 1) * order)],
        mine,
        by_far,
        by_odd,
        by_both,
        hots,
        cost=3*medium,
    )
    residuals = [residual]

    def operator_of(half_ref, near_ref):
        near_bit = place()[4]
        own, other = half_ref[:middle], near_ref[:middle]
        return jnp.concatenate([by_bit(near_bit, own, other), by_bit(near_bit, other, own)], 0)

    def push(slots_ref, residual_ref, half_ref, near_ref, out_ref):
        taken = dot3(residual_ref[...], operator_of(half_ref, near_ref), 1, 1)
        out_ref[:, :order] = slots_ref[:, :order] - taken
        if out_ref.shape[1] > order:
            out_ref[:, order:] = slots_ref[:, order:]

    def blocks_of(own, other):
        near_bit = place()[4]
        row = lax.broadcasted_iota(jnp.int32, (middle, middle), 0)
        lane = lax.broadcasted_iota(jnp.int32, (middle, middle), 1)
        packed = jnp.concatenate([by_bit(near_bit, own, other), by_bit(near_bit, other, own)], 0)
        both = packed[:middle, :middle]
        last = jnp.where(row < lane, both, 0.0)
        last = jnp.where(row == lane, packed[middle : middle + 1, :middle], last)
        return jnp.where(row >= lane, both, 0.0), packed[:middle, middle:], last

    def alone(residual_ref, half_ref, near_ref, out_ref, down_ref):
        down_ref[...] = operator_of(half_ref, near_ref)
        first, below, last = blocks_of(half_ref[middle:], near_ref[middle:])
        one, two = residual_ref[:, :middle], residual_ref[:, middle:]
        upper, lower = dot3(one, first, 1, 1), dot3(one, below, 1, 1) + dot3(two, last)
        out_ref[:, :middle] = dot3(upper, first) + dot3(lower, below)
        out_ref[:, middle:] = dot3(lower, last, 1, 1)

    def level_sum(up_ref, partner_ref, residual_ref, rest_ref):
        total = up_ref[...] + partner_ref[...]
        residual_ref[...] = total[:, :order]
        rest_ref[...] = total[:, order:]

    partials, downs = [], []
    halves_near[0], residual, slots = after(halves_near[0], residual, slots)
    (going_up,) = stage(
        push, [(block, (depth - 1) * order)], slots, residual, halves[0], halves_near[0]
    )
    for level in range(2, depth):
        partner = swap(going_up, 2 ** (level - 1), 0)
        if level == depth - 1:
            reached, going_up = after(reached, going_up)
            new_half, root = stage(
                last_forward, [(carried, order), (packed_rows, order)], carry, reached
            )
            halves.append(new_half)
            from_far = swap(far_sum, 0, 2, lambda leaf, sep: sep // 2 == 1)
            halves_near.append(swap(new_half, 0, 1))
            by_root = swap(root, leaves // 4, 0)
        residual, slots = stage(
            level_sum,
            [(block, order), (block, (depth - level) * order)],
            going_up,
            partner,
            cost=3 * medium,
        )
        residuals.append(residual)
        halves_near[level - 1], residual, slots = after(halves_near[level - 1], residual, slots)
        (going_up,) = stage(
            push,
            [(block, (depth - level) * order)],
            slots,
            residual,
            halves[level - 1],
            halves_near[level - 1],
        )
    partner = swap(going_up, 2 ** (depth - 1), 0)

    for level in range(1, depth):
        residual, going_up = after(residuals[level - 1], going_up)
        partial, down = stage(
            alone,
            [(block, order), (order, order)],
            residual,
            halves[level - 1],
            halves_near[level - 1],
        )
        partials.append(partial)
        downs.append(down)
    by_root, partial = after(by_root, partial)
    (root,) = stage(root_half, [(packed_rows, order)], root, by_root)
    root_near = swap(root, 0, 1)
    partner, root = after(partner, root)

    def root_sum(up_ref, partner_ref, out_ref):
        out_ref[...] = up_ref[...] + partner_ref[...]

    (residual,) = stage(root_sum, [(block, order)], going_up, partner, cost=medium)
    root_near, residual = after(root_near, residual)

    def way_down(residual_ref, root_ref, root_near_ref, hot_ref, *refs):
        leaf, _, odd, far_bit, _ = place()
        partial_refs, down_refs = refs[: depth - 1], refs[depth - 1 : 2 * depth - 2]
        out_refs = refs[2 * depth - 2 :]
        first, below, last = blocks_of(root_ref[...], root_near_ref[...])
        one, two = residual_ref[:, :middle], residual_ref[:, middle:]
        upper, lower = dot3(one, first, 1, 1), dot3(one, below, 1, 1) + dot3(two, last)
        solved = [None] * depth
        solved[-1] = jnp.concatenate(
            [dot3(upper, first) + dot3(lower, below), dot3(lower, last, 1, 1)], 1
        )
        for level in range(depth - 1, 0, -1):
            solved[level - 1] = partial_refs[level - 1][...] - dot3(
                solved[level], down_refs[level - 1][...]
            )
        even_solved = jnp.zeros_like(solved[0])
        for level in range(2, depth + 1):
            here = lax.rem(leaf - odd, 2**level) == 2 ** (level - 1)
            even_solved = jnp.where(here, solved[level - 1], even_solved)
        own_solved = by_bit(odd, even_solved, solved[0])
        other_solved = by_bit(odd, solved[0], even_solved)
        for flip, out_ref in enumerate(out_refs):
            rows_of = other_solved if flip >= 2 else own_solved
            out_ref[:, updates:] = by_bit(
                far_bit ^ (flip % 2), rows_of[:, : 2 * quarter], rows_of[:, 2 * quarter :]
            )
        for level in range(depth):
            picked = hot_dot(solved[level], hot_ref[level], 0)
            for flip, out_ref in enumerate(out_refs):
                side = flip // 2
                out_ref[:, level * capacity : (level + 1) * capacity] = picked[
                    :, side * capacity : (side + 1) * capacity
                ]

    stay, to_far, to_odd, to_both = stage(
        way_down,
        [(block, width)] * 4,
        residual,
        root,
        root_near,
        hots,
        *partials,
        *downs,
    )
    both = swap(to_both, 1, 2)
    beyond = swap(to_far, 0, 2)
    side = swap(to_odd, 1, 0)

    def last_left(own_ref, far_ref, left_ref, keep_ref, pass_ref):
        near_bit = place()[4]
        total = own_ref[...] + far_ref[...]
        left_ref[:rows, :updates] = -total[:, :updates]
        left_ref[:rows, updates:] = jnp.zeros((rows, 2 * quarter), f32)
        row = lax.broadcasted_iota(jnp.int32, (quarter, width), 0)
        lane = lax.broadcasted_iota(jnp.int32, (quarter, width), 1)
        left_ref[rows:] = jnp.where(lane == updates + near_bit * quarter + row, 1.0, 0.0)
        first, second = total[:, updates : updates + half], total[:, updates + half :]
        keep_ref[...] = by_bit(near_bit, first, second)
        pass_ref[...] = by_bit(near_bit, second, first)

    from_far, stay = after(from_far, stay)
    left, base_keep, base_pass = stage(
        last_left, [(rows + quarter, width), (rows, half), (rows, half)], own_sum, from_far
    )
    both, beyond, side, left = after(both, beyond, side, left)

    def grouped(*refs):
        _, _, odd, far_bit, _ = place()
        out_ref = refs[-1]
        for flip, ref in enumerate(refs[:-1]):
            out_ref[at((2 * odd + far_bit) ^ flip, block)] = ref[...]

    (group,) = stage(grouped, [(half, width)], stay, beyond, side, both)
    base_near = swap(base_pass, 0, 1)
    group_near = swap(group, 0, 1)

    def own_columns(left_ref, group_ref, out_ref):
        out_ref[...] = dot3(left_ref[...], group_ref[...], 1, 1)

    (ours,) = stage(own_columns, [(rows + quarter, half)], left, group)
    group_near, ours = after(group_near, ours)

    def finish(left_ref, group_ref, ours_ref, base_ref, base_near_ref, leaf_ref, rows_ref):
        near_bit = place()[4]
        ours = ours_ref[...]
        theirs = dot3(left_ref[...], group_ref[...], 1, 1)
        ours_x, theirs_x = base_ref[...] + ours[:rows], base_near_ref[...] + theirs[:rows]
        leaf_ref[:, :half] = by_bit(near_bit, ours_x, theirs_x)
        leaf_ref[:, half:] = by_bit(near_bit, theirs_x, ours_x)
        rows_ref[:, :half] = by_bit(near_bit, ours[rows:], theirs[rows:])
        rows_ref[:, half:] = by_bit(near_bit, theirs[rows:], ours[rows:])

    leaf_x, separator_rows = stage(
        finish,
        [(rows, columns), (quarter, columns)],
        left,
        group_near,
        ours,
        base_keep,
        base_near,
    )
    return (leaf_x[None], separator_rows[None])


def solution(mesh):
    placed = (
        P("leaf", "sep", None),
        P("leaf", "sep", None),
        P("leaf", None, "sep"),
        P("leaf", None),
        P("leaf", None),
        P("leaf", "sep", None),
        P("leaf", None, None),
        P("leaf", None, None),
    )
    return jax.shard_map(
        per_device,
        mesh=mesh,
        in_specs=placed,
        out_specs=(P("leaf", "sep", None), P("leaf", "sep", None)),
        check_vma=False,
    )
```

```python
import jax
import jax.numpy as jnp
from jax import lax
from jax.experimental import pallas as pl
from jax.experimental.pallas import tpu as pltpu
from jax.sharding import PartitionSpec as P

axes = ("leaf", "sep")
f32 = jnp.float32
bf16 = jnp.bfloat16
brief, medium, long = 0, 10**9, 10**11


def swap(payload, leaf_flip, sep_flip, senders=None):
    leaves, seps = lax.axis_size("leaf"), lax.axis_size("sep")
    pairs = [
        (leaf * seps + sep, (leaf ^ leaf_flip) * seps + (sep ^ sep_flip))
        for leaf in range(leaves)
        for sep in range(seps)
        if senders is None or senders(leaf, sep)
    ]
    return lax.ppermute(payload, axes, pairs)


def quarter_swap(payload, moves):
    leaves, seps = lax.axis_size("leaf"), lax.axis_size("sep")
    size = leaves // 4
    pairs = [
        ((start * size + leaf) * seps + sep, (end * size + leaf) * seps + sep)
        for start, end in moves
        for leaf in range(size)
        for sep in range(seps)
    ]
    return lax.ppermute(payload, axes, pairs)


def after(*arrays):
    return lax.optimization_barrier(arrays)


def product(left, right, left_dim, right_dim, precision=None):
    return lax.dot_general(
        left,
        right,
        (((left_dim,), (right_dim,)), ((), ())),
        precision=precision,
        preferred_element_type=f32,
    )


def dot(left, right, left_dim=1, right_dim=0):
    return product(left, right, left_dim, right_dim, lax.Precision.HIGHEST)


def pieces_of(array):
    high = array.astype(bf16)
    return high, (array - high.astype(f32)).astype(bf16)


def dot3(left, right, left_dim=1, right_dim=0):
    left_high, left_low = pieces_of(left)
    right_high, right_low = pieces_of(right)
    small = product(left_high, right_low, left_dim, right_dim)
    small = small + product(left_low, right_high, left_dim, right_dim)
    return product(left_high, right_high, left_dim, right_dim) + small


def hot_dot(left, right, right_dim):
    high = left.astype(bf16)
    rest = left - high.astype(f32)
    middle = rest.astype(bf16)
    low = (rest - middle.astype(f32)).astype(bf16)
    out = product(jnp.concatenate([high, middle, low], 0), right, 1, right_dim)
    size = left.shape[0]
    return out[:size] + (out[size : 2 * size] + out[2 * size :])


def stage(body, shapes, *operands, scratch=(), space=pltpu.VMEM, cost=brief):
    return pl.pallas_call(
        body,
        out_shape=[
            jax.ShapeDtypeStruct(shape, f32) if isinstance(shape, tuple) else shape
            for shape in shapes
        ],
        in_specs=[pl.BlockSpec(memory_space=space)] * len(operands),
        out_specs=[pl.BlockSpec(memory_space=pltpu.VMEM)] * len(shapes),
        scratch_shapes=[
            pltpu.VMEM(shape, f32) if isinstance(shape, tuple) else shape for shape in scratch
        ],
        compiler_params=pltpu.CompilerParams(vmem_limit_bytes=16 * 2**20),
        cost_estimate=pl.CostEstimate(flops=cost, bytes_accessed=0, transcendentals=0),
    )(*operands)


def place():
    leaf, sep = lax.axis_index("leaf"), lax.axis_index("sep")
    return leaf, sep, lax.rem(leaf, 2), sep // 2, lax.rem(sep, 2)


def at(index, size):
    return pl.ds(pl.multiple_of(index * size, size), size)


def by_bit(bit, zero, one):
    return jnp.where(bit == 0, zero, one)


def per_device(
    leaf_source,
    leaf_inverse,
    leaf_update,
    row_lists,
    row_counts,
    separator_source,
    separator_inverse,
    separator_coupling,
):
    depth = row_counts.shape[1]
    source = leaf_source[0]
    inverse = leaf_inverse[0]
    update = jnp.swapaxes(leaf_update, 1, 2)[0]
    rows_source = separator_source[0]
    rows, columns = source.shape
    size = inverse.shape[1]
    updates = update.shape[1]
    capacity = updates // depth
    order = separator_inverse.shape[1]
    middle = order // 2
    packed_rows = middle // 2 + 8
    carried = middle + packed_rows
    list_rows = -(-depth // 8) * 8
    quarter = rows_source.shape[0]
    half = columns // 2
    block = columns // 8
    width = updates + 2 * quarter
    leaves = lax.axis_size("leaf")

    near = swap(source, 0, 1)
    update_near = swap(update, 0, 1)
    inverse_near = swap(inverse, 0, 1)
    rows_near = swap(rows_source, 0, 1)

    def own_columns_of(source_ref, out_ref):
        near_bit = place()[4]
        out_ref[...] = by_bit(near_bit, source_ref[:, :half], source_ref[:, half:])

    def chip_source(own_ref, near_ref, out_ref):
        near_bit = place()[4]
        out_ref[at(near_bit, rows)] = own_ref[...]
        out_ref[at(1 - near_bit, rows)] = by_bit(near_bit, near_ref[:, :half], near_ref[:, half:])

    (own_source,) = stage(own_columns_of, [(rows, half)], source)
    near, own_source = after(near, own_source)
    (chip,) = stage(chip_source, [(2 * rows, half)], own_source, near)
    far = swap(chip, 0, 2)

    def operators(coupling_ref, inverse, lists, out_ref, packed):
        near_bit = place()[4]
        out_ref[:middle] = dot(coupling_ref[at(near_bit, middle)], inverse[...])
        row = lax.broadcasted_iota(jnp.int32, (middle, middle), 0)
        lane = lax.broadcasted_iota(jnp.int32, (middle, middle), 1)
        last = inverse[middle:, middle:]
        packed[:middle, :middle] = jnp.where(row >= lane, inverse[:middle, :middle], jnp.transpose(last))
        packed[:middle, middle:] = inverse[middle:, :middle]
        packed[middle:] = jnp.zeros((2 * packed_rows - middle, order), f32)
        packed[middle : middle + 1, :middle] = jnp.sum(jnp.where(row == lane, last, 0.0), 0, keepdims=True)
        out_ref[middle:carried] = packed[at(near_bit, packed_rows)]
        out_ref[carried:] = jnp.full((list_rows, order), -1.0, f32)
        slot = lax.broadcasted_iota(jnp.int32, (1, capacity), 1)
        for level in range(depth):
            names = lists[:, level * capacity : (level + 1) * capacity]
            live = slot < lists[:, updates + level : updates + level + 1]
            out_ref[carried + level : carried + level + 1, :capacity] = jnp.where(live, names, -1).astype(f32)

    chip, coupling, own_inverse = after(chip, separator_coupling[0], separator_inverse[0])
    names_and_counts = jnp.concatenate([row_lists, row_counts], 1)
    (payload,) = stage(
        operators,
        [(carried + list_rows, order)],
        coupling,
        own_inverse,
        names_and_counts,
        scratch=[(2 * packed_rows, order)],
        cost=3 * medium,
    )

    def own_part(inverse_ref, inverse_near_ref, update_ref, update_near_ref, rows_ref, rows_near_ref, chip_ref, y_ref, all_ref, far_ref, mine_ref, update_out_ref, turned_ref):
        _, _, _, far_bit, near_bit = place()
        own, other = at(near_bit, rows), at(1 - near_bit, rows)
        all_ref[own] = inverse_ref[...]
        all_ref[other] = inverse_near_ref[...]
        update_out_ref[own] = update_ref[...]
        update_out_ref[other] = update_near_ref[...]
        whole = all_ref[...]
        first, second = whole[:, : 2 * rows], whole[:, 2 * rows :]
        far_ref[...] = by_bit(far_bit, second, first)
        y_ref[...] = dot3(by_bit(far_bit, first, second), chip_ref[...])
        mine_ref[:, :rows] = by_bit(near_bit, first[:, :rows], first[:, rows:])
        mine_ref[:, rows:] = by_bit(near_bit, second[:, :rows], second[:, rows:])
        turned, turned_near = jnp.transpose(rows_ref[...]), jnp.transpose(rows_near_ref[...])
        turned = by_bit(near_bit, turned[:half], turned[half:])
        turned_near = by_bit(near_bit, turned_near[:half], turned_near[half:])
        turned_ref[...] = by_bit(
            near_bit,
            jnp.concatenate([turned, turned_near], 1),
            jnp.concatenate([turned_near, turned], 1),
        )

    received = swap(payload, 1, 0)
    inverse_near, rows_near, payload = after(inverse_near, rows_near, payload)
    own_y, inverse_all, inverse_far, inverse_mine, update_all, turned = stage(
        own_part,
        [(2 * rows, half), (2 * rows, size), (2 * rows, 2 * rows), (2 * rows, 2 * rows), (2 * rows, updates), (half, 2 * quarter)],
        inverse,
        inverse_near,
        update,
        update_near,
        rows_source,
        rows_near,
        chip,
    )
    far, own_y = after(far, own_y)

    def leaf_part(own_ref, inverse_ref, far_ref, update_ref, turned_ref, y_ref, *refs):
        _, _, odd, far_bit, _ = place()
        out_refs, terms = refs[:-1], refs[-1]
        leaf_y = own_ref[...] + dot3(inverse_ref[...], far_ref[...])
        y_ref[...] = leaf_y
        terms[...] = dot3(leaf_y, update_ref[...], 0, 0)
        for flip, out_ref in enumerate(out_refs):
            part = at((2 * odd + far_bit) ^ flip, block)
            out_ref[:, :updates] = terms[part]
            out_ref[:, updates:] = turned_ref[part]

    leaf_y, mine, to_far, to_odd, to_both = stage(
        leaf_part,
        [(2 * rows, half)] + [(block, width)] * 4,
        own_y,
        inverse_far,
        far,
        update_all,
        turned,
        scratch=[(half, updates)],
    )
    by_both = swap(to_both, 1, 2)
    by_far = swap(to_far, 0, 2)
    by_odd = swap(to_odd, 1, 0)

    def forward(level):
        def body(carry_ref, received_ref, half_ref, next_ref):
            upper = lax.rem(place()[0] // 2 ** (level - 1), 2) == 1
            carry, received = carry_ref[:carried], received_ref[:carried]
            half_ref[...] = jnp.where(upper, carry, received)
            next_ref[...] = jnp.where(upper, received, carry)

        return body

    def last_forward(carry_ref, received_ref, half_ref, root_ref):
        part = place()[0] // (leaves // 4)
        carry, received = carry_ref[...], received_ref[...]
        half_ref[...] = jnp.where(lax.rem(part, 2) == 1, carry, received)
        root_ref[...] = jnp.where(part == 1, received[middle:], carry[middle:])

    def root_half(root_ref, received_ref, out_ref):
        part = place()[0] // (leaves // 4)
        inner = jnp.logical_or(part == 1, part == 2)
        out_ref[...] = jnp.where(inner, root_ref[...], received_ref[...])

    received, mine = after(received, mine)
    new_half, carry = stage(forward(1), [(carried, order)] * 2, payload, received)
    halves, halves_near = [new_half], [swap(new_half, 0, 1)]
    for level in range(2, depth - 1):
        reached = swap(carry, 2 ** (level - 1), 0)
        new_half, carry = stage(forward(level), [(carried, order)] * 2, carry, reached)
        halves.append(new_half)
        halves_near.append(swap(new_half, 0, 1))
    reached = quarter_swap(carry, ((1, 0), (3, 2), (2, 1)))

    def one_hots(own_ref, other_ref, hot_ref):
        rows_of_node = lax.broadcasted_iota(jnp.int32, (order, capacity), 0)
        for level in range(depth):
            for index, ref in enumerate((own_ref, other_ref)):
                names = ref[carried + level : carried + level + 1, :capacity].astype(jnp.int32)
                hot = jnp.where(rows_of_node == names, 1.0, 0.0).astype(bf16)
                hot_ref[level, :, index * capacity : (index + 1) * capacity] = hot

    carry, payload = after(carry, payload)
    (hots,) = stage(
        one_hots, [jax.ShapeDtypeStruct((depth, order, 2 * capacity), bf16)], payload, received
    )

    def transposed(all_ref, mine_ref, update_ref, y_ref, own_ref, far_ref, work):
        far_bit = place()[3]
        work[:, :half] = dot3(all_ref[...], y_ref[...], 0, 0)
        both = dot3(mine_ref[...], update_ref[...], 0, 0)
        own_ref[:, :updates] = by_bit(far_bit, both[:rows], both[rows:])
        far_ref[:, :updates] = by_bit(far_bit, both[rows:], both[:rows])
        for index in range(2):
            part = slice(updates + index * half, updates + (index + 1) * half)
            own_ref[:, part] = work[at(2 * far_bit + index, rows)]
            far_ref[:, part] = work[at(2 - 2 * far_bit + index, rows)]

    leaf_y, hots = after(leaf_y, hots)
    own_sum, far_sum = stage(
        transposed,
        [(rows, updates + columns)] * 2,
        inverse_all,
        inverse_mine,
        update_all,
        leaf_y,
        scratch=[(size, half)],
    )
    by_both, by_far, by_odd, own_sum = after(by_both, by_far, by_odd, own_sum)

    def gathered_part(mine_ref, far_ref, odd_ref, both_ref, hot_ref, residual_ref, up_ref):
        leaf, _, odd, far_bit, _ = place()

        def joined(one, two):
            first, second = one[:, updates:], two[:, updates:]
            ordered = by_bit(
                far_bit,
                jnp.concatenate([first, second], 1),
                jnp.concatenate([second, first], 1),
            )
            return one[:, :updates] + two[:, :updates], ordered

        total, own_source = joined(mine_ref[...], far_ref[...])
        total_other, other_source = joined(odd_ref[...], both_ref[...])
        odd_source = by_bit(odd, other_source, own_source)
        even_source = by_bit(odd, own_source, other_source)
        for level in range(1, depth + 1):
            part = slice((level - 1) * capacity, level * capacity)
            both = jnp.concatenate([total[:, part], total_other[:, part]], 1)
            gathered = hot_dot(both, hot_ref[level - 1], 1)
            if level == 1:
                residual_ref[...] = odd_source - gathered
            else:
                here = lax.rem(leaf - odd, 2**level) == 2 ** (level - 1)
                slot = jnp.where(here, even_source, 0.0) - gathered
                up_ref[:, (level - 2) * order : (level - 1) * order] = slot

    residual, slots = stage(
        gathered_part,
        [(block, order), (block, (depth - 1) * order)],
        mine,
        by_far,
        by_odd,
        by_both,
        hots,
        cost=3*medium,
    )
    residuals = [residual]

    def operator_of(half_ref, near_ref):
        near_bit = place()[4]
        own, other = half_ref[:middle], near_ref[:middle]
        return jnp.concatenate([by_bit(near_bit, own, other), by_bit(near_bit, other, own)], 0)

    def push(slots_ref, residual_ref, half_ref, near_ref, out_ref):
        taken = dot3(residual_ref[...], operator_of(half_ref, near_ref), 1, 1)
        out_ref[:, :order] = slots_ref[:, :order] - taken
        if out_ref.shape[1] > order:
            out_ref[:, order:] = slots_ref[:, order:]

    def blocks_of(own, other):
        near_bit = place()[4]
        row = lax.broadcasted_iota(jnp.int32, (middle, middle), 0)
        lane = lax.broadcasted_iota(jnp.int32, (middle, middle), 1)
        packed = jnp.concatenate([by_bit(near_bit, own, other), by_bit(near_bit, other, own)], 0)
        both = packed[:middle, :middle]
        last = jnp.where(row < lane, both, 0.0)
        last = jnp.where(row == lane, packed[middle : middle + 1, :middle], last)
        return jnp.where(row >= lane, both, 0.0), packed[:middle, middle:], last

    def alone(residual_ref, half_ref, near_ref, out_ref, down_ref):
        down_ref[...] = operator_of(half_ref, near_ref)
        first, below, last = blocks_of(half_ref[middle:], near_ref[middle:])
        one, two = residual_ref[:, :middle], residual_ref[:, middle:]
        upper, lower = dot3(one, first, 1, 1), dot3(one, below, 1, 1) + dot3(two, last)
        out_ref[:, :middle] = dot3(upper, first) + dot3(lower, below)
        out_ref[:, middle:] = dot3(lower, last, 1, 1)

    def level_sum(up_ref, partner_ref, residual_ref, rest_ref):
        total = up_ref[...] + partner_ref[...]
        residual_ref[...] = total[:, :order]
        rest_ref[...] = total[:, order:]

    partials, downs = [], []
    halves_near[0], residual, slots = after(halves_near[0], residual, slots)
    (going_up,) = stage(
        push, [(block, (depth - 1) * order)], slots, residual, halves[0], halves_near[0]
    )
    for level in range(2, depth):
        partner = swap(going_up, 2 ** (level - 1), 0)
        if level == depth - 1:
            reached, going_up = after(reached, going_up)
            new_half, root = stage(
                last_forward, [(carried, order), (packed_rows, order)], carry, reached
            )
            halves.append(new_half)
            from_far = swap(far_sum, 0, 2, lambda leaf, sep: sep // 2 == 1)
            halves_near.append(swap(new_half, 0, 1))
            by_root = swap(root, leaves // 4, 0)
        residual, slots = stage(
            level_sum,
            [(block, order), (block, (depth - level) * order)],
            going_up,
            partner,
            cost=3 * medium,
        )
        residuals.append(residual)
        halves_near[level - 1], residual, slots = after(halves_near[level - 1], residual, slots)
        (going_up,) = stage(
            push,
            [(block, (depth - level) * order)],
            slots,
            residual,
            halves[level - 1],
            halves_near[level - 1],
        )
    partner = swap(going_up, 2 ** (depth - 1), 0)

    for level in range(1, depth):
        residual, going_up = after(residuals[level - 1], going_up)
        partial, down = stage(
            alone,
            [(block, order), (order, order)],
            residual,
            halves[level - 1],
            halves_near[level - 1],
        )
        partials.append(partial)
        downs.append(down)
    by_root, partial = after(by_root, partial)
    (root,) = stage(root_half, [(packed_rows, order)], root, by_root)
    root_near = swap(root, 0, 1)
    partner, root = after(partner, root)

    def root_sum(up_ref, partner_ref, out_ref):
        out_ref[...] = up_ref[...] + partner_ref[...]

    (residual,) = stage(root_sum, [(block, order)], going_up, partner, cost=medium)
    root_near, residual = after(root_near, residual)

    def way_down(residual_ref, root_ref, root_near_ref, hot_ref, *refs):
        leaf, _, odd, far_bit, _ = place()
        partial_refs, down_refs = refs[: depth - 1], refs[depth - 1 : 2 * depth - 2]
        out_refs = refs[2 * depth - 2 :]
        first, below, last = blocks_of(root_ref[...], root_near_ref[...])
        one, two = residual_ref[:, :middle], residual_ref[:, middle:]
        upper, lower = dot3(one, first, 1, 1), dot3(one, below, 1, 1) + dot3(two, last)
        solved = [None] * depth
        solved[-1] = jnp.concatenate(
            [dot3(upper, first) + dot3(lower, below), dot3(lower, last, 1, 1)], 1
        )
        for level in range(depth - 1, 0, -1):
            solved[level - 1] = partial_refs[level - 1][...] - dot3(
                solved[level], down_refs[level - 1][...]
            )
        even_solved = jnp.zeros_like(solved[0])
        for level in range(2, depth + 1):
            here = lax.rem(leaf - odd, 2**level) == 2 ** (level - 1)
            even_solved = jnp.where(here, solved[level - 1], even_solved)
        own_solved = by_bit(odd, even_solved, solved[0])
        other_solved = by_bit(odd, solved[0], even_solved)
        for flip, out_ref in enumerate(out_refs):
            rows_of = other_solved if flip >= 2 else own_solved
            out_ref[:, updates:] = by_bit(
                far_bit ^ (flip % 2), rows_of[:, : 2 * quarter], rows_of[:, 2 * quarter :]
            )
        for level in range(depth):
            picked = hot_dot(solved[level], hot_ref[level], 0)
            for flip, out_ref in enumerate(out_refs):
                side = flip // 2
                out_ref[:, level * capacity : (level + 1) * capacity] = picked[
                    :, side * capacity : (side + 1) * capacity
                ]

    stay, to_far, to_odd, to_both = stage(
        way_down,
        [(block, width)] * 4,
        residual,
        root,
        root_near,
        hots,
        *partials,
        *downs,
    )
    both = swap(to_both, 1, 2)
    beyond = swap(to_far, 0, 2)
    side = swap(to_odd, 1, 0)

    def last_left(own_ref, far_ref, left_ref, keep_ref, pass_ref):
        near_bit = place()[4]
        total = own_ref[...] + far_ref[...]
        left_ref[:rows, :updates] = -total[:, :updates]
        left_ref[:rows, updates:] = jnp.zeros((rows, 2 * quarter), f32)
        row = lax.broadcasted_iota(jnp.int32, (quarter, width), 0)
        lane = lax.broadcasted_iota(jnp.int32, (quarter, width), 1)
        left_ref[rows:] = jnp.where(lane == updates + near_bit * quarter + row, 1.0, 0.0)
        first, second = total[:, updates : updates + half], total[:, updates + half :]
        keep_ref[...] = by_bit(near_bit, first, second)
        pass_ref[...] = by_bit(near_bit, second, first)

    from_far, stay = after(from_far, stay)
    left, base_keep, base_pass = stage(
        last_left, [(rows + quarter, width), (rows, half), (rows, half)], own_sum, from_far
    )
    both, beyond, side, left = after(both, beyond, side, left)

    def grouped(*refs):
        _, _, odd, far_bit, _ = place()
        out_ref = refs[-1]
        for flip, ref in enumerate(refs[:-1]):
            out_ref[at((2 * odd + far_bit) ^ flip, block)] = ref[...]

    (group,) = stage(grouped, [(half, width)], stay, beyond, side, both)
    base_near = swap(base_pass, 0, 1)
    group_near = swap(group, 0, 1)

    def own_columns(left_ref, group_ref, out_ref):
        out_ref[...] = dot3(left_ref[...], group_ref[...], 1, 1)

    (ours,) = stage(own_columns, [(rows + quarter, half)], left, group)
    group_near, ours = after(group_near, ours)

    def finish(left_ref, group_ref, ours_ref, base_ref, base_near_ref, leaf_ref, rows_ref):
        near_bit = place()[4]
        ours = ours_ref[...]
        theirs = dot3(left_ref[...], group_ref[...], 1, 1)
        ours_x, theirs_x = base_ref[...] + ours[:rows], base_near_ref[...] + theirs[:rows]
        leaf_ref[:, :half] = by_bit(near_bit, ours_x, theirs_x)
        leaf_ref[:, half:] = by_bit(near_bit, theirs_x, ours_x)
        rows_ref[:, :half] = by_bit(near_bit, ours[rows:], theirs[rows:])
        rows_ref[:, half:] = by_bit(near_bit, theirs[rows:], ours[rows:])

    leaf_x, separator_rows = stage(
        finish,
        [(rows, columns), (quarter, columns)],
        left,
        group_near,
        ours,
        base_keep,
        base_near,
    )
    return (leaf_x[None], separator_rows[None])


def solution(mesh):
    placed = (
        P("leaf", "sep", None),
        P("leaf", "sep", None),
        P("leaf", None, "sep"),
        P("leaf", None),
        P("leaf", None),
        P("leaf", "sep", None),
        P("leaf", None, None),
        P("leaf", None, None),
    )
    return jax.shard_map(
        per_device,
        mesh=mesh,
        in_specs=placed,
        out_specs=(P("leaf", "sep", None), P("leaf", "sep", None)),
        check_vma=False,
    )
```

```python
import jax
import jax.numpy as jnp
from jax import lax
from jax.experimental import pallas as pl
from jax.experimental.pallas import tpu as pltpu
from jax.sharding import PartitionSpec as P

axes = ("leaf", "sep")
f32 = jnp.float32
bf16 = jnp.bfloat16
brief, medium, long = 0, 10**9, 10**11


def swap(payload, leaf_flip, sep_flip, senders=None):
    leaves, seps = lax.axis_size("leaf"), lax.axis_size("sep")
    pairs = [
        (leaf * seps + sep, (leaf ^ leaf_flip) * seps + (sep ^ sep_flip))
        for leaf in range(leaves)
        for sep in range(seps)
        if senders is None or senders(leaf, sep)
    ]
    return lax.ppermute(payload, axes, pairs)


def quarter_swap(payload, moves):
    leaves, seps = lax.axis_size("leaf"), lax.axis_size("sep")
    size = leaves // 4
    pairs = [
        ((start * size + leaf) * seps + sep, (end * size + leaf) * seps + sep)
        for start, end in moves
        for leaf in range(size)
        for sep in range(seps)
    ]
    return lax.ppermute(payload, axes, pairs)


def after(*arrays):
    return lax.optimization_barrier(arrays)


def product(left, right, left_dim, right_dim, precision=None):
    return lax.dot_general(
        left,
        right,
        (((left_dim,), (right_dim,)), ((), ())),
        precision=precision,
        preferred_element_type=f32,
    )


def dot(left, right, left_dim=1, right_dim=0):
    return product(left, right, left_dim, right_dim, lax.Precision.HIGHEST)


def pieces_of(array):
    high = array.astype(bf16)
    return high, (array - high.astype(f32)).astype(bf16)


def dot3(left, right, left_dim=1, right_dim=0):
    left_high, left_low = pieces_of(left)
    right_high, right_low = pieces_of(right)
    small = product(left_high, right_low, left_dim, right_dim)
    small = small + product(left_low, right_high, left_dim, right_dim)
    return product(left_high, right_high, left_dim, right_dim) + small


def hot_dot(left, right, right_dim):
    high, low = pieces_of(left)
    out = product(jnp.concatenate([high, low], 0), right, 1, right_dim)
    return out[: left.shape[0]] + out[left.shape[0] :]


def stage(body, shapes, *operands, scratch=(), space=pltpu.VMEM, cost=brief):
    return pl.pallas_call(
        body,
        out_shape=[
            jax.ShapeDtypeStruct(shape, f32) if isinstance(shape, tuple) else shape
            for shape in shapes
        ],
        in_specs=[pl.BlockSpec(memory_space=space)] * len(operands),
        out_specs=[pl.BlockSpec(memory_space=pltpu.VMEM)] * len(shapes),
        scratch_shapes=[
            pltpu.VMEM(shape, f32) if isinstance(shape, tuple) else shape for shape in scratch
        ],
        compiler_params=pltpu.CompilerParams(vmem_limit_bytes=16 * 2**20),
        cost_estimate=pl.CostEstimate(flops=cost, bytes_accessed=0, transcendentals=0),
    )(*operands)


def place():
    leaf, sep = lax.axis_index("leaf"), lax.axis_index("sep")
    return leaf, sep, lax.rem(leaf, 2), sep // 2, lax.rem(sep, 2)


def at(index, size):
    return pl.ds(pl.multiple_of(index * size, size), size)


def by_bit(bit, zero, one):
    return jnp.where(bit == 0, zero, one)


def per_device(
    leaf_source,
    leaf_inverse,
    leaf_update,
    row_lists,
    row_counts,
    separator_source,
    separator_inverse,
    separator_coupling,
):
    depth = row_counts.shape[1]
    source = leaf_source[0]
    inverse = leaf_inverse[0]
    update = jnp.swapaxes(leaf_update, 1, 2)[0]
    rows_source = separator_source[0]
    rows, columns = source.shape
    size = inverse.shape[1]
    updates = update.shape[1]
    capacity = updates // depth
    order = separator_inverse.shape[1]
    middle = order // 2
    packed_rows = middle // 2 + 8
    carried = middle + packed_rows
    list_rows = -(-depth // 8) * 8
    quarter = rows_source.shape[0]
    half = columns // 2
    block = columns // 8
    width = updates + 2 * quarter
    leaves = lax.axis_size("leaf")

    near = swap(source, 0, 1)
    update_near = swap(update, 0, 1)
    inverse_near = swap(inverse, 0, 1)
    rows_near = swap(rows_source, 0, 1)

    def own_columns_of(source_ref, out_ref):
        near_bit = place()[4]
        out_ref[...] = by_bit(near_bit, source_ref[:, :half], source_ref[:, half:])

    def chip_source(own_ref, near_ref, out_ref):
        near_bit = place()[4]
        out_ref[at(near_bit, rows)] = own_ref[...]
        out_ref[at(1 - near_bit, rows)] = by_bit(near_bit, near_ref[:, :half], near_ref[:, half:])

    (own_source,) = stage(own_columns_of, [(rows, half)], source)
    near, own_source = after(near, own_source)
    (chip,) = stage(chip_source, [(2 * rows, half)], own_source, near)
    far = swap(chip, 0, 2)

    def operators(coupling_ref, inverse, lists, out_ref, packed, square):
        near_bit = place()[4]
        out_ref[:middle] = dot(coupling_ref[at(near_bit, middle)], inverse[...])
        square[...] = dot(inverse[...], inverse[...], 0, 0)
        row = lax.broadcasted_iota(jnp.int32, (middle, middle), 0)
        lane = lax.broadcasted_iota(jnp.int32, (middle, middle), 1)
        last = square[middle:, middle:]
        packed[:middle, :middle] = jnp.where(row >= lane, square[:middle, :middle], last)
        packed[:middle, middle:] = square[middle:, :middle]
        packed[middle:] = jnp.zeros((2 * packed_rows - middle, order), f32)
        packed[middle : middle + 1, :middle] = jnp.sum(jnp.where(row == lane, last, 0.0), 0, keepdims=True)
        out_ref[middle:carried] = packed[at(near_bit, packed_rows)]
        out_ref[carried:] = jnp.full((list_rows, order), -1.0, f32)
        slot = lax.broadcasted_iota(jnp.int32, (1, capacity), 1)
        for level in range(depth):
            names = lists[:, level * capacity : (level + 1) * capacity]
            live = slot < lists[:, updates + level : updates + level + 1]
            out_ref[carried + level : carried + level + 1, :capacity] = jnp.where(live, names, -1).astype(f32)

    chip, coupling, own_inverse = after(chip, separator_coupling[0], separator_inverse[0])
    names_and_counts = jnp.concatenate([row_lists, row_counts], 1)
    (payload,) = stage(
        operators,
        [(carried + list_rows, order)],
        coupling,
        own_inverse,
        names_and_counts,
        scratch=[(2 * packed_rows, order), (order, order)],
        cost=3 * medium,
    )

    def own_part(inverse_ref, inverse_near_ref, update_ref, update_near_ref, rows_ref, rows_near_ref, chip_ref, y_ref, all_ref, far_ref, mine_ref, update_out_ref, turned_ref):
        _, _, _, far_bit, near_bit = place()
        own, other = at(near_bit, rows), at(1 - near_bit, rows)
        all_ref[own] = inverse_ref[...]
        all_ref[other] = inverse_near_ref[...]
        update_out_ref[own] = update_ref[...]
        update_out_ref[other] = update_near_ref[...]
        whole = all_ref[...]
        first, second = whole[:, : 2 * rows], whole[:, 2 * rows :]
        far_ref[...] = by_bit(far_bit, second, first)
        y_ref[...] = dot3(by_bit(far_bit, first, second), chip_ref[...])
        mine_ref[:, :rows] = by_bit(near_bit, first[:, :rows], first[:, rows:])
        mine_ref[:, rows:] = by_bit(near_bit, second[:, :rows], second[:, rows:])
        turned, turned_near = jnp.transpose(rows_ref[...]), jnp.transpose(rows_near_ref[...])
        turned = by_bit(near_bit, turned[:half], turned[half:])
        turned_near = by_bit(near_bit, turned_near[:half], turned_near[half:])
        turned_ref[...] = by_bit(
            near_bit,
            jnp.concatenate([turned, turned_near], 1),
            jnp.concatenate([turned_near, turned], 1),
        )

    received = swap(payload, 1, 0)
    inverse_near, rows_near, payload = after(inverse_near, rows_near, payload)
    own_y, inverse_all, inverse_far, inverse_mine, update_all, turned = stage(
        own_part,
        [(2 * rows, half), (2 * rows, size), (2 * rows, 2 * rows), (2 * rows, 2 * rows), (2 * rows, updates), (half, 2 * quarter)],
        inverse,
        inverse_near,
        update,
        update_near,
        rows_source,
        rows_near,
        chip,
    )
    far, own_y = after(far, own_y)

    def leaf_part(own_ref, inverse_ref, far_ref, update_ref, turned_ref, y_ref, *refs):
        _, _, odd, far_bit, _ = place()
        out_refs, terms = refs[:-1], refs[-1]
        leaf_y = own_ref[...] + dot3(inverse_ref[...], far_ref[...])
        y_ref[...] = leaf_y
        terms[...] = dot3(leaf_y, update_ref[...], 0, 0)
        for flip, out_ref in enumerate(out_refs):
            part = at((2 * odd + far_bit) ^ flip, block)
            out_ref[:, :updates] = terms[part]
            out_ref[:, updates:] = turned_ref[part]

    leaf_y, mine, to_far, to_odd, to_both = stage(
        leaf_part,
        [(2 * rows, half)] + [(block, width)] * 4,
        own_y,
        inverse_far,
        far,
        update_all,
        turned,
        scratch=[(half, updates)],
    )
    by_both = swap(to_both, 1, 2)
    by_far = swap(to_far, 0, 2)
    by_odd = swap(to_odd, 1, 0)

    def forward(level):
        def body(carry_ref, received_ref, half_ref, next_ref):
            upper = lax.rem(place()[0] // 2 ** (level - 1), 2) == 1
            carry, received = carry_ref[:carried], received_ref[:carried]
            half_ref[...] = jnp.where(upper, carry, received)
            next_ref[...] = jnp.where(upper, received, carry)

        return body

    def last_forward(carry_ref, received_ref, half_ref, root_ref):
        part = place()[0] // (leaves // 4)
        carry, received = carry_ref[...], received_ref[...]
        half_ref[...] = jnp.where(lax.rem(part, 2) == 1, carry, received)
        root_ref[...] = jnp.where(part == 1, received[middle:], carry[middle:])

    def root_half(root_ref, received_ref, out_ref):
        part = place()[0] // (leaves // 4)
        inner = jnp.logical_or(part == 1, part == 2)
        out_ref[...] = jnp.where(inner, root_ref[...], received_ref[...])

    received, mine = after(received, mine)
    new_half, carry = stage(forward(1), [(carried, order)] * 2, payload, received)
    halves, halves_near = [new_half], [swap(new_half, 0, 1)]
    for level in range(2, depth - 1):
        reached = swap(carry, 2 ** (level - 1), 0)
        new_half, carry = stage(forward(level), [(carried, order)] * 2, carry, reached)
        halves.append(new_half)
        halves_near.append(swap(new_half, 0, 1))
    reached = quarter_swap(carry, ((1, 0), (3, 2), (2, 1)))

    def one_hots(own_ref, other_ref, hot_ref):
        rows_of_node = lax.broadcasted_iota(jnp.int32, (order, capacity), 0)
        for level in range(depth):
            for index, ref in enumerate((own_ref, other_ref)):
                names = ref[carried + level : carried + level + 1, :capacity].astype(jnp.int32)
                hot = jnp.where(rows_of_node == names, 1.0, 0.0).astype(bf16)
                hot_ref[level, :, index * capacity : (index + 1) * capacity] = hot

    carry, payload = after(carry, payload)
    (hots,) = stage(
        one_hots, [jax.ShapeDtypeStruct((depth, order, 2 * capacity), bf16)], payload, received
    )

    def transposed(all_ref, mine_ref, update_ref, y_ref, own_ref, far_ref, work):
        far_bit = place()[3]
        work[:, :half] = dot3(all_ref[...], y_ref[...], 0, 0)
        both = dot3(mine_ref[...], update_ref[...], 0, 0)
        own_ref[:, :updates] = by_bit(far_bit, both[:rows], both[rows:])
        far_ref[:, :updates] = by_bit(far_bit, both[rows:], both[:rows])
        for index in range(2):
            part = slice(updates + index * half, updates + (index + 1) * half)
            own_ref[:, part] = work[at(2 * far_bit + index, rows)]
            far_ref[:, part] = work[at(2 - 2 * far_bit + index, rows)]

    leaf_y, hots = after(leaf_y, hots)
    own_sum, far_sum = stage(
        transposed,
        [(rows, updates + columns)] * 2,
        inverse_all,
        inverse_mine,
        update_all,
        leaf_y,
        scratch=[(size, half)],
    )
    by_both, by_far, by_odd, own_sum = after(by_both, by_far, by_odd, own_sum)

    def gathered_part(mine_ref, far_ref, odd_ref, both_ref, hot_ref, residual_ref, up_ref):
        leaf, _, odd, far_bit, _ = place()

        def joined(one, two):
            first, second = one[:, updates:], two[:, updates:]
            ordered = by_bit(
                far_bit,
                jnp.concatenate([first, second], 1),
                jnp.concatenate([second, first], 1),
            )
            return one[:, :updates] + two[:, :updates], ordered

        total, own_source = joined(mine_ref[...], far_ref[...])
        total_other, other_source = joined(odd_ref[...], both_ref[...])
        odd_source = by_bit(odd, other_source, own_source)
        even_source = by_bit(odd, own_source, other_source)
        for level in range(1, depth + 1):
            part = slice((level - 1) * capacity, level * capacity)
            both = jnp.concatenate([total[:, part], total_other[:, part]], 1)
            gathered = hot_dot(both, hot_ref[level - 1], 1)
            if level == 1:
                residual_ref[...] = odd_source - gathered
            else:
                here = lax.rem(leaf - odd, 2**level) == 2 ** (level - 1)
                slot = jnp.where(here, even_source, 0.0) - gathered
                up_ref[:, (level - 2) * order : (level - 1) * order] = slot

    residual, slots = stage(
        gathered_part,
        [(block, order), (block, (depth - 1) * order)],
        mine,
        by_far,
        by_odd,
        by_both,
        hots,
        cost=3*medium,
    )
    residuals = [residual]

    def operator_of(half_ref, near_ref):
        near_bit = place()[4]
        own, other = half_ref[:middle], near_ref[:middle]
        return jnp.concatenate([by_bit(near_bit, own, other), by_bit(near_bit, other, own)], 0)

    def push(slots_ref, residual_ref, half_ref, near_ref, out_ref):
        taken = dot3(residual_ref[...], operator_of(half_ref, near_ref), 1, 1)
        out_ref[:, :order] = slots_ref[:, :order] - taken
        if out_ref.shape[1] > order:
            out_ref[:, order:] = slots_ref[:, order:]

    def squared(residual, own, other):
        near_bit = place()[4]
        row = lax.broadcasted_iota(jnp.int32, (middle, middle), 0)
        lane = lax.broadcasted_iota(jnp.int32, (middle, middle), 1)
        packed = jnp.concatenate([by_bit(near_bit, own, other), by_bit(near_bit, other, own)], 0)
        both, below = packed[:middle, :middle], packed[:middle, middle:]
        lower, upper = jnp.where(row > lane, both, 0.0), jnp.where(row < lane, both, 0.0)
        first = jnp.where(row >= lane, both, 0.0)
        last = jnp.where(row == lane, packed[middle : middle + 1, :middle], upper)
        one, two = residual[:, :middle], residual[:, middle:]
        return jnp.concatenate(
            [
                dot3(one, first) + dot3(one, lower, 1, 1) + dot3(two, below),
                dot3(one, below, 1, 1) + dot3(two, last) + dot3(two, upper, 1, 1),
            ],
            1,
        )

    def alone(residual_ref, half_ref, near_ref, out_ref, down_ref):
        down_ref[...] = operator_of(half_ref, near_ref)
        out_ref[...] = squared(residual_ref[...], half_ref[middle:], near_ref[middle:])

    def below_root(*refs):
        count = depth - 1
        partial_refs, down_refs = refs[:count], refs[count : 2 * count]
        base_ref, high_ref, low_ref = refs[2 * count :]
        base, taken = partial_refs[-1][...], -down_refs[-1][...]
        for level in range(depth - 1, 0, -1):
            if level < depth - 1:
                down = down_refs[level - 1][...]
                base = partial_refs[level - 1][...] - dot3(base, down)
                taken = -dot3(taken, down)
            part = slice((level - 1) * order, level * order)
            base_ref[:, part] = base
            high_ref[:, part], low_ref[:, part] = pieces_of(taken)

    def level_sum(up_ref, partner_ref, residual_ref, rest_ref):
        total = up_ref[...] + partner_ref[...]
        residual_ref[...] = total[:, :order]
        rest_ref[...] = total[:, order:]

    partials, downs = [], []
    halves_near[0], residual, slots = after(halves_near[0], residual, slots)
    (going_up,) = stage(
        push, [(block, (depth - 1) * order)], slots, residual, halves[0], halves_near[0]
    )
    for level in range(2, depth):
        partner = swap(going_up, 2 ** (level - 1), 0)
        if level == depth - 1:
            reached, going_up = after(reached, going_up)
            new_half, root = stage(
                last_forward, [(carried, order), (packed_rows, order)], carry, reached
            )
            halves.append(new_half)
            from_far = swap(far_sum, 0, 2, lambda leaf, sep: sep // 2 == 1)
            halves_near.append(swap(new_half, 0, 1))
            by_root = swap(root, leaves // 4, 0)
        residual, slots = stage(
            level_sum,
            [(block, order), (block, (depth - level) * order)],
            going_up,
            partner,
            cost=3 * medium,
        )
        residuals.append(residual)
        halves_near[level - 1], residual, slots = after(halves_near[level - 1], residual, slots)
        (going_up,) = stage(
            push,
            [(block, (depth - level) * order)],
            slots,
            residual,
            halves[level - 1],
            halves_near[level - 1],
        )
    partner = swap(going_up, 2 ** (depth - 1), 0)

    for level in range(1, depth):
        residual, going_up = after(residuals[level - 1], going_up)
        partial, down = stage(
            alone,
            [(block, order), (order, order)],
            residual,
            halves[level - 1],
            halves_near[level - 1],
        )
        partials.append(partial)
        downs.append(down)
    by_root, partial = after(by_root, partial)
    (root,) = stage(root_half, [(packed_rows, order)], root, by_root)
    root_near = swap(root, 0, 1)
    partials[-1], root = after(partials[-1], root)
    pieces = jax.ShapeDtypeStruct((order, (depth - 1) * order), bf16)
    base, taken_high, taken_low = stage(
        below_root, [(block, (depth - 1) * order), pieces, pieces], *partials, *downs
    )
    partner, root, base = after(partner, root, base)

    def root_sum(up_ref, partner_ref, out_ref):
        out_ref[...] = up_ref[...] + partner_ref[...]

    (residual,) = stage(root_sum, [(block, order)], going_up, partner, cost=medium)
    root_near, residual = after(root_near, residual)

    def way_down(residual_ref, root_ref, root_near_ref, hot_ref, base_ref, high_ref, low_ref, *out_refs):
        leaf, _, odd, far_bit, _ = place()
        top = squared(residual_ref[...], root_ref[...], root_near_ref[...])
        high, low = pieces_of(top)
        large = product(jnp.concatenate([high, low], 0), high_ref[...], 1, 0)
        small = large[block:] + product(high, low_ref[...], 1, 0)
        under = base_ref[...] + (large[:block] + small)
        solved = [under[:, level * order : (level + 1) * order] for level in range(depth - 1)]
        solved.append(top)
        even_solved = jnp.zeros_like(solved[0])
        for level in range(2, depth + 1):
            here = lax.rem(leaf - odd, 2**level) == 2 ** (level - 1)
            even_solved = jnp.where(here, solved[level - 1], even_solved)
        own_solved = by_bit(odd, even_solved, solved[0])
        other_solved = by_bit(odd, solved[0], even_solved)
        for flip, out_ref in enumerate(out_refs):
            rows_of = other_solved if flip >= 2 else own_solved
            out_ref[:, updates:] = by_bit(
                far_bit ^ (flip % 2), rows_of[:, : 2 * quarter], rows_of[:, 2 * quarter :]
            )
        for level in range(depth):
            picked = hot_dot(solved[level], hot_ref[level], 0)
            for flip, out_ref in enumerate(out_refs):
                side = flip // 2
                out_ref[:, level * capacity : (level + 1) * capacity] = picked[
                    :, side * capacity : (side + 1) * capacity
                ]

    stay, to_far, to_odd, to_both = stage(
        way_down,
        [(block, width)] * 4,
        residual,
        root,
        root_near,
        hots,
        base,
        taken_high,
        taken_low,
    )
    both = swap(to_both, 1, 2)
    beyond = swap(to_far, 0, 2)
    side = swap(to_odd, 1, 0)

    def last_left(own_ref, far_ref, left_ref, keep_ref, pass_ref):
        near_bit = place()[4]
        total = own_ref[...] + far_ref[...]
        left_ref[:rows, :updates] = -total[:, :updates]
        left_ref[:rows, updates:] = jnp.zeros((rows, 2 * quarter), f32)
        row = lax.broadcasted_iota(jnp.int32, (quarter, width), 0)
        lane = lax.broadcasted_iota(jnp.int32, (quarter, width), 1)
        left_ref[rows:] = jnp.where(lane == updates + near_bit * quarter + row, 1.0, 0.0)
        first, second = total[:, updates : updates + half], total[:, updates + half :]
        keep_ref[...] = by_bit(near_bit, first, second)
        pass_ref[...] = by_bit(near_bit, second, first)

    from_far, stay = after(from_far, stay)
    left, base_keep, base_pass = stage(
        last_left, [(rows + quarter, width), (rows, half), (rows, half)], own_sum, from_far
    )
    both, beyond, side, left = after(both, beyond, side, left)

    def grouped(*refs):
        _, _, odd, far_bit, _ = place()
        out_ref = refs[-1]
        for flip, ref in enumerate(refs[:-1]):
            out_ref[at((2 * odd + far_bit) ^ flip, block)] = ref[...]

    (group,) = stage(grouped, [(half, width)], stay, beyond, side, both)
    base_near = swap(base_pass, 0, 1)
    group_near = swap(group, 0, 1)

    def own_columns(left_ref, group_ref, out_ref):
        out_ref[...] = dot3(left_ref[...], group_ref[...], 1, 1)

    (ours,) = stage(own_columns, [(rows + quarter, half)], left, group)
    group_near, ours = after(group_near, ours)

    def finish(left_ref, group_ref, ours_ref, base_ref, base_near_ref, leaf_ref, rows_ref):
        near_bit = place()[4]
        ours = ours_ref[...]
        theirs = dot3(left_ref[...], group_ref[...], 1, 1)
        ours_x, theirs_x = base_ref[...] + ours[:rows], base_near_ref[...] + theirs[:rows]
        leaf_ref[:, :half] = by_bit(near_bit, ours_x, theirs_x)
        leaf_ref[:, half:] = by_bit(near_bit, theirs_x, ours_x)
        rows_ref[:, :half] = by_bit(near_bit, ours[rows:], theirs[rows:])
        rows_ref[:, half:] = by_bit(near_bit, theirs[rows:], ours[rows:])

    leaf_x, separator_rows = stage(
        finish,
        [(rows, columns), (quarter, columns)],
        left,
        group_near,
        ours,
        base_keep,
        base_near,
    )
    return (leaf_x[None], separator_rows[None])


def solution(mesh):
    placed = (
        P("leaf", "sep", None),
        P("leaf", "sep", None),
        P("leaf", None, "sep"),
        P("leaf", None),
        P("leaf", None),
        P("leaf", "sep", None),
        P("leaf", None, None),
        P("leaf", None, None),
    )
    return jax.shard_map(
        per_device,
        mesh=mesh,
        in_specs=placed,
        out_specs=(P("leaf", "sep", None), P("leaf", "sep", None)),
        check_vma=False,
    )
```

```python
import jax
import jax.numpy as jnp
from jax import lax
from jax.experimental import pallas as pl
from jax.experimental.pallas import tpu as pltpu
from jax.sharding import PartitionSpec as P

axes = ("leaf", "sep")
f32 = jnp.float32
bf16 = jnp.bfloat16
brief, medium, long = 0, 10**9, 10**11


def swap(payload, leaf_flip, sep_flip, senders=None):
    leaves, seps = lax.axis_size("leaf"), lax.axis_size("sep")
    pairs = [
        (leaf * seps + sep, (leaf ^ leaf_flip) * seps + (sep ^ sep_flip))
        for leaf in range(leaves)
        for sep in range(seps)
        if senders is None or senders(leaf, sep)
    ]
    return lax.ppermute(payload, axes, pairs)


def quarter_swap(payload, moves):
    leaves, seps = lax.axis_size("leaf"), lax.axis_size("sep")
    size = leaves // 4
    pairs = [
        ((start * size + leaf) * seps + sep, (end * size + leaf) * seps + sep)
        for start, end in moves
        for leaf in range(size)
        for sep in range(seps)
    ]
    return lax.ppermute(payload, axes, pairs)


def after(*arrays):
    return lax.optimization_barrier(arrays)


def product(left, right, left_dim, right_dim, precision=None):
    return lax.dot_general(
        left,
        right,
        (((left_dim,), (right_dim,)), ((), ())),
        precision=precision,
        preferred_element_type=f32,
    )


def dot(left, right, left_dim=1, right_dim=0):
    return product(left, right, left_dim, right_dim, lax.Precision.HIGHEST)


def pieces_of(array):
    high = array.astype(bf16)
    return high, (array - high.astype(f32)).astype(bf16)


def dot3(left, right, left_dim=1, right_dim=0):
    left_high, left_low = pieces_of(left)
    right_high, right_low = pieces_of(right)
    small = product(left_high, right_low, left_dim, right_dim)
    small = small + product(left_low, right_high, left_dim, right_dim)
    return product(left_high, right_high, left_dim, right_dim) + small


def hot_dot(left, right, right_dim):
    high, low = pieces_of(left)
    out = product(jnp.concatenate([high, low], 0), right, 1, right_dim)
    return out[: left.shape[0]] + out[left.shape[0] :]


def stage(body, shapes, *operands, scratch=(), space=pltpu.VMEM, cost=brief):
    return pl.pallas_call(
        body,
        out_shape=[
            jax.ShapeDtypeStruct(shape, f32) if isinstance(shape, tuple) else shape
            for shape in shapes
        ],
        in_specs=[pl.BlockSpec(memory_space=space)] * len(operands),
        out_specs=[pl.BlockSpec(memory_space=pltpu.VMEM)] * len(shapes),
        scratch_shapes=[
            pltpu.VMEM(shape, f32) if isinstance(shape, tuple) else shape for shape in scratch
        ],
        compiler_params=pltpu.CompilerParams(vmem_limit_bytes=16 * 2**20),
        cost_estimate=pl.CostEstimate(flops=cost, bytes_accessed=0, transcendentals=0),
    )(*operands)


def place():
    leaf, sep = lax.axis_index("leaf"), lax.axis_index("sep")
    return leaf, sep, lax.rem(leaf, 2), sep // 2, lax.rem(sep, 2)


def at(index, size):
    return pl.ds(pl.multiple_of(index * size, size), size)


def by_bit(bit, zero, one):
    return jnp.where(bit == 0, zero, one)


def per_device(
    leaf_source,
    leaf_inverse,
    leaf_update,
    row_lists,
    row_counts,
    separator_source,
    separator_inverse,
    separator_coupling,
):
    depth = row_counts.shape[1]
    source = leaf_source[0]
    inverse = leaf_inverse[0]
    update = jnp.swapaxes(leaf_update, 1, 2)[0]
    rows_source = separator_source[0]
    rows, columns = source.shape
    size = inverse.shape[1]
    updates = update.shape[1]
    capacity = updates // depth
    order = separator_inverse.shape[1]
    middle = order // 2
    packed_rows = middle // 2 + 8
    carried = middle + packed_rows
    list_rows = -(-depth // 8) * 8
    quarter = rows_source.shape[0]
    half = columns // 2
    block = columns // 8
    width = updates + 2 * quarter
    leaves = lax.axis_size("leaf")

    near = swap(source, 0, 1)
    update_near = swap(update, 0, 1)
    inverse_near = swap(inverse, 0, 1)
    rows_near = swap(rows_source, 0, 1)

    def own_columns_of(source_ref, out_ref):
        near_bit = place()[4]
        out_ref[...] = by_bit(near_bit, source_ref[:, :half], source_ref[:, half:])

    def chip_source(own_ref, near_ref, out_ref):
        near_bit = place()[4]
        out_ref[at(near_bit, rows)] = own_ref[...]
        out_ref[at(1 - near_bit, rows)] = by_bit(near_bit, near_ref[:, :half], near_ref[:, half:])

    (own_source,) = stage(own_columns_of, [(rows, half)], source)
    near, own_source = after(near, own_source)
    (chip,) = stage(chip_source, [(2 * rows, half)], own_source, near)
    far = swap(chip, 0, 2)

    def operators(coupling_ref, inverse, lists, out_ref, packed, square):
        near_bit = place()[4]
        out_ref[:middle] = dot3(coupling_ref[at(near_bit, middle)], inverse[...])
        square[...] = dot3(inverse[...], inverse[...], 0, 0)
        row = lax.broadcasted_iota(jnp.int32, (middle, middle), 0)
        lane = lax.broadcasted_iota(jnp.int32, (middle, middle), 1)
        last = square[middle:, middle:]
        packed[:middle, :middle] = jnp.where(row >= lane, square[:middle, :middle], last)
        packed[:middle, middle:] = square[middle:, :middle]
        packed[middle:] = jnp.zeros((2 * packed_rows - middle, order), f32)
        packed[middle : middle + 1, :middle] = jnp.sum(jnp.where(row == lane, last, 0.0), 0, keepdims=True)
        out_ref[middle:carried] = packed[at(near_bit, packed_rows)]
        out_ref[carried:] = jnp.full((list_rows, order), -1.0, f32)
        slot = lax.broadcasted_iota(jnp.int32, (1, capacity), 1)
        for level in range(depth):
            names = lists[:, level * capacity : (level + 1) * capacity]
            live = slot < lists[:, updates + level : updates + level + 1]
            out_ref[carried + level : carried + level + 1, :capacity] = jnp.where(live, names, -1).astype(f32)

    chip, coupling, own_inverse = after(chip, separator_coupling[0], separator_inverse[0])
    names_and_counts = jnp.concatenate([row_lists, row_counts], 1)
    (payload,) = stage(
        operators,
        [(carried + list_rows, order)],
        coupling,
        own_inverse,
        names_and_counts,
        scratch=[(2 * packed_rows, order), (order, order)],
        cost=3 * medium,
    )

    def own_part(inverse_ref, inverse_near_ref, update_ref, update_near_ref, rows_ref, rows_near_ref, chip_ref, y_ref, all_ref, far_ref, mine_ref, update_out_ref, turned_ref):
        _, _, _, far_bit, near_bit = place()
        own, other = at(near_bit, rows), at(1 - near_bit, rows)
        all_ref[own] = inverse_ref[...]
        all_ref[other] = inverse_near_ref[...]
        update_out_ref[own] = update_ref[...]
        update_out_ref[other] = update_near_ref[...]
        whole = all_ref[...]
        first, second = whole[:, : 2 * rows], whole[:, 2 * rows :]
        far_ref[...] = by_bit(far_bit, second, first)
        y_ref[...] = dot3(by_bit(far_bit, first, second), chip_ref[...])
        chip_block = by_bit(far_bit, first, second)
        mine_ref[...] = by_bit(near_bit, chip_block[:, :rows], chip_block[:, rows:])
        turned, turned_near = jnp.transpose(rows_ref[...]), jnp.transpose(rows_near_ref[...])
        turned = by_bit(near_bit, turned[:half], turned[half:])
        turned_near = by_bit(near_bit, turned_near[:half], turned_near[half:])
        turned_ref[...] = by_bit(
            near_bit,
            jnp.concatenate([turned, turned_near], 1),
            jnp.concatenate([turned_near, turned], 1),
        )

    received = swap(payload, 1, 0)
    inverse_near, rows_near, payload = after(inverse_near, rows_near, payload)
    own_y, inverse_all, inverse_far, inverse_mine, update_all, turned = stage(
        own_part,
        [(2 * rows, half), (2 * rows, size), (2 * rows, 2 * rows), (2 * rows, rows), (2 * rows, updates), (half, 2 * quarter)],
        inverse,
        inverse_near,
        update,
        update_near,
        rows_source,
        rows_near,
        chip,
    )

    def turned_update(far_ref, mine_ref, update_ref, y_ref, turned_far_ref, turned_mine_ref, terms_ref):
        update = update_ref[...]
        turned_far_ref[...] = dot3(far_ref[...], update, 0, 0)
        turned_mine_ref[...] = dot3(mine_ref[...], update, 0, 0)
        terms_ref[...] = dot3(y_ref[...], update, 0, 0)

    turned_far, own_sum, own_terms = stage(
        turned_update,
        [(2 * rows, updates), (rows, updates), (half, updates)],
        inverse_far,
        inverse_mine,
        update_all,
        own_y,
    )
    far, own_terms = after(far, own_terms)

    def leaf_part(own_ref, turned_far_ref, far_ref, turned_ref, *refs):
        _, _, odd, far_bit, _ = place()
        out_refs, terms = refs[:-1], refs[-1]
        terms[...] = own_ref[...] + dot3(far_ref[...], turned_far_ref[...], 0, 0)
        for flip, out_ref in enumerate(out_refs):
            part = at((2 * odd + far_bit) ^ flip, block)
            out_ref[:, :updates] = terms[part]
            out_ref[:, updates:] = turned_ref[part]

    mine, to_far, to_odd, to_both = stage(
        leaf_part,
        [(block, width)] * 4,
        own_terms,
        turned_far,
        far,
        turned,
        scratch=[(half, updates)],
    )
    by_both = swap(to_both, 1, 2)
    by_far = swap(to_far, 0, 2)
    by_odd = swap(to_odd, 1, 0)

    def forward(level):
        def body(carry_ref, received_ref, half_ref, next_ref):
            upper = lax.rem(place()[0] // 2 ** (level - 1), 2) == 1
            carry, received = carry_ref[:carried], received_ref[:carried]
            half_ref[...] = jnp.where(upper, carry, received)
            next_ref[...] = jnp.where(upper, received, carry)

        return body

    def last_forward(carry_ref, received_ref, half_ref, root_ref):
        part = place()[0] // (leaves // 4)
        carry, received = carry_ref[...], received_ref[...]
        half_ref[...] = jnp.where(lax.rem(part, 2) == 1, carry, received)
        root_ref[...] = jnp.where(part == 1, received[middle:], carry[middle:])

    def root_half(root_ref, received_ref, out_ref):
        part = place()[0] // (leaves // 4)
        inner = jnp.logical_or(part == 1, part == 2)
        out_ref[...] = jnp.where(inner, root_ref[...], received_ref[...])

    received, mine = after(received, mine)
    new_half, carry = stage(forward(1), [(carried, order)] * 2, payload, received)
    halves, halves_near = [new_half], [swap(new_half, 0, 1)]
    for level in range(2, depth - 1):
        reached = swap(carry, 2 ** (level - 1), 0)
        new_half, carry = stage(forward(level), [(carried, order)] * 2, carry, reached)
        halves.append(new_half)
        halves_near.append(swap(new_half, 0, 1))
    reached = quarter_swap(carry, ((1, 0), (3, 2), (2, 1)))

    def one_hots(own_ref, other_ref, hot_ref):
        rows_of_node = lax.broadcasted_iota(jnp.int32, (order, capacity), 0)
        for level in range(depth):
            for index, ref in enumerate((own_ref, other_ref)):
                names = ref[carried + level : carried + level + 1, :capacity].astype(jnp.int32)
                hot = jnp.where(rows_of_node == names, 1.0, 0.0).astype(bf16)
                hot_ref[level, :, index * capacity : (index + 1) * capacity] = hot

    carry, payload = after(carry, payload)
    (hots,) = stage(
        one_hots, [jax.ShapeDtypeStruct((depth, order, 2 * capacity), bf16)], payload, received
    )

    def transposed(all_ref, inverse_far_ref, own_y_ref, far_ref, turned_far_ref, own_ref, out_ref, work):
        _, _, _, far_bit, near_bit = place()
        leaf_y = own_y_ref[...] + dot3(inverse_far_ref[...], far_ref[...])
        work[...] = dot3(all_ref[...], leaf_y, 0, 0)
        out_ref[:, :updates] = turned_far_ref[at(near_bit, rows)]
        for index in range(2):
            part = slice(index * half, (index + 1) * half)
            shifted = slice(updates + index * half, updates + (index + 1) * half)
            own_ref[:, part] = work[at(2 * far_bit + index, rows)]
            out_ref[:, shifted] = work[at(2 - 2 * far_bit + index, rows)]

    own_y, hots = after(own_y, hots)
    own_ys, far_sum = stage(
        transposed,
        [(rows, columns), (rows, updates + columns)],
        inverse_all,
        inverse_far,
        own_y,
        far,
        turned_far,
        scratch=[(size, half)],
    )
    by_both, by_far, by_odd, own_ys = after(by_both, by_far, by_odd, own_ys)

    def gathered_part(mine_ref, far_ref, odd_ref, both_ref, hot_ref, residual_ref, up_ref):
        leaf, _, odd, far_bit, _ = place()

        def joined(one, two):
            first, second = one[:, updates:], two[:, updates:]
            ordered = by_bit(
                far_bit,
                jnp.concatenate([first, second], 1),
                jnp.concatenate([second, first], 1),
            )
            return one[:, :updates] + two[:, :updates], ordered

        total, own_source = joined(mine_ref[...], far_ref[...])
        total_other, other_source = joined(odd_ref[...], both_ref[...])
        odd_source = by_bit(odd, other_source, own_source)
        even_source = by_bit(odd, own_source, other_source)
        for level in range(1, depth + 1):
            part = slice((level - 1) * capacity, level * capacity)
            both = jnp.concatenate([total[:, part], total_other[:, part]], 1)
            gathered = hot_dot(both, hot_ref[level - 1], 1)
            if level == 1:
                residual_ref[...] = odd_source - gathered
            else:
                here = lax.rem(leaf - odd, 2**level) == 2 ** (level - 1)
                slot = jnp.where(here, even_source, 0.0) - gathered
                up_ref[:, (level - 2) * order : (level - 1) * order] = slot

    residual, slots = stage(
        gathered_part,
        [(block, order), (block, (depth - 1) * order)],
        mine,
        by_far,
        by_odd,
        by_both,
        hots,
        cost=3*medium,
    )
    residuals = [residual]

    def operator_of(half_ref, near_ref):
        near_bit = place()[4]
        own, other = half_ref[:middle], near_ref[:middle]
        return jnp.concatenate([by_bit(near_bit, own, other), by_bit(near_bit, other, own)], 0)

    def push(slots_ref, residual_ref, half_ref, near_ref, out_ref):
        taken = dot3(residual_ref[...], operator_of(half_ref, near_ref), 1, 1)
        out_ref[:, :order] = slots_ref[:, :order] - taken
        if out_ref.shape[1] > order:
            out_ref[:, order:] = slots_ref[:, order:]

    def squared(residual, own, other):
        near_bit = place()[4]
        row = lax.broadcasted_iota(jnp.int32, (middle, middle), 0)
        lane = lax.broadcasted_iota(jnp.int32, (middle, middle), 1)
        packed = jnp.concatenate([by_bit(near_bit, own, other), by_bit(near_bit, other, own)], 0)
        both, below = packed[:middle, :middle], packed[:middle, middle:]
        lower, upper = jnp.where(row > lane, both, 0.0), jnp.where(row < lane, both, 0.0)
        first = jnp.where(row >= lane, both, 0.0)
        last = jnp.where(row == lane, packed[middle : middle + 1, :middle], upper)
        one, two = residual[:, :middle], residual[:, middle:]
        return jnp.concatenate(
            [
                dot3(one, first) + dot3(one, lower, 1, 1) + dot3(two, below),
                dot3(one, below, 1, 1) + dot3(two, last) + dot3(two, upper, 1, 1),
            ],
            1,
        )

    def alone(residual_ref, half_ref, near_ref, out_ref, down_ref):
        down_ref[...] = operator_of(half_ref, near_ref)
        out_ref[...] = squared(residual_ref[...], half_ref[middle:], near_ref[middle:])

    def below_root(*refs):
        count = depth - 1
        partial_refs, down_refs = refs[:count], refs[count : 2 * count]
        base_ref, high_ref, low_ref = refs[2 * count :]
        base, taken = partial_refs[-1][...], -down_refs[-1][...]
        for level in range(depth - 1, 0, -1):
            if level < depth - 1:
                down = down_refs[level - 1][...]
                base = partial_refs[level - 1][...] - dot3(base, down)
                taken = -dot3(taken, down)
            part = slice((level - 1) * order, level * order)
            base_ref[:, part] = base
            high_ref[:, part], low_ref[:, part] = pieces_of(taken)

    def level_sum(up_ref, partner_ref, residual_ref, rest_ref):
        total = up_ref[...] + partner_ref[...]
        residual_ref[...] = total[:, :order]
        rest_ref[...] = total[:, order:]

    partials, downs = [], []
    halves_near[0], residual, slots = after(halves_near[0], residual, slots)
    (going_up,) = stage(
        push, [(block, (depth - 1) * order)], slots, residual, halves[0], halves_near[0]
    )
    for level in range(2, depth):
        partner = swap(going_up, 2 ** (level - 1), 0)
        if level == depth - 1:
            reached, going_up = after(reached, going_up)
            new_half, root = stage(
                last_forward, [(carried, order), (packed_rows, order)], carry, reached
            )
            halves.append(new_half)
            from_far = swap(far_sum, 0, 2, lambda leaf, sep: sep // 2 == 1)
            halves_near.append(swap(new_half, 0, 1))
            by_root = swap(root, leaves // 4, 0)
        residual, slots = stage(
            level_sum,
            [(block, order), (block, (depth - level) * order)],
            going_up,
            partner,
            cost=2 * medium,
        )
        residuals.append(residual)
        halves_near[level - 1], residual, slots = after(halves_near[level - 1], residual, slots)
        (going_up,) = stage(
            push,
            [(block, (depth - level) * order)],
            slots,
            residual,
            halves[level - 1],
            halves_near[level - 1],
        )
    partner = swap(going_up, 2 ** (depth - 1), 0)

    for level in range(1, depth):
        residual, going_up = after(residuals[level - 1], going_up)
        partial, down = stage(
            alone,
            [(block, order), (order, order)],
            residual,
            halves[level - 1],
            halves_near[level - 1],
        )
        partials.append(partial)
        downs.append(down)
    by_root, partial = after(by_root, partial)
    (root,) = stage(root_half, [(packed_rows, order)], root, by_root)
    root_near = swap(root, 0, 1)
    partials[-1], root = after(partials[-1], root)
    pieces = jax.ShapeDtypeStruct((order, (depth - 1) * order), bf16)
    base, taken_high, taken_low = stage(
        below_root, [(block, (depth - 1) * order), pieces, pieces], *partials, *downs
    )
    partner, root, base = after(partner, root, base)

    def root_sum(up_ref, partner_ref, out_ref):
        out_ref[...] = up_ref[...] + partner_ref[...]

    (residual,) = stage(root_sum, [(block, order)], going_up, partner, cost=medium)
    root_near, residual = after(root_near, residual)

    def way_down(residual_ref, root_ref, root_near_ref, hot_ref, base_ref, high_ref, low_ref, *out_refs):
        leaf, _, odd, far_bit, _ = place()
        top = squared(residual_ref[...], root_ref[...], root_near_ref[...])
        high, low = pieces_of(top)
        large = product(jnp.concatenate([high, low], 0), high_ref[...], 1, 0)
        small = large[block:] + product(high, low_ref[...], 1, 0)
        under = base_ref[...] + (large[:block] + small)
        solved = [under[:, level * order : (level + 1) * order] for level in range(depth - 1)]
        solved.append(top)
        even_solved = jnp.zeros_like(solved[0])
        for level in range(2, depth + 1):
            here = lax.rem(leaf - odd, 2**level) == 2 ** (level - 1)
            even_solved = jnp.where(here, solved[level - 1], even_solved)
        own_solved = by_bit(odd, even_solved, solved[0])
        other_solved = by_bit(odd, solved[0], even_solved)
        for flip, out_ref in enumerate(out_refs):
            rows_of = other_solved if flip >= 2 else own_solved
            out_ref[:, updates:] = by_bit(
                far_bit ^ (flip % 2), rows_of[:, : 2 * quarter], rows_of[:, 2 * quarter :]
            )
        for level in range(depth):
            picked = hot_dot(solved[level], hot_ref[level], 0)
            for flip, out_ref in enumerate(out_refs):
                side = flip // 2
                out_ref[:, level * capacity : (level + 1) * capacity] = picked[
                    :, side * capacity : (side + 1) * capacity
                ]

    stay, to_far, to_odd, to_both = stage(
        way_down,
        [(block, width)] * 4,
        residual,
        root,
        root_near,
        hots,
        base,
        taken_high,
        taken_low,
    )
    both = swap(to_both, 1, 2)
    beyond = swap(to_far, 0, 2)
    side = swap(to_odd, 1, 0)

    def last_left(own_ref, own_y_ref, far_ref, left_ref, keep_ref, pass_ref):
        near_bit = place()[4]
        left_ref[:rows, :updates] = -(own_ref[...] + far_ref[:, :updates])
        left_ref[:rows, updates:] = jnp.zeros((rows, 2 * quarter), f32)
        row = lax.broadcasted_iota(jnp.int32, (quarter, width), 0)
        lane = lax.broadcasted_iota(jnp.int32, (quarter, width), 1)
        left_ref[rows:] = jnp.where(lane == updates + near_bit * quarter + row, 1.0, 0.0)
        total = own_y_ref[...] + far_ref[:, updates:]
        first, second = total[:, :half], total[:, half:]
        keep_ref[...] = by_bit(near_bit, first, second)
        pass_ref[...] = by_bit(near_bit, second, first)

    from_far, stay = after(from_far, stay)
    left, base_keep, base_pass = stage(
        last_left, [(rows + quarter, width), (rows, half), (rows, half)], own_sum, own_ys, from_far
    )
    both, beyond, side, left = after(both, beyond, side, left)

    def grouped(*refs):
        _, _, odd, far_bit, _ = place()
        out_ref = refs[-1]
        for flip, ref in enumerate(refs[:-1]):
            out_ref[at((2 * odd + far_bit) ^ flip, block)] = ref[...]

    (group,) = stage(grouped, [(half, width)], stay, beyond, side, both)
    base_near = swap(base_pass, 0, 1)
    group_near = swap(group, 0, 1)

    def own_columns(left_ref, group_ref, out_ref):
        out_ref[...] = dot3(left_ref[...], group_ref[...], 1, 1)

    (ours,) = stage(own_columns, [(rows + quarter, half)], left, group)
    group_near, ours = after(group_near, ours)

    def finish(left_ref, group_ref, ours_ref, base_ref, base_near_ref, leaf_ref, rows_ref):
        near_bit = place()[4]
        ours = ours_ref[...]
        theirs = dot3(left_ref[...], group_ref[...], 1, 1)
        ours_x, theirs_x = base_ref[...] + ours[:rows], base_near_ref[...] + theirs[:rows]
        leaf_ref[:, :half] = by_bit(near_bit, ours_x, theirs_x)
        leaf_ref[:, half:] = by_bit(near_bit, theirs_x, ours_x)
        rows_ref[:, :half] = by_bit(near_bit, ours[rows:], theirs[rows:])
        rows_ref[:, half:] = by_bit(near_bit, theirs[rows:], ours[rows:])

    leaf_x, separator_rows = stage(
        finish,
        [(rows, columns), (quarter, columns)],
        left,
        group_near,
        ours,
        base_keep,
        base_near,
    )
    return (leaf_x[None], separator_rows[None])


def solution(mesh):
    placed = (
        P("leaf", "sep", None),
        P("leaf", "sep", None),
        P("leaf", None, "sep"),
        P("leaf", None),
        P("leaf", None),
        P("leaf", "sep", None),
        P("leaf", None, None),
        P("leaf", None, None),
    )
    return jax.shard_map(
        per_device,
        mesh=mesh,
        in_specs=placed,
        out_specs=(P("leaf", "sep", None), P("leaf", "sep", None)),
        check_vma=False,
    )
```

```python
import jax
import jax.numpy as jnp
from jax import lax
from jax.experimental import pallas as pl
from jax.experimental.pallas import tpu as pltpu
from jax.sharding import PartitionSpec as P

axes = ("leaf", "sep")
f32 = jnp.float32
bf16 = jnp.bfloat16
brief, medium, long = 0, 10**9, 10**11


def swap(payload, leaf_flip, sep_flip, senders=None):
    leaves, seps = lax.axis_size("leaf"), lax.axis_size("sep")
    pairs = [
        (leaf * seps + sep, (leaf ^ leaf_flip) * seps + (sep ^ sep_flip))
        for leaf in range(leaves)
        for sep in range(seps)
        if senders is None or senders(leaf, sep)
    ]
    return lax.ppermute(payload, axes, pairs)


def quarter_swap(payload, moves):
    leaves, seps = lax.axis_size("leaf"), lax.axis_size("sep")
    size = leaves // 4
    pairs = [
        ((start * size + leaf) * seps + sep, (end * size + leaf) * seps + sep)
        for start, end in moves
        for leaf in range(size)
        for sep in range(seps)
    ]
    return lax.ppermute(payload, axes, pairs)


def after(*arrays):
    return lax.optimization_barrier(arrays)


def product(left, right, left_dim, right_dim, precision=None):
    return lax.dot_general(
        left,
        right,
        (((left_dim,), (right_dim,)), ((), ())),
        precision=precision,
        preferred_element_type=f32,
    )


def dot(left, right, left_dim=1, right_dim=0):
    return product(left, right, left_dim, right_dim, lax.Precision.HIGHEST)


def pieces_of(array):
    high = array.astype(bf16)
    return high, (array - high.astype(f32)).astype(bf16)


def dot3(left, right, left_dim=1, right_dim=0):
    left_high, left_low = pieces_of(left)
    right_high, right_low = pieces_of(right)
    small = product(left_high, right_low, left_dim, right_dim)
    small = small + product(left_low, right_high, left_dim, right_dim)
    return product(left_high, right_high, left_dim, right_dim) + small


def hot_dot(left, right, right_dim):
    high, low = pieces_of(left)
    out = product(jnp.concatenate([high, low], 0), right, 1, right_dim)
    return out[: left.shape[0]] + out[left.shape[0] :]


def stage(body, shapes, *operands, scratch=(), space=pltpu.VMEM, cost=brief):
    return pl.pallas_call(
        body,
        out_shape=[
            jax.ShapeDtypeStruct(shape, f32) if isinstance(shape, tuple) else shape
            for shape in shapes
        ],
        in_specs=[pl.BlockSpec(memory_space=space)] * len(operands),
        out_specs=[pl.BlockSpec(memory_space=pltpu.VMEM)] * len(shapes),
        scratch_shapes=[
            pltpu.VMEM(shape, f32) if isinstance(shape, tuple) else shape for shape in scratch
        ],
        compiler_params=pltpu.CompilerParams(vmem_limit_bytes=16 * 2**20),
        cost_estimate=pl.CostEstimate(flops=cost, bytes_accessed=0, transcendentals=0),
    )(*operands)


def place():
    leaf, sep = lax.axis_index("leaf"), lax.axis_index("sep")
    return leaf, sep, lax.rem(leaf, 2), sep // 2, lax.rem(sep, 2)


def at(index, size):
    return pl.ds(pl.multiple_of(index * size, size), size)


def by_bit(bit, zero, one):
    return jnp.where(bit == 0, zero, one)


def per_device(
    leaf_source,
    leaf_inverse,
    leaf_update,
    row_lists,
    row_counts,
    separator_source,
    separator_inverse,
    separator_coupling,
):
    depth = row_counts.shape[1]
    source = leaf_source[0]
    inverse = leaf_inverse[0]
    update = jnp.swapaxes(leaf_update, 1, 2)[0]
    rows_source = separator_source[0]
    rows, columns = source.shape
    size = inverse.shape[1]
    updates = update.shape[1]
    capacity = updates // depth
    order = separator_inverse.shape[1]
    middle = order // 2
    packed_rows = middle // 2 + 8
    carried = middle + packed_rows
    list_rows = -(-depth // 8) * 8
    quarter = rows_source.shape[0]
    half = columns // 2
    block = columns // 8
    width = updates + 2 * quarter
    leaves = lax.axis_size("leaf")

    near = swap(source, 0, 1)
    update_near = swap(update, 0, 1)
    inverse_near = swap(inverse, 0, 1)
    rows_near = swap(rows_source, 0, 1)

    def own_columns_of(source_ref, out_ref):
        near_bit = place()[4]
        out_ref[...] = by_bit(near_bit, source_ref[:, :half], source_ref[:, half:])

    def chip_source(own_ref, near_ref, out_ref):
        near_bit = place()[4]
        out_ref[at(near_bit, rows)] = own_ref[...]
        out_ref[at(1 - near_bit, rows)] = by_bit(near_bit, near_ref[:, :half], near_ref[:, half:])

    (own_source,) = stage(own_columns_of, [(rows, half)], source)
    near, own_source = after(near, own_source)
    (chip,) = stage(chip_source, [(2 * rows, half)], own_source, near)
    far = swap(chip, 0, 2)

    def operators(coupling_ref, inverse, lists, out_ref, packed, square):
        near_bit = place()[4]
        out_ref[:middle] = dot3(coupling_ref[at(near_bit, middle)], inverse[...])
        square[...] = dot3(inverse[...], inverse[...], 0, 0)
        row = lax.broadcasted_iota(jnp.int32, (middle, middle), 0)
        lane = lax.broadcasted_iota(jnp.int32, (middle, middle), 1)
        last = square[middle:, middle:]
        packed[:middle, :middle] = jnp.where(row >= lane, square[:middle, :middle], last)
        packed[:middle, middle:] = square[middle:, :middle]
        packed[middle:] = jnp.zeros((2 * packed_rows - middle, order), f32)
        packed[middle : middle + 1, :middle] = jnp.sum(jnp.where(row == lane, last, 0.0), 0, keepdims=True)
        out_ref[middle:carried] = packed[at(near_bit, packed_rows)]
        out_ref[carried:] = jnp.full((list_rows, order), -1.0, f32)
        slot = lax.broadcasted_iota(jnp.int32, (1, capacity), 1)
        for level in range(depth):
            names = lists[:, level * capacity : (level + 1) * capacity]
            live = slot < lists[:, updates + level : updates + level + 1]
            out_ref[carried + level : carried + level + 1, :capacity] = jnp.where(live, names, -1).astype(f32)

    chip, coupling, own_inverse = after(chip, separator_coupling[0], separator_inverse[0])
    names_and_counts = jnp.concatenate([row_lists, row_counts], 1)
    (payload,) = stage(
        operators,
        [(carried + list_rows, order)],
        coupling,
        own_inverse,
        names_and_counts,
        scratch=[(2 * packed_rows, order), (order, order)],
        cost=3 * medium,
    )

    def own_part(inverse_ref, inverse_near_ref, update_ref, update_near_ref, chip_ref, y_ref, all_ref, far_ref, mine_ref, update_out_ref):
        _, _, _, far_bit, near_bit = place()
        own, other = at(near_bit, rows), at(1 - near_bit, rows)
        all_ref[own] = inverse_ref[...]
        all_ref[other] = inverse_near_ref[...]
        update_out_ref[own] = update_ref[...]
        update_out_ref[other] = update_near_ref[...]
        whole = all_ref[...]
        first, second = whole[:, : 2 * rows], whole[:, 2 * rows :]
        far_ref[...] = by_bit(far_bit, second, first)
        y_ref[...] = dot3(by_bit(far_bit, first, second), chip_ref[...])
        chip_block = by_bit(far_bit, first, second)
        mine_ref[...] = by_bit(near_bit, chip_block[:, :rows], chip_block[:, rows:])

    received = swap(payload, 1, 0)
    inverse_near, payload = after(inverse_near, payload)
    own_y, inverse_all, inverse_far, inverse_mine, update_all = stage(
        own_part,
        [(2 * rows, half), (2 * rows, size), (2 * rows, 2 * rows), (2 * rows, rows), (2 * rows, updates)],
        inverse,
        inverse_near,
        update,
        update_near,
        chip,
    )

    def turned_update(far_ref, mine_ref, update_ref, y_ref, turned_far_ref, turned_mine_ref, terms_ref):
        update = update_ref[...]
        turned_far_ref[...] = dot3(far_ref[...], update, 0, 0)
        turned_mine_ref[...] = dot3(mine_ref[...], update, 0, 0)
        terms_ref[...] = dot3(y_ref[...], update, 0, 0)

    turned_far, own_sum, own_terms = stage(
        turned_update,
        [(2 * rows, updates), (rows, updates), (half, updates)],
        inverse_far,
        inverse_mine,
        update_all,
        own_y,
    )

    def turned_rows(rows_ref, rows_near_ref, out_ref):
        near_bit = place()[4]
        turned, turned_near = jnp.transpose(rows_ref[...]), jnp.transpose(rows_near_ref[...])
        turned = by_bit(near_bit, turned[:half], turned[half:])
        turned_near = by_bit(near_bit, turned_near[:half], turned_near[half:])
        out_ref[...] = by_bit(
            near_bit,
            jnp.concatenate([turned, turned_near], 1),
            jnp.concatenate([turned_near, turned], 1),
        )

    rows_near, own_terms = after(rows_near, own_terms)
    (turned,) = stage(turned_rows, [(half, 2 * quarter)], rows_source, rows_near)
    far, turned = after(far, turned)

    def leaf_part(own_ref, turned_far_ref, far_ref, turned_ref, *refs):
        _, _, odd, far_bit, _ = place()
        out_refs, terms = refs[:-1], refs[-1]
        terms[...] = own_ref[...] + dot3(far_ref[...], turned_far_ref[...], 0, 0)
        for flip, out_ref in enumerate(out_refs):
            part = at((2 * odd + far_bit) ^ flip, block)
            out_ref[:, :updates] = terms[part]
            out_ref[:, updates:] = turned_ref[part]

    mine, to_far, to_odd, to_both = stage(
        leaf_part,
        [(block, width)] * 4,
        own_terms,
        turned_far,
        far,
        turned,
        scratch=[(half, updates)],
    )
    by_both = swap(to_both, 1, 2)
    by_far = swap(to_far, 0, 2)
    by_odd = swap(to_odd, 1, 0)

    def forward(level):
        def body(carry_ref, received_ref, half_ref, next_ref):
            upper = lax.rem(place()[0] // 2 ** (level - 1), 2) == 1
            carry, received = carry_ref[:carried], received_ref[:carried]
            half_ref[...] = jnp.where(upper, carry, received)
            next_ref[...] = jnp.where(upper, received, carry)

        return body

    def last_forward(carry_ref, received_ref, half_ref, root_ref):
        part = place()[0] // (leaves // 4)
        carry, received = carry_ref[...], received_ref[...]
        half_ref[...] = jnp.where(lax.rem(part, 2) == 1, carry, received)
        root_ref[...] = jnp.where(part == 1, received[middle:], carry[middle:])

    def root_half(root_ref, received_ref, out_ref):
        part = place()[0] // (leaves // 4)
        inner = jnp.logical_or(part == 1, part == 2)
        out_ref[...] = jnp.where(inner, root_ref[...], received_ref[...])

    received, mine = after(received, mine)
    new_half, carry = stage(forward(1), [(carried, order)] * 2, payload, received)
    halves, halves_near = [new_half], [swap(new_half, 0, 1)]
    for level in range(2, depth - 1):
        reached = swap(carry, 2 ** (level - 1), 0)
        new_half, carry = stage(forward(level), [(carried, order)] * 2, carry, reached)
        halves.append(new_half)
        halves_near.append(swap(new_half, 0, 1))
    reached = quarter_swap(carry, ((1, 0), (3, 2), (2, 1)))

    def one_hots(own_ref, other_ref, hot_ref):
        rows_of_node = lax.broadcasted_iota(jnp.int32, (order, capacity), 0)
        for level in range(depth):
            for index, ref in enumerate((own_ref, other_ref)):
                names = ref[carried + level : carried + level + 1, :capacity].astype(jnp.int32)
                hot = jnp.where(rows_of_node == names, 1.0, 0.0).astype(bf16)
                hot_ref[level, :, index * capacity : (index + 1) * capacity] = hot

    carry, payload = after(carry, payload)
    (hots,) = stage(
        one_hots, [jax.ShapeDtypeStruct((depth, order, 2 * capacity), bf16)], payload, received
    )

    def transposed(all_ref, inverse_far_ref, own_y_ref, far_ref, turned_far_ref, own_ref, out_ref, work):
        _, _, _, far_bit, near_bit = place()
        leaf_y = own_y_ref[...] + dot3(inverse_far_ref[...], far_ref[...])
        work[...] = dot3(all_ref[...], leaf_y, 0, 0)
        out_ref[:, :updates] = turned_far_ref[at(near_bit, rows)]
        for index in range(2):
            part = slice(index * half, (index + 1) * half)
            shifted = slice(updates + index * half, updates + (index + 1) * half)
            own_ref[:, part] = work[at(2 * far_bit + index, rows)]
            out_ref[:, shifted] = work[at(2 - 2 * far_bit + index, rows)]

    own_y, hots = after(own_y, hots)
    own_ys, far_sum = stage(
        transposed,
        [(rows, columns), (rows, updates + columns)],
        inverse_all,
        inverse_far,
        own_y,
        far,
        turned_far,
        scratch=[(size, half)],
    )
    by_both, by_far, by_odd, own_ys = after(by_both, by_far, by_odd, own_ys)

    def gathered_part(mine_ref, far_ref, odd_ref, both_ref, hot_ref, residual_ref, up_ref):
        leaf, _, odd, far_bit, _ = place()

        def joined(one, two):
            first, second = one[:, updates:], two[:, updates:]
            ordered = by_bit(
                far_bit,
                jnp.concatenate([first, second], 1),
                jnp.concatenate([second, first], 1),
            )
            return one[:, :updates] + two[:, :updates], ordered

        total, own_source = joined(mine_ref[...], far_ref[...])
        total_other, other_source = joined(odd_ref[...], both_ref[...])
        odd_source = by_bit(odd, other_source, own_source)
        even_source = by_bit(odd, own_source, other_source)
        for level in range(1, depth + 1):
            part = slice((level - 1) * capacity, level * capacity)
            both = jnp.concatenate([total[:, part], total_other[:, part]], 1)
            gathered = hot_dot(both, hot_ref[level - 1], 1)
            if level == 1:
                residual_ref[...] = odd_source - gathered
            else:
                here = lax.rem(leaf - odd, 2**level) == 2 ** (level - 1)
                slot = jnp.where(here, even_source, 0.0) - gathered
                up_ref[:, (level - 2) * order : (level - 1) * order] = slot

    residual, slots = stage(
        gathered_part,
        [(block, order), (block, (depth - 1) * order)],
        mine,
        by_far,
        by_odd,
        by_both,
        hots,
        cost=3*medium,
    )
    residuals = [residual]

    def operator_of(half_ref, near_ref):
        near_bit = place()[4]
        own, other = half_ref[:middle], near_ref[:middle]
        return jnp.concatenate([by_bit(near_bit, own, other), by_bit(near_bit, other, own)], 0)

    def push(slots_ref, residual_ref, half_ref, near_ref, out_ref):
        taken = dot3(residual_ref[...], operator_of(half_ref, near_ref), 1, 1)
        out_ref[:, :order] = slots_ref[:, :order] - taken
        if out_ref.shape[1] > order:
            out_ref[:, order:] = slots_ref[:, order:]

    def squared(residual, own, other):
        near_bit = place()[4]
        row = lax.broadcasted_iota(jnp.int32, (middle, middle), 0)
        lane = lax.broadcasted_iota(jnp.int32, (middle, middle), 1)
        packed = jnp.concatenate([by_bit(near_bit, own, other), by_bit(near_bit, other, own)], 0)
        both, below = packed[:middle, :middle], packed[:middle, middle:]
        lower, upper = jnp.where(row > lane, both, 0.0), jnp.where(row < lane, both, 0.0)
        first = jnp.where(row >= lane, both, 0.0)
        last = jnp.where(row == lane, packed[middle : middle + 1, :middle], upper)
        one, two = residual[:, :middle], residual[:, middle:]
        return jnp.concatenate(
            [
                dot3(one, first) + dot3(one, lower, 1, 1) + dot3(two, below),
                dot3(one, below, 1, 1) + dot3(two, last) + dot3(two, upper, 1, 1),
            ],
            1,
        )

    def alone(residual_ref, half_ref, near_ref, out_ref, down_ref):
        down_ref[...] = operator_of(half_ref, near_ref)
        out_ref[...] = squared(residual_ref[...], half_ref[middle:], near_ref[middle:])

    def below_root(*refs):
        count = depth - 1
        partial_refs, down_refs = refs[:count], refs[count : 2 * count]
        base_ref, high_ref, low_ref = refs[2 * count :]
        base, taken = partial_refs[-1][...], -down_refs[-1][...]
        for level in range(depth - 1, 0, -1):
            if level < depth - 1:
                down = down_refs[level - 1][...]
                base = partial_refs[level - 1][...] - dot3(base, down)
                taken = -dot3(taken, down)
            part = slice((level - 1) * order, level * order)
            base_ref[:, part] = base
            high_ref[:, part], low_ref[:, part] = pieces_of(taken)

    def level_sum(up_ref, partner_ref, residual_ref, rest_ref):
        total = up_ref[...] + partner_ref[...]
        residual_ref[...] = total[:, :order]
        rest_ref[...] = total[:, order:]

    partials, downs = [], []
    halves_near[0], residual, slots = after(halves_near[0], residual, slots)
    (going_up,) = stage(
        push, [(block, (depth - 1) * order)], slots, residual, halves[0], halves_near[0]
    )
    for level in range(2, depth):
        partner = swap(going_up, 2 ** (level - 1), 0)
        if level == depth - 1:
            reached, going_up = after(reached, going_up)
            new_half, root = stage(
                last_forward, [(carried, order), (packed_rows, order)], carry, reached
            )
            halves.append(new_half)
            from_far = swap(far_sum, 0, 2, lambda leaf, sep: sep // 2 == 1)
            halves_near.append(swap(new_half, 0, 1))
            by_root = swap(root, leaves // 4, 0)
        residual, slots = stage(
            level_sum,
            [(block, order), (block, (depth - level) * order)],
            going_up,
            partner,
            cost=2 * medium,
        )
        residuals.append(residual)
        halves_near[level - 1], residual, slots = after(halves_near[level - 1], residual, slots)
        (going_up,) = stage(
            push,
            [(block, (depth - level) * order)],
            slots,
            residual,
            halves[level - 1],
            halves_near[level - 1],
        )
    partner = swap(going_up, 2 ** (depth - 1), 0)

    for level in range(1, depth):
        residual, going_up = after(residuals[level - 1], going_up)
        partial, down = stage(
            alone,
            [(block, order), (order, order)],
            residual,
            halves[level - 1],
            halves_near[level - 1],
        )
        partials.append(partial)
        downs.append(down)
    by_root, partial = after(by_root, partial)
    (root,) = stage(root_half, [(packed_rows, order)], root, by_root)
    root_near = swap(root, 0, 1)
    partials[-1], root = after(partials[-1], root)
    pieces = jax.ShapeDtypeStruct((order, (depth - 1) * order), bf16)
    base, taken_high, taken_low = stage(
        below_root, [(block, (depth - 1) * order), pieces, pieces], *partials, *downs
    )
    partner, root, base = after(partner, root, base)

    def root_sum(up_ref, partner_ref, out_ref):
        out_ref[...] = up_ref[...] + partner_ref[...]

    (residual,) = stage(root_sum, [(block, order)], going_up, partner, cost=medium)
    root_near, residual = after(root_near, residual)

    def way_down(residual_ref, root_ref, root_near_ref, hot_ref, base_ref, high_ref, low_ref, *out_refs):
        leaf, _, odd, far_bit, _ = place()
        top = squared(residual_ref[...], root_ref[...], root_near_ref[...])
        high, low = pieces_of(top)
        large = product(jnp.concatenate([high, low], 0), high_ref[...], 1, 0)
        small = large[block:] + product(high, low_ref[...], 1, 0)
        under = base_ref[...] + (large[:block] + small)
        solved = [under[:, level * order : (level + 1) * order] for level in range(depth - 1)]
        solved.append(top)
        even_solved = jnp.zeros_like(solved[0])
        for level in range(2, depth + 1):
            here = lax.rem(leaf - odd, 2**level) == 2 ** (level - 1)
            even_solved = jnp.where(here, solved[level - 1], even_solved)
        own_solved = by_bit(odd, even_solved, solved[0])
        other_solved = by_bit(odd, solved[0], even_solved)
        for flip, out_ref in enumerate(out_refs):
            rows_of = other_solved if flip >= 2 else own_solved
            out_ref[:, updates:] = by_bit(
                far_bit ^ (flip % 2), rows_of[:, : 2 * quarter], rows_of[:, 2 * quarter :]
            )
        for level in range(depth):
            picked = hot_dot(solved[level], hot_ref[level], 0)
            for flip, out_ref in enumerate(out_refs):
                side = flip // 2
                out_ref[:, level * capacity : (level + 1) * capacity] = picked[
                    :, side * capacity : (side + 1) * capacity
                ]

    stay, to_far, to_odd, to_both = stage(
        way_down,
        [(block, width)] * 4,
        residual,
        root,
        root_near,
        hots,
        base,
        taken_high,
        taken_low,
    )
    both = swap(to_both, 1, 2)
    beyond = swap(to_far, 0, 2)
    side = swap(to_odd, 1, 0)

    def last_left(own_ref, own_y_ref, far_ref, left_ref, keep_ref, pass_ref):
        near_bit = place()[4]
        left_ref[:rows, :updates] = -(own_ref[...] + far_ref[:, :updates])
        left_ref[:rows, updates:] = jnp.zeros((rows, 2 * quarter), f32)
        row = lax.broadcasted_iota(jnp.int32, (quarter, width), 0)
        lane = lax.broadcasted_iota(jnp.int32, (quarter, width), 1)
        left_ref[rows:] = jnp.where(lane == updates + near_bit * quarter + row, 1.0, 0.0)
        total = own_y_ref[...] + far_ref[:, updates:]
        first, second = total[:, :half], total[:, half:]
        keep_ref[...] = by_bit(near_bit, first, second)
        pass_ref[...] = by_bit(near_bit, second, first)

    from_far, stay = after(from_far, stay)
    left, base_keep, base_pass = stage(
        last_left, [(rows + quarter, width), (rows, half), (rows, half)], own_sum, own_ys, from_far
    )
    both, beyond, side, left = after(both, beyond, side, left)

    def grouped(*refs):
        _, _, odd, far_bit, _ = place()
        out_ref = refs[-1]
        for flip, ref in enumerate(refs[:-1]):
            out_ref[at((2 * odd + far_bit) ^ flip, block)] = ref[...]

    (group,) = stage(grouped, [(half, width)], stay, beyond, side, both)
    base_near = swap(base_pass, 0, 1)
    group_near = swap(group, 0, 1)

    def own_columns(left_ref, group_ref, out_ref):
        out_ref[...] = dot3(left_ref[...], group_ref[...], 1, 1)

    (ours,) = stage(own_columns, [(rows + quarter, half)], left, group)
    group_near, ours = after(group_near, ours)

    def finish(left_ref, group_ref, ours_ref, base_ref, base_near_ref, leaf_ref, rows_ref):
        near_bit = place()[4]
        ours = ours_ref[...]
        theirs = dot3(left_ref[...], group_ref[...], 1, 1)
        ours_x, theirs_x = base_ref[...] + ours[:rows], base_near_ref[...] + theirs[:rows]
        leaf_ref[:, :half] = by_bit(near_bit, ours_x, theirs_x)
        leaf_ref[:, half:] = by_bit(near_bit, theirs_x, ours_x)
        rows_ref[:, :half] = by_bit(near_bit, ours[rows:], theirs[rows:])
        rows_ref[:, half:] = by_bit(near_bit, theirs[rows:], ours[rows:])

    leaf_x, separator_rows = stage(
        finish,
        [(rows, columns), (quarter, columns)],
        left,
        group_near,
        ours,
        base_keep,
        base_near,
    )
    return (leaf_x[None], separator_rows[None])


def solution(mesh):
    placed = (
        P("leaf", "sep", None),
        P("leaf", "sep", None),
        P("leaf", None, "sep"),
        P("leaf", None),
        P("leaf", None),
        P("leaf", "sep", None),
        P("leaf", None, None),
        P("leaf", None, None),
    )
    return jax.shard_map(
        per_device,
        mesh=mesh,
        in_specs=placed,
        out_specs=(P("leaf", "sep", None), P("leaf", "sep", None)),
        check_vma=False,
    )
```

```python
import jax
import jax.numpy as jnp
from jax import lax
from jax.experimental import pallas as pl
from jax.experimental.pallas import tpu as pltpu
from jax.sharding import PartitionSpec as P

axes = ("leaf", "sep")
f32 = jnp.float32
bf16 = jnp.bfloat16
brief, medium, long = 0, 10**9, 10**11


def swap(payload, leaf_flip, sep_flip, senders=None):
    leaves, seps = lax.axis_size("leaf"), lax.axis_size("sep")
    pairs = [
        (leaf * seps + sep, (leaf ^ leaf_flip) * seps + (sep ^ sep_flip))
        for leaf in range(leaves)
        for sep in range(seps)
        if senders is None or senders(leaf, sep)
    ]
    return lax.ppermute(payload, axes, pairs)


def quarter_swap(payload, moves):
    leaves, seps = lax.axis_size("leaf"), lax.axis_size("sep")
    size = leaves // 4
    pairs = [
        ((start * size + leaf) * seps + sep, (end * size + leaf) * seps + sep)
        for start, end in moves
        for leaf in range(size)
        for sep in range(seps)
    ]
    return lax.ppermute(payload, axes, pairs)


def after(*arrays):
    return lax.optimization_barrier(arrays)


def product(left, right, left_dim, right_dim, precision=None):
    return lax.dot_general(
        left,
        right,
        (((left_dim,), (right_dim,)), ((), ())),
        precision=precision,
        preferred_element_type=f32,
    )


def dot(left, right, left_dim=1, right_dim=0):
    return product(left, right, left_dim, right_dim, lax.Precision.HIGHEST)


def pieces_of(array):
    high = array.astype(bf16)
    return high, (array - high.astype(f32)).astype(bf16)


def dot3(left, right, left_dim=1, right_dim=0):
    left_high, left_low = pieces_of(left)
    right_high, right_low = pieces_of(right)
    small = product(left_high, right_low, left_dim, right_dim)
    small = small + product(left_low, right_high, left_dim, right_dim)
    return product(left_high, right_high, left_dim, right_dim) + small


def hot_dot(left, right, right_dim):
    high, low = pieces_of(left)
    out = product(jnp.concatenate([high, low], 0), right, 1, right_dim)
    return out[: left.shape[0]] + out[left.shape[0] :]


def stage(body, shapes, *operands, scratch=(), space=pltpu.VMEM, cost=brief):
    return pl.pallas_call(
        body,
        out_shape=[
            jax.ShapeDtypeStruct(shape, f32) if isinstance(shape, tuple) else shape
            for shape in shapes
        ],
        in_specs=[pl.BlockSpec(memory_space=space)] * len(operands),
        out_specs=[pl.BlockSpec(memory_space=pltpu.VMEM)] * len(shapes),
        scratch_shapes=[
            pltpu.VMEM(shape, f32) if isinstance(shape, tuple) else shape for shape in scratch
        ],
        compiler_params=pltpu.CompilerParams(vmem_limit_bytes=16 * 2**20),
        cost_estimate=pl.CostEstimate(flops=cost, bytes_accessed=0, transcendentals=0),
    )(*operands)


def place():
    leaf, sep = lax.axis_index("leaf"), lax.axis_index("sep")
    return leaf, sep, lax.rem(leaf, 2), sep // 2, lax.rem(sep, 2)


def at(index, size):
    return pl.ds(pl.multiple_of(index * size, size), size)


def by_bit(bit, zero, one):
    return jnp.where(bit == 0, zero, one)


def per_device(
    leaf_source,
    leaf_inverse,
    leaf_update,
    row_lists,
    row_counts,
    separator_source,
    separator_inverse,
    separator_coupling,
):
    depth = row_counts.shape[1]
    source = leaf_source[0]
    inverse = leaf_inverse[0]
    update = jnp.swapaxes(leaf_update, 1, 2)[0]
    rows_source = separator_source[0]
    rows, columns = source.shape
    size = inverse.shape[1]
    updates = update.shape[1]
    capacity = updates // depth
    order = separator_inverse.shape[1]
    middle = order // 2
    packed_rows = middle // 2 + 8
    carried = middle + packed_rows
    list_rows = -(-depth // 8) * 8
    quarter = rows_source.shape[0]
    half = columns // 2
    block = columns // 8
    width = updates + 2 * quarter
    leaves = lax.axis_size("leaf")

    near = swap(source, 0, 1)
    update_near = swap(update, 0, 1)
    inverse_near = swap(inverse, 0, 1)
    rows_near = swap(rows_source, 0, 1)

    def own_columns_of(source_ref, out_ref):
        near_bit = place()[4]
        out_ref[...] = by_bit(near_bit, source_ref[:, :half], source_ref[:, half:])

    def chip_source(own_ref, near_ref, out_ref):
        near_bit = place()[4]
        out_ref[at(near_bit, rows)] = own_ref[...]
        out_ref[at(1 - near_bit, rows)] = by_bit(near_bit, near_ref[:, :half], near_ref[:, half:])

    (own_source,) = stage(own_columns_of, [(rows, half)], source)
    near, own_source = after(near, own_source)
    (chip,) = stage(chip_source, [(2 * rows, half)], own_source, near)
    far = swap(chip, 0, 2)

    def operators(coupling_ref, inverse, lists, out_ref, packed, square):
        near_bit = place()[4]
        out_ref[:middle] = dot3(coupling_ref[at(near_bit, middle)], inverse[...])
        square[...] = dot3(inverse[...], inverse[...], 0, 0)
        row = lax.broadcasted_iota(jnp.int32, (middle, middle), 0)
        lane = lax.broadcasted_iota(jnp.int32, (middle, middle), 1)
        last = square[middle:, middle:]
        packed[:middle, :middle] = jnp.where(row >= lane, square[:middle, :middle], last)
        packed[:middle, middle:] = square[middle:, :middle]
        packed[middle:] = jnp.zeros((2 * packed_rows - middle, order), f32)
        packed[middle : middle + 1, :middle] = jnp.sum(jnp.where(row == lane, last, 0.0), 0, keepdims=True)
        out_ref[middle:carried] = packed[at(near_bit, packed_rows)]
        out_ref[carried:] = jnp.full((list_rows, order), -1.0, f32)
        slot = lax.broadcasted_iota(jnp.int32, (1, capacity), 1)
        for level in range(depth):
            names = lists[:, level * capacity : (level + 1) * capacity]
            live = slot < lists[:, updates + level : updates + level + 1]
            out_ref[carried + level : carried + level + 1, :capacity] = jnp.where(live, names, -1).astype(f32)

    chip, coupling, own_inverse = after(chip, separator_coupling[0], separator_inverse[0])
    names_and_counts = jnp.concatenate([row_lists, row_counts], 1)
    (payload,) = stage(
        operators,
        [(carried + list_rows, order)],
        coupling,
        own_inverse,
        names_and_counts,
        scratch=[(2 * packed_rows, order), (order, order)],
        cost=3 * medium,
    )

    def own_part(inverse_ref, inverse_near_ref, update_ref, update_near_ref, chip_ref, y_ref, block_ref, far_ref, mine_ref, update_out_ref, all_ref):
        _, _, _, far_bit, near_bit = place()
        own, other = at(near_bit, rows), at(1 - near_bit, rows)
        all_ref[own] = inverse_ref[...]
        all_ref[other] = inverse_near_ref[...]
        update_out_ref[own] = update_ref[...]
        update_out_ref[other] = update_near_ref[...]
        whole = all_ref[...]
        first, second = whole[:, : 2 * rows], whole[:, 2 * rows :]
        far_ref[...] = by_bit(far_bit, second, first)
        y_ref[...] = dot3(by_bit(far_bit, first, second), chip_ref[...])
        chip_block = by_bit(far_bit, first, second)
        block_ref[...] = chip_block
        mine_ref[...] = by_bit(near_bit, chip_block[:, :rows], chip_block[:, rows:])

    received = swap(payload, 1, 0)
    inverse_near, payload = after(inverse_near, payload)
    own_y, inverse_chip, inverse_far, inverse_mine, update_all = stage(
        own_part,
        [(2 * rows, half), (2 * rows, 2 * rows), (2 * rows, 2 * rows), (2 * rows, rows), (2 * rows, updates)],
        inverse,
        inverse_near,
        update,
        update_near,
        chip,
        scratch=[(2 * rows, size)],
    )

    def turned_update(far_ref, mine_ref, update_ref, y_ref, turned_far_ref, turned_mine_ref, terms_ref):
        update = update_ref[...]
        turned_far_ref[...] = dot3(far_ref[...], update, 0, 0)
        turned_mine_ref[...] = dot3(mine_ref[...], update, 0, 0)
        terms_ref[...] = dot3(y_ref[...], update, 0, 0)

    turned_far, own_sum, own_terms = stage(
        turned_update,
        [(2 * rows, updates), (rows, updates), (half, updates)],
        inverse_far,
        inverse_mine,
        update_all,
        own_y,
    )

    def turned_rows(rows_ref, rows_near_ref, out_ref):
        near_bit = place()[4]
        turned, turned_near = jnp.transpose(rows_ref[...]), jnp.transpose(rows_near_ref[...])
        turned = by_bit(near_bit, turned[:half], turned[half:])
        turned_near = by_bit(near_bit, turned_near[:half], turned_near[half:])
        out_ref[...] = by_bit(
            near_bit,
            jnp.concatenate([turned, turned_near], 1),
            jnp.concatenate([turned_near, turned], 1),
        )

    rows_near, own_terms = after(rows_near, own_terms)
    (turned,) = stage(turned_rows, [(half, 2 * quarter)], rows_source, rows_near)
    far, turned = after(far, turned)

    def leaf_part(own_ref, turned_far_ref, far_ref, turned_ref, *refs):
        _, _, odd, far_bit, _ = place()
        out_refs, terms = refs[:-1], refs[-1]
        terms[...] = own_ref[...] + dot3(far_ref[...], turned_far_ref[...], 0, 0)
        for flip, out_ref in enumerate(out_refs):
            part = at((2 * odd + far_bit) ^ flip, block)
            out_ref[:, :updates] = terms[part]
            out_ref[:, updates:] = turned_ref[part]

    mine, to_far, to_odd, to_both = stage(
        leaf_part,
        [(block, width)] * 4,
        own_terms,
        turned_far,
        far,
        turned,
        scratch=[(half, updates)],
    )
    by_both = swap(to_both, 1, 2)
    by_far = swap(to_far, 0, 2)
    by_odd = swap(to_odd, 1, 0)

    def forward(level):
        def body(carry_ref, received_ref, half_ref, next_ref):
            upper = lax.rem(place()[0] // 2 ** (level - 1), 2) == 1
            carry, received = carry_ref[:carried], received_ref[:carried]
            half_ref[...] = jnp.where(upper, carry, received)
            next_ref[...] = jnp.where(upper, received, carry)

        return body

    def last_forward(carry_ref, received_ref, half_ref, root_ref):
        part = place()[0] // (leaves // 4)
        carry, received = carry_ref[...], received_ref[...]
        half_ref[...] = jnp.where(lax.rem(part, 2) == 1, carry, received)
        root_ref[...] = jnp.where(part == 1, received[middle:], carry[middle:])

    def root_half(root_ref, received_ref, out_ref):
        part = place()[0] // (leaves // 4)
        inner = jnp.logical_or(part == 1, part == 2)
        out_ref[...] = jnp.where(inner, root_ref[...], received_ref[...])

    received, mine = after(received, mine)
    new_half, carry = stage(forward(1), [(carried, order)] * 2, payload, received)
    halves, halves_near = [new_half], [swap(new_half, 0, 1)]
    for level in range(2, depth - 1):
        reached = swap(carry, 2 ** (level - 1), 0)
        new_half, carry = stage(forward(level), [(carried, order)] * 2, carry, reached)
        halves.append(new_half)
        halves_near.append(swap(new_half, 0, 1))
    reached = quarter_swap(carry, ((1, 0), (3, 2), (2, 1)))

    def one_hots(own_ref, other_ref, hot_ref):
        rows_of_node = lax.broadcasted_iota(jnp.int32, (order, capacity), 0)
        for level in range(depth):
            for index, ref in enumerate((own_ref, other_ref)):
                names = ref[carried + level : carried + level + 1, :capacity].astype(jnp.int32)
                hot = jnp.where(rows_of_node == names, 1.0, 0.0).astype(bf16)
                hot_ref[level, :, index * capacity : (index + 1) * capacity] = hot

    carry, payload = after(carry, payload)
    (hots,) = stage(
        one_hots, [jax.ShapeDtypeStruct((depth, order, 2 * capacity), bf16)], payload, received
    )

    def transposed(inverse_far_ref, own_y_ref, far_ref, turned_far_ref, y_ref, out_ref):
        near_bit = place()[4]
        inverse_far = inverse_far_ref[...]
        leaf_y = own_y_ref[...] + dot3(inverse_far, far_ref[...])
        y_ref[...] = leaf_y
        turned_y = dot3(inverse_far, leaf_y, 0, 0)
        out_ref[:, :updates] = turned_far_ref[at(near_bit, rows)]
        out_ref[:, updates : updates + half] = turned_y[:rows]
        out_ref[:, updates + half :] = turned_y[rows:]

    own_y, hots = after(own_y, hots)
    leaf_y, far_sum = stage(
        transposed,
        [(2 * rows, half), (rows, updates + columns)],
        inverse_far,
        own_y,
        far,
        turned_far,
    )
    by_both, by_far, by_odd, leaf_y = after(by_both, by_far, by_odd, leaf_y)

    def gathered_part(mine_ref, far_ref, odd_ref, both_ref, hot_ref, residual_ref, up_ref):
        leaf, _, odd, far_bit, _ = place()

        def joined(one, two):
            first, second = one[:, updates:], two[:, updates:]
            ordered = by_bit(
                far_bit,
                jnp.concatenate([first, second], 1),
                jnp.concatenate([second, first], 1),
            )
            return one[:, :updates] + two[:, :updates], ordered

        total, own_source = joined(mine_ref[...], far_ref[...])
        total_other, other_source = joined(odd_ref[...], both_ref[...])
        odd_source = by_bit(odd, other_source, own_source)
        even_source = by_bit(odd, own_source, other_source)
        for level in range(1, depth + 1):
            part = slice((level - 1) * capacity, level * capacity)
            both = jnp.concatenate([total[:, part], total_other[:, part]], 1)
            gathered = hot_dot(both, hot_ref[level - 1], 1)
            if level == 1:
                residual_ref[...] = odd_source - gathered
            else:
                here = lax.rem(leaf - odd, 2**level) == 2 ** (level - 1)
                slot = jnp.where(here, even_source, 0.0) - gathered
                up_ref[:, (level - 2) * order : (level - 1) * order] = slot

    residual, slots = stage(
        gathered_part,
        [(block, order), (block, (depth - 1) * order)],
        mine,
        by_far,
        by_odd,
        by_both,
        hots,
        cost=3*medium,
    )
    residuals = [residual]

    def operator_of(half_ref, near_ref):
        near_bit = place()[4]
        own, other = half_ref[:middle], near_ref[:middle]
        return jnp.concatenate([by_bit(near_bit, own, other), by_bit(near_bit, other, own)], 0)

    def push(slots_ref, residual_ref, half_ref, near_ref, out_ref):
        taken = dot3(residual_ref[...], operator_of(half_ref, near_ref), 1, 1)
        out_ref[:, :order] = slots_ref[:, :order] - taken
        if out_ref.shape[1] > order:
            out_ref[:, order:] = slots_ref[:, order:]

    def squared(residual, own, other):
        near_bit = place()[4]
        row = lax.broadcasted_iota(jnp.int32, (middle, middle), 0)
        lane = lax.broadcasted_iota(jnp.int32, (middle, middle), 1)
        packed = jnp.concatenate([by_bit(near_bit, own, other), by_bit(near_bit, other, own)], 0)
        both, below = packed[:middle, :middle], packed[:middle, middle:]
        lower, upper = jnp.where(row > lane, both, 0.0), jnp.where(row < lane, both, 0.0)
        first = jnp.where(row >= lane, both, 0.0)
        last = jnp.where(row == lane, packed[middle : middle + 1, :middle], upper)
        one, two = residual[:, :middle], residual[:, middle:]
        return jnp.concatenate(
            [
                dot3(one, first) + dot3(one, lower, 1, 1) + dot3(two, below),
                dot3(one, below, 1, 1) + dot3(two, last) + dot3(two, upper, 1, 1),
            ],
            1,
        )

    def alone(residual_ref, half_ref, near_ref, out_ref, down_ref):
        down_ref[...] = operator_of(half_ref, near_ref)
        out_ref[...] = squared(residual_ref[...], half_ref[middle:], near_ref[middle:])

    def below_root(*refs):
        count = depth - 1
        partial_refs, down_refs = refs[:count], refs[count : 2 * count]
        base_ref, high_ref, low_ref = refs[2 * count :]
        base, taken = partial_refs[-1][...], -down_refs[-1][...]
        for level in range(depth - 1, 0, -1):
            if level < depth - 1:
                down = down_refs[level - 1][...]
                base = partial_refs[level - 1][...] - dot3(base, down)
                taken = -dot3(taken, down)
            part = slice((level - 1) * order, level * order)
            base_ref[:, part] = base
            high_ref[:, part], low_ref[:, part] = pieces_of(taken)

    def level_sum(up_ref, partner_ref, residual_ref, rest_ref):
        total = up_ref[...] + partner_ref[...]
        residual_ref[...] = total[:, :order]
        rest_ref[...] = total[:, order:]

    partials, downs = [], []
    halves_near[0], residual, slots = after(halves_near[0], residual, slots)
    (going_up,) = stage(
        push, [(block, (depth - 1) * order)], slots, residual, halves[0], halves_near[0]
    )
    for level in range(2, depth):
        partner = swap(going_up, 2 ** (level - 1), 0)
        if level == depth - 1:
            reached, going_up = after(reached, going_up)
            new_half, root = stage(
                last_forward, [(carried, order), (packed_rows, order)], carry, reached
            )
            halves.append(new_half)
            from_far = swap(far_sum, 0, 2, lambda leaf, sep: sep // 2 == 1)
            halves_near.append(swap(new_half, 0, 1))
            by_root = swap(root, leaves // 4, 0)
        residual, slots = stage(
            level_sum,
            [(block, order), (block, (depth - level) * order)],
            going_up,
            partner,
            cost=2 * medium,
        )
        residuals.append(residual)
        halves_near[level - 1], residual, slots = after(halves_near[level - 1], residual, slots)
        (going_up,) = stage(
            push,
            [(block, (depth - level) * order)],
            slots,
            residual,
            halves[level - 1],
            halves_near[level - 1],
        )
    partner = swap(going_up, 2 ** (depth - 1), 0)

    for level in range(1, depth):
        residual, going_up = after(residuals[level - 1], going_up)
        partial, down = stage(
            alone,
            [(block, order), (order, order)],
            residual,
            halves[level - 1],
            halves_near[level - 1],
        )
        partials.append(partial)
        downs.append(down)
    by_root, partial = after(by_root, partial)
    (root,) = stage(root_half, [(packed_rows, order)], root, by_root)
    root_near = swap(root, 0, 1)
    partials[-1], root = after(partials[-1], root)
    pieces = jax.ShapeDtypeStruct((order, (depth - 1) * order), bf16)
    base, taken_high, taken_low = stage(
        below_root, [(block, (depth - 1) * order), pieces, pieces], *partials, *downs
    )
    partner, root, base = after(partner, root, base)

    def root_sum(up_ref, partner_ref, out_ref):
        out_ref[...] = up_ref[...] + partner_ref[...]

    (residual,) = stage(root_sum, [(block, order)], going_up, partner, cost=medium)
    root_near, residual = after(root_near, residual)

    def way_down(residual_ref, root_ref, root_near_ref, hot_ref, base_ref, high_ref, low_ref, *out_refs):
        leaf, _, odd, far_bit, _ = place()
        top = squared(residual_ref[...], root_ref[...], root_near_ref[...])
        high, low = pieces_of(top)
        large = product(jnp.concatenate([high, low], 0), high_ref[...], 1, 0)
        small = large[block:] + product(high, low_ref[...], 1, 0)
        under = base_ref[...] + (large[:block] + small)
        solved = [under[:, level * order : (level + 1) * order] for level in range(depth - 1)]
        solved.append(top)
        even_solved = jnp.zeros_like(solved[0])
        for level in range(2, depth + 1):
            here = lax.rem(leaf - odd, 2**level) == 2 ** (level - 1)
            even_solved = jnp.where(here, solved[level - 1], even_solved)
        own_solved = by_bit(odd, even_solved, solved[0])
        other_solved = by_bit(odd, solved[0], even_solved)
        for flip, out_ref in enumerate(out_refs):
            rows_of = other_solved if flip >= 2 else own_solved
            out_ref[:, updates:] = by_bit(
                far_bit ^ (flip % 2), rows_of[:, : 2 * quarter], rows_of[:, 2 * quarter :]
            )
        for level in range(depth):
            picked = hot_dot(solved[level], hot_ref[level], 0)
            for flip, out_ref in enumerate(out_refs):
                side = flip // 2
                out_ref[:, level * capacity : (level + 1) * capacity] = picked[
                    :, side * capacity : (side + 1) * capacity
                ]

    stay, to_far, to_odd, to_both = stage(
        way_down,
        [(block, width)] * 4,
        residual,
        root,
        root_near,
        hots,
        base,
        taken_high,
        taken_low,
    )
    both = swap(to_both, 1, 2)
    beyond = swap(to_far, 0, 2)
    side = swap(to_odd, 1, 0)

    def last_left(own_ref, chip_ref, y_ref, far_ref, left_ref, keep_ref, pass_ref):
        near_bit = place()[4]
        left_ref[:rows, :updates] = -(own_ref[...] + far_ref[:, :updates])
        left_ref[:rows, updates:] = jnp.zeros((rows, 2 * quarter), f32)
        row = lax.broadcasted_iota(jnp.int32, (quarter, width), 0)
        lane = lax.broadcasted_iota(jnp.int32, (quarter, width), 1)
        left_ref[rows:] = jnp.where(lane == updates + near_bit * quarter + row, 1.0, 0.0)
        turned_y = dot3(chip_ref[...], y_ref[...], 0, 0)
        first = turned_y[:rows] + far_ref[:, updates : updates + half]
        second = turned_y[rows:] + far_ref[:, updates + half :]
        keep_ref[...] = by_bit(near_bit, first, second)
        pass_ref[...] = by_bit(near_bit, second, first)

    from_far, stay = after(from_far, stay)
    left, base_keep, base_pass = stage(
        last_left, [(rows + quarter, width), (rows, half), (rows, half)], own_sum, inverse_chip, leaf_y, from_far
    )
    both, beyond, side, left = after(both, beyond, side, left)

    def grouped(*refs):
        _, _, odd, far_bit, _ = place()
        out_ref = refs[-1]
        for flip, ref in enumerate(refs[:-1]):
            out_ref[at((2 * odd + far_bit) ^ flip, block)] = ref[...]

    (group,) = stage(grouped, [(half, width)], stay, beyond, side, both)
    base_near = swap(base_pass, 0, 1)
    group_near = swap(group, 0, 1)

    def own_columns(left_ref, group_ref, out_ref):
        out_ref[...] = dot3(left_ref[...], group_ref[...], 1, 1)

    (ours,) = stage(own_columns, [(rows + quarter, half)], left, group)
    group_near, ours = after(group_near, ours)

    def finish(left_ref, group_ref, ours_ref, base_ref, base_near_ref, leaf_ref, rows_ref):
        near_bit = place()[4]
        ours = ours_ref[...]
        theirs = dot3(left_ref[...], group_ref[...], 1, 1)
        ours_x, theirs_x = base_ref[...] + ours[:rows], base_near_ref[...] + theirs[:rows]
        leaf_ref[:, :half] = by_bit(near_bit, ours_x, theirs_x)
        leaf_ref[:, half:] = by_bit(near_bit, theirs_x, ours_x)
        rows_ref[:, :half] = by_bit(near_bit, ours[rows:], theirs[rows:])
        rows_ref[:, half:] = by_bit(near_bit, theirs[rows:], ours[rows:])

    leaf_x, separator_rows = stage(
        finish,
        [(rows, columns), (quarter, columns)],
        left,
        group_near,
        ours,
        base_keep,
        base_near,
    )
    return (leaf_x[None], separator_rows[None])


def solution(mesh):
    placed = (
        P("leaf", "sep", None),
        P("leaf", "sep", None),
        P("leaf", None, "sep"),
        P("leaf", None),
        P("leaf", None),
        P("leaf", "sep", None),
        P("leaf", None, None),
        P("leaf", None, None),
    )
    return jax.shard_map(
        per_device,
        mesh=mesh,
        in_specs=placed,
        out_specs=(P("leaf", "sep", None), P("leaf", "sep", None)),
        check_vma=False,
    )
```

```python
import jax
import jax.numpy as jnp
from jax import lax
from jax.experimental import pallas as pl
from jax.experimental.pallas import tpu as pltpu
from jax.sharding import PartitionSpec as P

axes = ("leaf", "sep")
f32 = jnp.float32
bf16 = jnp.bfloat16
brief, medium, long = 0, 10**9, 10**11


def swap(payload, leaf_flip, sep_flip, senders=None):
    leaves, seps = lax.axis_size("leaf"), lax.axis_size("sep")
    pairs = [
        (leaf * seps + sep, (leaf ^ leaf_flip) * seps + (sep ^ sep_flip))
        for leaf in range(leaves)
        for sep in range(seps)
        if senders is None or senders(leaf, sep)
    ]
    return lax.ppermute(payload, axes, pairs)


def quarter_swap(payload, moves):
    leaves, seps = lax.axis_size("leaf"), lax.axis_size("sep")
    size = leaves // 4
    pairs = [
        ((start * size + leaf) * seps + sep, (end * size + leaf) * seps + sep)
        for start, end in moves
        for leaf in range(size)
        for sep in range(seps)
    ]
    return lax.ppermute(payload, axes, pairs)


def after(*arrays):
    return lax.optimization_barrier(arrays)


def product(left, right, left_dim, right_dim, precision=None):
    return lax.dot_general(
        left,
        right,
        (((left_dim,), (right_dim,)), ((), ())),
        precision=precision,
        preferred_element_type=f32,
    )


def dot(left, right, left_dim=1, right_dim=0):
    return product(left, right, left_dim, right_dim, lax.Precision.HIGHEST)


def pieces_of(array):
    high = array.astype(bf16)
    return high, (array - high.astype(f32)).astype(bf16)


def dot3(left, right, left_dim=1, right_dim=0):
    left_high, left_low = pieces_of(left)
    right_high, right_low = pieces_of(right)
    small = product(left_high, right_low, left_dim, right_dim)
    small = small + product(left_low, right_high, left_dim, right_dim)
    return product(left_high, right_high, left_dim, right_dim) + small


def hot_dot(left, right, right_dim):
    high, low = pieces_of(left)
    out = product(jnp.concatenate([high, low], 0), right, 1, right_dim)
    return out[: left.shape[0]] + out[left.shape[0] :]


def stage(body, shapes, *operands, scratch=(), space=pltpu.VMEM, cost=brief):
    return pl.pallas_call(
        body,
        out_shape=[
            jax.ShapeDtypeStruct(shape, f32) if isinstance(shape, tuple) else shape
            for shape in shapes
        ],
        in_specs=[pl.BlockSpec(memory_space=space)] * len(operands),
        out_specs=[pl.BlockSpec(memory_space=pltpu.VMEM)] * len(shapes),
        scratch_shapes=[
            pltpu.VMEM(shape, f32) if isinstance(shape, tuple) else shape for shape in scratch
        ],
        compiler_params=pltpu.CompilerParams(vmem_limit_bytes=16 * 2**20),
        cost_estimate=pl.CostEstimate(flops=cost, bytes_accessed=0, transcendentals=0),
    )(*operands)


def place():
    leaf, sep = lax.axis_index("leaf"), lax.axis_index("sep")
    return leaf, sep, lax.rem(leaf, 2), sep // 2, lax.rem(sep, 2)


def at(index, size):
    return pl.ds(pl.multiple_of(index * size, size), size)


def by_bit(bit, zero, one):
    return jnp.where(bit == 0, zero, one)


def per_device(
    leaf_source,
    leaf_inverse,
    leaf_update,
    row_lists,
    row_counts,
    separator_source,
    separator_inverse,
    separator_coupling,
):
    depth = row_counts.shape[1]
    source = leaf_source[0]
    inverse = leaf_inverse[0]
    update = jnp.swapaxes(leaf_update, 1, 2)[0]
    rows_source = separator_source[0]
    rows, columns = source.shape
    size = inverse.shape[1]
    updates = update.shape[1]
    capacity = updates // depth
    order = separator_inverse.shape[1]
    middle = order // 2
    packed_rows = middle // 2 + 8
    carried = middle + packed_rows
    list_rows = -(-depth // 8) * 8
    quarter = rows_source.shape[0]
    half = columns // 2
    block = columns // 8
    width = updates + 2 * quarter
    leaves = lax.axis_size("leaf")

    near = swap(source, 0, 1)
    update_near = swap(update, 0, 1)
    inverse_near = swap(inverse, 0, 1)
    rows_near = swap(rows_source, 0, 1)

    def own_columns_of(source_ref, out_ref):
        near_bit = place()[4]
        out_ref[...] = by_bit(near_bit, source_ref[:, :half], source_ref[:, half:])

    def chip_source(own_ref, near_ref, out_ref):
        near_bit = place()[4]
        out_ref[at(near_bit, rows)] = own_ref[...]
        out_ref[at(1 - near_bit, rows)] = by_bit(near_bit, near_ref[:, :half], near_ref[:, half:])

    (own_source,) = stage(own_columns_of, [(rows, half)], source)
    near, own_source = after(near, own_source)
    (chip,) = stage(chip_source, [(2 * rows, half)], own_source, near)
    far = swap(chip, 0, 2)

    def operators(coupling_ref, inverse, lists, out_ref, packed, square):
        near_bit = place()[4]
        out_ref[:middle] = dot3(coupling_ref[at(near_bit, middle)], inverse[...])
        square[...] = dot3(inverse[...], inverse[...], 0, 0)
        row = lax.broadcasted_iota(jnp.int32, (middle, middle), 0)
        lane = lax.broadcasted_iota(jnp.int32, (middle, middle), 1)
        last = square[middle:, middle:]
        packed[:middle, :middle] = jnp.where(row >= lane, square[:middle, :middle], last)
        packed[:middle, middle:] = square[middle:, :middle]
        packed[middle:] = jnp.zeros((2 * packed_rows - middle, order), f32)
        packed[middle : middle + 1, :middle] = jnp.sum(jnp.where(row == lane, last, 0.0), 0, keepdims=True)
        out_ref[middle:carried] = packed[at(near_bit, packed_rows)]
        out_ref[carried:] = jnp.full((list_rows, order), -1.0, f32)
        slot = lax.broadcasted_iota(jnp.int32, (1, capacity), 1)
        for level in range(depth):
            names = lists[:, level * capacity : (level + 1) * capacity]
            live = slot < lists[:, updates + level : updates + level + 1]
            out_ref[carried + level : carried + level + 1, :capacity] = jnp.where(live, names, -1).astype(f32)

    chip, coupling, own_inverse = after(chip, separator_coupling[0], separator_inverse[0])
    names_and_counts = jnp.concatenate([row_lists, row_counts], 1)
    (payload,) = stage(
        operators,
        [(carried + list_rows, order)],
        coupling,
        own_inverse,
        names_and_counts,
        scratch=[(2 * packed_rows, order), (order, order)],
        cost=3 * medium,
    )

    def own_part(inverse_ref, inverse_near_ref, update_ref, update_near_ref, chip_ref, y_ref, block_ref, far_ref, mine_ref, update_out_ref, all_ref):
        _, _, _, far_bit, near_bit = place()
        own, other = at(near_bit, rows), at(1 - near_bit, rows)
        all_ref[own] = inverse_ref[...]
        all_ref[other] = inverse_near_ref[...]
        update_out_ref[own] = update_ref[...]
        update_out_ref[other] = update_near_ref[...]
        whole = all_ref[...]
        first, second = whole[:, : 2 * rows], whole[:, 2 * rows :]
        far_ref[...] = by_bit(far_bit, second, first)
        y_ref[...] = dot3(by_bit(far_bit, first, second), chip_ref[...])
        chip_block = by_bit(far_bit, first, second)
        block_ref[...] = chip_block
        mine_ref[...] = by_bit(near_bit, chip_block[:, :rows], chip_block[:, rows:])

    received = swap(payload, 1, 0)
    inverse_near, payload = after(inverse_near, payload)
    own_y, inverse_chip, inverse_far, inverse_mine, update_all = stage(
        own_part,
        [(2 * rows, half), (2 * rows, 2 * rows), (2 * rows, 2 * rows), (2 * rows, rows), (2 * rows, updates)],
        inverse,
        inverse_near,
        update,
        update_near,
        chip,
        scratch=[(2 * rows, size)],
    )

    def turned_update(far_ref, mine_ref, update_ref, y_ref, turned_far_ref, turned_mine_ref, terms_ref):
        update = update_ref[...]
        turned_far_ref[...] = dot3(far_ref[...], update, 0, 0)
        turned_mine_ref[...] = dot3(mine_ref[...], update, 0, 0)
        terms_ref[...] = dot3(y_ref[...], update, 0, 0)

    turned_far, own_sum, own_terms = stage(
        turned_update,
        [(2 * rows, updates), (rows, updates), (half, updates)],
        inverse_far,
        inverse_mine,
        update_all,
        own_y,
    )

    def turned_rows(rows_ref, rows_near_ref, out_ref):
        near_bit = place()[4]
        turned, turned_near = jnp.transpose(rows_ref[...]), jnp.transpose(rows_near_ref[...])
        turned = by_bit(near_bit, turned[:half], turned[half:])
        turned_near = by_bit(near_bit, turned_near[:half], turned_near[half:])
        out_ref[...] = by_bit(
            near_bit,
            jnp.concatenate([turned, turned_near], 1),
            jnp.concatenate([turned_near, turned], 1),
        )

    rows_near, own_terms = after(rows_near, own_terms)
    (turned,) = stage(turned_rows, [(half, 2 * quarter)], rows_source, rows_near)
    far, turned = after(far, turned)

    def leaf_part(own_ref, turned_far_ref, far_ref, turned_ref, *refs):
        _, _, odd, far_bit, _ = place()
        out_refs, terms = refs[:-1], refs[-1]
        terms[...] = own_ref[...] + dot3(far_ref[...], turned_far_ref[...], 0, 0)
        for flip, out_ref in enumerate(out_refs):
            part = at((2 * odd + far_bit) ^ flip, block)
            out_ref[:, :updates] = terms[part]
            out_ref[:, updates:] = turned_ref[part]

    mine, to_far, to_odd, to_both = stage(
        leaf_part,
        [(block, width)] * 4,
        own_terms,
        turned_far,
        far,
        turned,
        scratch=[(half, updates)],
    )
    by_both = swap(to_both, 1, 2)
    by_far = swap(to_far, 0, 2)
    by_odd = swap(to_odd, 1, 0)

    def forward(level):
        def body(carry_ref, received_ref, half_ref, next_ref):
            upper = lax.rem(place()[0] // 2 ** (level - 1), 2) == 1
            carry, received = carry_ref[:carried], received_ref[:carried]
            half_ref[...] = jnp.where(upper, carry, received)
            next_ref[...] = jnp.where(upper, received, carry)

        return body

    def last_forward(carry_ref, received_ref, half_ref, root_ref):
        part = place()[0] // (leaves // 4)
        carry, received = carry_ref[...], received_ref[...]
        half_ref[...] = jnp.where(lax.rem(part, 2) == 1, carry, received)
        root_ref[...] = jnp.where(part == 1, received[middle:], carry[middle:])

    def root_half(root_ref, received_ref, out_ref):
        part = place()[0] // (leaves // 4)
        inner = jnp.logical_or(part == 1, part == 2)
        out_ref[...] = jnp.where(inner, root_ref[...], received_ref[...])

    received, mine = after(received, mine)
    new_half, carry = stage(forward(1), [(carried, order)] * 2, payload, received)
    halves, halves_near = [new_half], [swap(new_half, 0, 1)]
    for level in range(2, depth - 1):
        reached = swap(carry, 2 ** (level - 1), 0)
        new_half, carry = stage(forward(level), [(carried, order)] * 2, carry, reached)
        halves.append(new_half)
        halves_near.append(swap(new_half, 0, 1))
    reached = quarter_swap(carry, ((1, 0), (3, 2), (2, 1)))

    def one_hots(own_ref, other_ref, hot_ref):
        rows_of_node = lax.broadcasted_iota(jnp.int32, (order, capacity), 0)
        for level in range(depth):
            for index, ref in enumerate((own_ref, other_ref)):
                names = ref[carried + level : carried + level + 1, :capacity].astype(jnp.int32)
                hot = jnp.where(rows_of_node == names, 1.0, 0.0).astype(bf16)
                hot_ref[level, :, index * capacity : (index + 1) * capacity] = hot

    carry, payload = after(carry, payload)
    (hots,) = stage(
        one_hots, [jax.ShapeDtypeStruct((depth, order, 2 * capacity), bf16)], payload, received
    )

    def transposed(inverse_far_ref, own_y_ref, far_ref, turned_far_ref, y_ref, out_ref):
        near_bit = place()[4]
        inverse_far = inverse_far_ref[...]
        leaf_y = own_y_ref[...] + dot3(inverse_far, far_ref[...])
        y_ref[...] = leaf_y
        turned_y = dot3(inverse_far, leaf_y, 0, 0)
        out_ref[:, :updates] = turned_far_ref[at(near_bit, rows)]
        out_ref[:, updates : updates + half] = turned_y[:rows]
        out_ref[:, updates + half :] = turned_y[rows:]

    own_y, hots = after(own_y, hots)
    leaf_y, far_sum = stage(
        transposed,
        [(2 * rows, half), (rows, updates + columns)],
        inverse_far,
        own_y,
        far,
        turned_far,
    )
    by_both, by_far, by_odd, leaf_y = after(by_both, by_far, by_odd, leaf_y)

    def gathered_part(mine_ref, far_ref, odd_ref, both_ref, hot_ref, residual_ref, up_ref):
        leaf, _, odd, far_bit, _ = place()

        def joined(one, two):
            first, second = one[:, updates:], two[:, updates:]
            ordered = by_bit(
                far_bit,
                jnp.concatenate([first, second], 1),
                jnp.concatenate([second, first], 1),
            )
            return one[:, :updates] + two[:, :updates], ordered

        total, own_source = joined(mine_ref[...], far_ref[...])
        total_other, other_source = joined(odd_ref[...], both_ref[...])
        odd_source = by_bit(odd, other_source, own_source)
        even_source = by_bit(odd, own_source, other_source)
        for level in range(1, depth + 1):
            part = slice((level - 1) * capacity, level * capacity)
            both = jnp.concatenate([total[:, part], total_other[:, part]], 1)
            gathered = hot_dot(both, hot_ref[level - 1], 1)
            if level == 1:
                residual_ref[...] = odd_source - gathered
            else:
                here = lax.rem(leaf - odd, 2**level) == 2 ** (level - 1)
                slot = jnp.where(here, even_source, 0.0) - gathered
                up_ref[:, (level - 2) * order : (level - 1) * order] = slot

    residual, slots = stage(
        gathered_part,
        [(block, order), (block, (depth - 1) * order)],
        mine,
        by_far,
        by_odd,
        by_both,
        hots,
        cost=3*medium,
    )
    residuals = [residual]

    def operator_of(half_ref, near_ref):
        near_bit = place()[4]
        own, other = half_ref[:middle], near_ref[:middle]
        return jnp.concatenate([by_bit(near_bit, own, other), by_bit(near_bit, other, own)], 0)

    def push(slots_ref, residual_ref, half_ref, near_ref, out_ref):
        taken = dot3(residual_ref[...], operator_of(half_ref, near_ref), 1, 1)
        out_ref[:, :order] = slots_ref[:, :order] - taken
        if out_ref.shape[1] > order:
            out_ref[:, order:] = slots_ref[:, order:]

    def squared(residual, own, other):
        near_bit = place()[4]
        row = lax.broadcasted_iota(jnp.int32, (middle, middle), 0)
        lane = lax.broadcasted_iota(jnp.int32, (middle, middle), 1)
        packed = jnp.concatenate([by_bit(near_bit, own, other), by_bit(near_bit, other, own)], 0)
        both, below = packed[:middle, :middle], packed[:middle, middle:]
        lower, upper = jnp.where(row > lane, both, 0.0), jnp.where(row < lane, both, 0.0)
        first = jnp.where(row >= lane, both, 0.0)
        last = jnp.where(row == lane, packed[middle : middle + 1, :middle], upper)
        one, two = residual[:, :middle], residual[:, middle:]
        return jnp.concatenate(
            [
                dot3(one, first) + dot3(one, lower, 1, 1) + dot3(two, below),
                dot3(one, below, 1, 1) + dot3(two, last) + dot3(two, upper, 1, 1),
            ],
            1,
        )

    def alone(residual_ref, half_ref, near_ref, out_ref, down_ref):
        down_ref[...] = operator_of(half_ref, near_ref)
        out_ref[...] = squared(residual_ref[...], half_ref[middle:], near_ref[middle:])

    def below_root(*refs):
        count = depth - 1
        partial_refs, down_refs = refs[:count], refs[count : 2 * count]
        base_ref, high_ref, low_ref = refs[2 * count :]
        base, taken = partial_refs[-1][...], -down_refs[-1][...]
        for level in range(depth - 1, 0, -1):
            if level < depth - 1:
                down = down_refs[level - 1][...]
                base = partial_refs[level - 1][...] - dot3(base, down)
                taken = -dot3(taken, down)
            part = slice((level - 1) * order, level * order)
            base_ref[:, part] = base
            high_ref[:, part], low_ref[:, part] = pieces_of(taken)

    def level_sum(up_ref, partner_ref, residual_ref, rest_ref):
        total = up_ref[...] + partner_ref[...]
        residual_ref[...] = total[:, :order]
        rest_ref[...] = total[:, order:]

    partials, downs = [], []
    halves_near[0], residual, slots = after(halves_near[0], residual, slots)
    (going_up,) = stage(
        push, [(block, (depth - 1) * order)], slots, residual, halves[0], halves_near[0]
    )
    for level in range(2, depth):
        partner = swap(going_up, 2 ** (level - 1), 0)
        if level == depth - 1:
            reached, going_up = after(reached, going_up)
            new_half, root = stage(
                last_forward, [(carried, order), (packed_rows, order)], carry, reached
            )
            halves.append(new_half)
            from_far = swap(far_sum, 0, 2)
            halves_near.append(swap(new_half, 0, 1))
            by_root = swap(root, leaves // 4, 0)
        residual, slots = stage(
            level_sum,
            [(block, order), (block, (depth - level) * order)],
            going_up,
            partner,
            cost=2 * medium,
        )
        residuals.append(residual)
        halves_near[level - 1], residual, slots = after(halves_near[level - 1], residual, slots)
        (going_up,) = stage(
            push,
            [(block, (depth - level) * order)],
            slots,
            residual,
            halves[level - 1],
            halves_near[level - 1],
        )
    partner = swap(going_up, 2 ** (depth - 1), 0)

    for level in range(1, depth):
        residual, going_up = after(residuals[level - 1], going_up)
        partial, down = stage(
            alone,
            [(block, order), (order, order)],
            residual,
            halves[level - 1],
            halves_near[level - 1],
        )
        partials.append(partial)
        downs.append(down)
    by_root, partial = after(by_root, partial)
    (root,) = stage(root_half, [(packed_rows, order)], root, by_root)
    root_near = swap(root, 0, 1)
    partials[-1], root = after(partials[-1], root)
    pieces = jax.ShapeDtypeStruct((order, (depth - 1) * order), bf16)
    base, taken_high, taken_low = stage(
        below_root, [(block, (depth - 1) * order), pieces, pieces], *partials, *downs
    )
    partner, root, base = after(partner, root, base)

    def root_sum(up_ref, partner_ref, out_ref):
        out_ref[...] = up_ref[...] + partner_ref[...]

    (residual,) = stage(root_sum, [(block, order)], going_up, partner, cost=medium)
    root_near, residual = after(root_near, residual)

    def way_down(residual_ref, root_ref, root_near_ref, hot_ref, base_ref, high_ref, low_ref, *out_refs):
        leaf, _, odd, far_bit, _ = place()
        top = squared(residual_ref[...], root_ref[...], root_near_ref[...])
        high, low = pieces_of(top)
        large = product(jnp.concatenate([high, low], 0), high_ref[...], 1, 0)
        small = large[block:] + product(high, low_ref[...], 1, 0)
        under = base_ref[...] + (large[:block] + small)
        solved = [under[:, level * order : (level + 1) * order] for level in range(depth - 1)]
        solved.append(top)
        even_solved = jnp.zeros_like(solved[0])
        for level in range(2, depth + 1):
            here = lax.rem(leaf - odd, 2**level) == 2 ** (level - 1)
            even_solved = jnp.where(here, solved[level - 1], even_solved)
        own_solved = by_bit(odd, even_solved, solved[0])
        other_solved = by_bit(odd, solved[0], even_solved)
        for flip, out_ref in enumerate(out_refs):
            rows_of = other_solved if flip >= 2 else own_solved
            out_ref[:, updates:] = by_bit(
                far_bit ^ (flip % 2), rows_of[:, : 2 * quarter], rows_of[:, 2 * quarter :]
            )
        for level in range(depth):
            picked = hot_dot(solved[level], hot_ref[level], 0)
            for flip, out_ref in enumerate(out_refs):
                side = flip // 2
                out_ref[:, level * capacity : (level + 1) * capacity] = picked[
                    :, side * capacity : (side + 1) * capacity
                ]

    stay, to_far, to_odd, to_both = stage(
        way_down,
        [(block, width)] * 4,
        residual,
        root,
        root_near,
        hots,
        base,
        taken_high,
        taken_low,
    )
    both = swap(to_both, 1, 2)
    beyond = swap(to_far, 0, 2)
    side = swap(to_odd, 1, 0)

    def last_left(own_ref, chip_ref, y_ref, far_ref, left_ref, keep_ref, pass_ref):
        near_bit = place()[4]
        left_ref[:rows, :updates] = -(own_ref[...] + far_ref[:, :updates])
        left_ref[:rows, updates:] = jnp.zeros((rows, 2 * quarter), f32)
        row = lax.broadcasted_iota(jnp.int32, (quarter, width), 0)
        lane = lax.broadcasted_iota(jnp.int32, (quarter, width), 1)
        left_ref[rows:] = jnp.where(lane == updates + near_bit * quarter + row, 1.0, 0.0)
        turned_y = dot3(chip_ref[...], y_ref[...], 0, 0)
        first = turned_y[:rows] + far_ref[:, updates : updates + half]
        second = turned_y[rows:] + far_ref[:, updates + half :]
        keep_ref[...] = by_bit(near_bit, first, second)
        pass_ref[...] = by_bit(near_bit, second, first)

    from_far, stay = after(from_far, stay)
    left, base_keep, base_pass = stage(
        last_left, [(rows + quarter, width), (rows, half), (rows, half)], own_sum, inverse_chip, leaf_y, from_far
    )
    both, beyond, side, left = after(both, beyond, side, left)

    def grouped(*refs):
        _, _, odd, far_bit, _ = place()
        out_ref = refs[-1]
        for flip, ref in enumerate(refs[:-1]):
            out_ref[at((2 * odd + far_bit) ^ flip, block)] = ref[...]

    (group,) = stage(grouped, [(half, width)], stay, beyond, side, both)
    base_near = swap(base_pass, 0, 1)
    group_near = swap(group, 0, 1)

    def own_columns(left_ref, group_ref, out_ref):
        out_ref[...] = dot3(left_ref[...], group_ref[...], 1, 1)

    (ours,) = stage(own_columns, [(rows + quarter, half)], left, group)
    group_near, ours = after(group_near, ours)

    def finish(left_ref, group_ref, ours_ref, base_ref, base_near_ref, leaf_ref, rows_ref):
        near_bit = place()[4]
        ours = ours_ref[...]
        theirs = dot3(left_ref[...], group_ref[...], 1, 1)
        ours_x, theirs_x = base_ref[...] + ours[:rows], base_near_ref[...] + theirs[:rows]
        leaf_ref[:, :half] = by_bit(near_bit, ours_x, theirs_x)
        leaf_ref[:, half:] = by_bit(near_bit, theirs_x, ours_x)
        rows_ref[:, :half] = by_bit(near_bit, ours[rows:], theirs[rows:])
        rows_ref[:, half:] = by_bit(near_bit, theirs[rows:], ours[rows:])

    leaf_x, separator_rows = stage(
        finish,
        [(rows, columns), (quarter, columns)],
        left,
        group_near,
        ours,
        base_keep,
        base_near,
    )
    return (leaf_x[None], separator_rows[None])


def solution(mesh):
    placed = (
        P("leaf", "sep", None),
        P("leaf", "sep", None),
        P("leaf", None, "sep"),
        P("leaf", None),
        P("leaf", None),
        P("leaf", "sep", None),
        P("leaf", None, None),
        P("leaf", None, None),
    )
    return jax.shard_map(
        per_device,
        mesh=mesh,
        in_specs=placed,
        out_specs=(P("leaf", "sep", None), P("leaf", "sep", None)),
        check_vma=False,
    )
```

```python
import jax
import jax.numpy as jnp
from jax import lax
from jax.experimental import pallas as pl
from jax.experimental.pallas import tpu as pltpu
from jax.sharding import PartitionSpec as P

axes = ("leaf", "sep")
f32 = jnp.float32
bf16 = jnp.bfloat16
brief, medium, long = 0, 10**9, 10**11


def swap(payload, leaf_flip, sep_flip, senders=None):
    leaves, seps = lax.axis_size("leaf"), lax.axis_size("sep")
    pairs = [
        (leaf * seps + sep, (leaf ^ leaf_flip) * seps + (sep ^ sep_flip))
        for leaf in range(leaves)
        for sep in range(seps)
        if senders is None or senders(leaf, sep)
    ]
    return lax.ppermute(payload, axes, pairs)


def quarter_swap(payload, moves):
    leaves, seps = lax.axis_size("leaf"), lax.axis_size("sep")
    size = leaves // 4
    pairs = [
        ((start * size + leaf) * seps + sep, (end * size + leaf) * seps + sep)
        for start, end in moves
        for leaf in range(size)
        for sep in range(seps)
    ]
    return lax.ppermute(payload, axes, pairs)


def after(*arrays):
    return lax.optimization_barrier(arrays)


def product(left, right, left_dim, right_dim, precision=None):
    return lax.dot_general(
        left,
        right,
        (((left_dim,), (right_dim,)), ((), ())),
        precision=precision,
        preferred_element_type=f32,
    )


def dot(left, right, left_dim=1, right_dim=0):
    return product(left, right, left_dim, right_dim, lax.Precision.HIGHEST)


def pieces_of(array):
    high = array.astype(bf16)
    return high, (array - high.astype(f32)).astype(bf16)


def dot3(left, right, left_dim=1, right_dim=0):
    left_high, left_low = pieces_of(left)
    right_high, right_low = pieces_of(right)
    small = product(left_high, right_low, left_dim, right_dim)
    small = small + product(left_low, right_high, left_dim, right_dim)
    return product(left_high, right_high, left_dim, right_dim) + small


def hot_dot(left, right, right_dim):
    high, low = pieces_of(left)
    out = product(jnp.concatenate([high, low], 0), right, 1, right_dim)
    return out[: left.shape[0]] + out[left.shape[0] :]


def stage(body, shapes, *operands, scratch=(), space=pltpu.VMEM, cost=brief):
    return pl.pallas_call(
        body,
        out_shape=[
            jax.ShapeDtypeStruct(shape, f32) if isinstance(shape, tuple) else shape
            for shape in shapes
        ],
        in_specs=[pl.BlockSpec(memory_space=space)] * len(operands),
        out_specs=[pl.BlockSpec(memory_space=pltpu.VMEM)] * len(shapes),
        scratch_shapes=[
            pltpu.VMEM(shape, f32) if isinstance(shape, tuple) else shape for shape in scratch
        ],
        compiler_params=pltpu.CompilerParams(vmem_limit_bytes=16 * 2**20),
        cost_estimate=pl.CostEstimate(flops=cost, bytes_accessed=0, transcendentals=0),
    )(*operands)


def place():
    leaf, sep = lax.axis_index("leaf"), lax.axis_index("sep")
    return leaf, sep, lax.rem(leaf, 2), sep // 2, lax.rem(sep, 2)


def at(index, size):
    return pl.ds(pl.multiple_of(index * size, size), size)


def by_bit(bit, zero, one):
    return jnp.where(bit == 0, zero, one)


def per_device(
    leaf_source,
    leaf_inverse,
    leaf_update,
    row_lists,
    row_counts,
    separator_source,
    separator_inverse,
    separator_coupling,
):
    depth = row_counts.shape[1]
    source = leaf_source[0]
    inverse = leaf_inverse[0]
    update = jnp.swapaxes(leaf_update, 1, 2)[0]
    rows_source = separator_source[0]
    rows, columns = source.shape
    size = inverse.shape[1]
    updates = update.shape[1]
    capacity = updates // depth
    order = separator_inverse.shape[1]
    middle = order // 2
    packed_rows = middle // 2 + 8
    carried = middle + packed_rows
    list_rows = -(-depth // 8) * 8
    quarter = rows_source.shape[0]
    half = columns // 2
    block = columns // 8
    width = updates + 2 * quarter
    leaves = lax.axis_size("leaf")

    near = swap(source, 0, 1)
    update_near = swap(update, 0, 1)
    inverse_near = swap(inverse, 0, 1)
    rows_near = swap(rows_source, 0, 1)

    def own_columns_of(source_ref, out_ref):
        near_bit = place()[4]
        out_ref[...] = by_bit(near_bit, source_ref[:, :half], source_ref[:, half:])

    def chip_source(own_ref, near_ref, out_ref):
        near_bit = place()[4]
        out_ref[at(near_bit, rows)] = own_ref[...]
        out_ref[at(1 - near_bit, rows)] = by_bit(near_bit, near_ref[:, :half], near_ref[:, half:])

    (own_source,) = stage(own_columns_of, [(rows, half)], source)
    near, own_source = after(near, own_source)
    (chip,) = stage(chip_source, [(2 * rows, half)], own_source, near)
    far = swap(chip, 0, 2)

    def operators(coupling_ref, inverse, lists, out_ref, packed, square):
        near_bit = place()[4]
        out_ref[:middle] = dot3(coupling_ref[at(near_bit, middle)], inverse[...])
        square[...] = dot3(inverse[...], inverse[...], 0, 0)
        row = lax.broadcasted_iota(jnp.int32, (middle, middle), 0)
        lane = lax.broadcasted_iota(jnp.int32, (middle, middle), 1)
        last = square[middle:, middle:]
        packed[:middle, :middle] = jnp.where(row >= lane, square[:middle, :middle], last)
        packed[:middle, middle:] = square[middle:, :middle]
        packed[middle:] = jnp.zeros((2 * packed_rows - middle, order), f32)
        packed[middle : middle + 1, :middle] = jnp.sum(jnp.where(row == lane, last, 0.0), 0, keepdims=True)
        out_ref[middle:carried] = packed[at(near_bit, packed_rows)]
        out_ref[carried:] = jnp.full((list_rows, order), -1.0, f32)
        slot = lax.broadcasted_iota(jnp.int32, (1, capacity), 1)
        for level in range(depth):
            names = lists[:, level * capacity : (level + 1) * capacity]
            live = slot < lists[:, updates + level : updates + level + 1]
            out_ref[carried + level : carried + level + 1, :capacity] = jnp.where(live, names, -1).astype(f32)

    chip, coupling, own_inverse = after(chip, separator_coupling[0], separator_inverse[0])
    names_and_counts = jnp.concatenate([row_lists, row_counts], 1)
    (payload,) = stage(
        operators,
        [(carried + list_rows, order)],
        coupling,
        own_inverse,
        names_and_counts,
        scratch=[(2 * packed_rows, order), (order, order)],
        cost=3 * medium,
    )

    def own_part(inverse_ref, inverse_near_ref, update_ref, update_near_ref, chip_ref, y_ref, block_ref, far_ref, mine_ref, update_out_ref, all_ref):
        _, _, _, far_bit, near_bit = place()
        own, other = at(near_bit, rows), at(1 - near_bit, rows)
        all_ref[own] = inverse_ref[...]
        all_ref[other] = inverse_near_ref[...]
        update_out_ref[own] = update_ref[...]
        update_out_ref[other] = update_near_ref[...]
        whole = all_ref[...]
        first, second = whole[:, : 2 * rows], whole[:, 2 * rows :]
        far_ref[...] = by_bit(far_bit, second, first)
        y_ref[...] = dot3(by_bit(far_bit, first, second), chip_ref[...])
        chip_block = by_bit(far_bit, first, second)
        block_ref[...] = chip_block
        mine_ref[...] = by_bit(near_bit, chip_block[:, :rows], chip_block[:, rows:])

    received = swap(payload, 1, 0)
    inverse_near, payload = after(inverse_near, payload)
    own_y, inverse_chip, inverse_far, inverse_mine, update_all = stage(
        own_part,
        [(2 * rows, half), (2 * rows, 2 * rows), (2 * rows, 2 * rows), (2 * rows, rows), (2 * rows, updates)],
        inverse,
        inverse_near,
        update,
        update_near,
        chip,
        scratch=[(2 * rows, size)],
    )

    def turned_update(far_ref, mine_ref, update_ref, y_ref, turned_far_ref, turned_mine_ref, terms_ref):
        update = update_ref[...]
        turned_far_ref[...] = dot3(far_ref[...], update, 0, 0)
        turned_mine_ref[...] = dot3(mine_ref[...], update, 0, 0)
        terms_ref[...] = dot3(y_ref[...], update, 0, 0)

    turned_far, own_sum, own_terms = stage(
        turned_update,
        [(2 * rows, updates), (rows, updates), (half, updates)],
        inverse_far,
        inverse_mine,
        update_all,
        own_y,
    )

    def turned_rows(rows_ref, rows_near_ref, out_ref):
        near_bit = place()[4]
        turned, turned_near = jnp.transpose(rows_ref[...]), jnp.transpose(rows_near_ref[...])
        turned = by_bit(near_bit, turned[:half], turned[half:])
        turned_near = by_bit(near_bit, turned_near[:half], turned_near[half:])
        out_ref[...] = by_bit(
            near_bit,
            jnp.concatenate([turned, turned_near], 1),
            jnp.concatenate([turned_near, turned], 1),
        )

    rows_near, own_terms = after(rows_near, own_terms)
    (turned,) = stage(turned_rows, [(half, 2 * quarter)], rows_source, rows_near)
    far, turned = after(far, turned)

    def leaf_part(own_ref, turned_far_ref, far_ref, turned_ref, *refs):
        _, _, odd, far_bit, _ = place()
        out_refs, terms = refs[:-1], refs[-1]
        terms[...] = own_ref[...] + dot3(far_ref[...], turned_far_ref[...], 0, 0)
        for flip, out_ref in enumerate(out_refs):
            part = at((2 * odd + far_bit) ^ flip, block)
            out_ref[:, :updates] = terms[part]
            out_ref[:, updates:] = turned_ref[part]

    mine, to_far, to_odd, to_both = stage(
        leaf_part,
        [(block, width)] * 4,
        own_terms,
        turned_far,
        far,
        turned,
        scratch=[(half, updates)],
    )
    by_both = swap(to_both, 1, 2)
    by_far = swap(to_far, 0, 2)
    by_odd = swap(to_odd, 1, 0)

    def forward(level):
        def body(carry_ref, received_ref, half_ref, next_ref):
            upper = lax.rem(place()[0] // 2 ** (level - 1), 2) == 1
            carry, received = carry_ref[:carried], received_ref[:carried]
            half_ref[...] = jnp.where(upper, carry, received)
            next_ref[...] = jnp.where(upper, received, carry)

        return body

    def last_forward(carry_ref, received_ref, half_ref, root_ref):
        part = place()[0] // (leaves // 4)
        carry, received = carry_ref[...], received_ref[...]
        half_ref[...] = jnp.where(lax.rem(part, 2) == 1, carry, received)
        root_ref[...] = jnp.where(part == 1, received[middle:], carry[middle:])

    def root_half(root_ref, received_ref, out_ref):
        part = place()[0] // (leaves // 4)
        inner = jnp.logical_or(part == 1, part == 2)
        out_ref[...] = jnp.where(inner, root_ref[...], received_ref[...])

    received, mine = after(received, mine)
    new_half, carry = stage(forward(1), [(carried, order)] * 2, payload, received)
    halves, halves_near = [new_half], [swap(new_half, 0, 1)]
    for level in range(2, depth - 1):
        reached = swap(carry, 2 ** (level - 1), 0)
        new_half, carry = stage(forward(level), [(carried, order)] * 2, carry, reached)
        halves.append(new_half)
        halves_near.append(swap(new_half, 0, 1))
    reached = quarter_swap(carry, ((1, 0), (3, 2), (2, 1)))

    def one_hots(own_ref, other_ref, hot_ref):
        rows_of_node = lax.broadcasted_iota(jnp.int32, (order, capacity), 0)
        for level in range(depth):
            for index, ref in enumerate((own_ref, other_ref)):
                names = ref[carried + level : carried + level + 1, :capacity].astype(jnp.int32)
                hot = jnp.where(rows_of_node == names, 1.0, 0.0).astype(bf16)
                hot_ref[level, :, index * capacity : (index + 1) * capacity] = hot

    carry, payload = after(carry, payload)
    (hots,) = stage(
        one_hots, [jax.ShapeDtypeStruct((depth, order, 2 * capacity), bf16)], payload, received
    )

    def transposed(inverse_far_ref, own_y_ref, far_ref, turned_far_ref, y_ref, out_ref):
        near_bit = place()[4]
        inverse_far = inverse_far_ref[...]
        leaf_y = own_y_ref[...] + dot3(inverse_far, far_ref[...])
        y_ref[...] = leaf_y
        turned_y = dot3(inverse_far, leaf_y, 0, 0)
        out_ref[:, :updates] = turned_far_ref[at(near_bit, rows)]
        out_ref[:, updates : updates + half] = turned_y[:rows]
        out_ref[:, updates + half :] = turned_y[rows:]

    own_y, hots = after(own_y, hots)
    leaf_y, far_sum = stage(
        transposed,
        [(2 * rows, half), (rows, updates + columns)],
        inverse_far,
        own_y,
        far,
        turned_far,
    )
    by_both, by_far, by_odd, leaf_y = after(by_both, by_far, by_odd, leaf_y)

    def gathered_part(mine_ref, far_ref, odd_ref, both_ref, hot_ref, residual_ref, up_ref):
        leaf, _, odd, far_bit, _ = place()

        def joined(one, two):
            first, second = one[:, updates:], two[:, updates:]
            ordered = by_bit(
                far_bit,
                jnp.concatenate([first, second], 1),
                jnp.concatenate([second, first], 1),
            )
            return one[:, :updates] + two[:, :updates], ordered

        total, own_source = joined(mine_ref[...], far_ref[...])
        total_other, other_source = joined(odd_ref[...], both_ref[...])
        odd_source = by_bit(odd, other_source, own_source)
        even_source = by_bit(odd, own_source, other_source)
        for level in range(1, depth + 1):
            part = slice((level - 1) * capacity, level * capacity)
            both = jnp.concatenate([total[:, part], total_other[:, part]], 1)
            gathered = hot_dot(both, hot_ref[level - 1], 1)
            if level == 1:
                residual_ref[...] = odd_source - gathered
            else:
                here = lax.rem(leaf - odd, 2**level) == 2 ** (level - 1)
                slot = jnp.where(here, even_source, 0.0) - gathered
                up_ref[:, (level - 2) * order : (level - 1) * order] = slot

    residual, slots = stage(
        gathered_part,
        [(block, order), (block, (depth - 1) * order)],
        mine,
        by_far,
        by_odd,
        by_both,
        hots,
        cost=3*medium,
    )
    residuals = [residual]

    def operator_of(half_ref, near_ref):
        near_bit = place()[4]
        own, other = half_ref[:middle], near_ref[:middle]
        return jnp.concatenate([by_bit(near_bit, own, other), by_bit(near_bit, other, own)], 0)

    def push(slots_ref, residual_ref, half_ref, near_ref, out_ref):
        taken = dot3(residual_ref[...], operator_of(half_ref, near_ref), 1, 1)
        out_ref[:, :order] = slots_ref[:, :order] - taken
        if out_ref.shape[1] > order:
            out_ref[:, order:] = slots_ref[:, order:]

    def squared(residual, own, other):
        near_bit = place()[4]
        row = lax.broadcasted_iota(jnp.int32, (middle, middle), 0)
        lane = lax.broadcasted_iota(jnp.int32, (middle, middle), 1)
        packed = jnp.concatenate([by_bit(near_bit, own, other), by_bit(near_bit, other, own)], 0)
        both, below = packed[:middle, :middle], packed[:middle, middle:]
        lower, upper = jnp.where(row > lane, both, 0.0), jnp.where(row < lane, both, 0.0)
        first = jnp.where(row >= lane, both, 0.0)
        last = jnp.where(row == lane, packed[middle : middle + 1, :middle], upper)
        one, two = residual[:, :middle], residual[:, middle:]
        return jnp.concatenate(
            [
                dot3(one, first) + dot3(one, lower, 1, 1) + dot3(two, below),
                dot3(one, below, 1, 1) + dot3(two, last) + dot3(two, upper, 1, 1),
            ],
            1,
        )

    def alone(residual_ref, half_ref, near_ref, out_ref, down_ref):
        down_ref[...] = operator_of(half_ref, near_ref)
        out_ref[...] = squared(residual_ref[...], half_ref[middle:], near_ref[middle:])

    def below_root(*refs):
        count = depth - 1
        partial_refs, down_refs = refs[:count], refs[count : 2 * count]
        base_ref, high_ref, low_ref = refs[2 * count :]
        base, taken = partial_refs[-1][...], -down_refs[-1][...]
        for level in range(depth - 1, 0, -1):
            if level < depth - 1:
                down = down_refs[level - 1][...]
                base = partial_refs[level - 1][...] - dot3(base, down)
                taken = -dot3(taken, down)
            part = slice((level - 1) * order, level * order)
            base_ref[:, part] = base
            high_ref[:, part], low_ref[:, part] = pieces_of(taken)

    def level_sum(up_ref, partner_ref, residual_ref, rest_ref):
        total = up_ref[...] + partner_ref[...]
        residual_ref[...] = total[:, :order]
        rest_ref[...] = total[:, order:]

    partials, downs = [], []
    halves_near[0], residual, slots = after(halves_near[0], residual, slots)
    (going_up,) = stage(
        push, [(block, (depth - 1) * order)], slots, residual, halves[0], halves_near[0]
    )
    for level in range(2, depth):
        partner = swap(going_up, 2 ** (level - 1), 0)
        if level == depth - 1:
            reached, going_up = after(reached, going_up)
            new_half, root = stage(
                last_forward, [(carried, order), (packed_rows, order)], carry, reached
            )
            halves.append(new_half)
            from_far = swap(far_sum, 0, 2)
            halves_near.append(swap(new_half, 0, 1))
            by_root = swap(root, leaves // 4, 0)
        residual, slots = stage(
            level_sum,
            [(block, order), (block, (depth - level) * order)],
            going_up,
            partner,
            cost=2 * medium,
        )
        residuals.append(residual)
        halves_near[level - 1], residual, slots = after(halves_near[level - 1], residual, slots)
        (going_up,) = stage(
            push,
            [(block, (depth - level) * order)],
            slots,
            residual,
            halves[level - 1],
            halves_near[level - 1],
        )
    partner = swap(going_up, 2 ** (depth - 1), 0)

    for level in range(1, depth):
        residual, going_up = after(residuals[level - 1], going_up)
        partial, down = stage(
            alone,
            [(block, order), (order, order)],
            residual,
            halves[level - 1],
            halves_near[level - 1],
        )
        partials.append(partial)
        downs.append(down)
    by_root, partial = after(by_root, partial)
    (root,) = stage(root_half, [(packed_rows, order)], root, by_root)
    root_near = swap(root, 0, 1)
    partials[-1], root = after(partials[-1], root)
    pieces = jax.ShapeDtypeStruct((order, (depth - 1) * order), bf16)
    base, taken_high, taken_low = stage(
        below_root, [(block, (depth - 1) * order), pieces, pieces], *partials, *downs
    )
    partner, root, base = after(partner, root, base)

    def root_sum(up_ref, partner_ref, out_ref):
        out_ref[...] = up_ref[...] + partner_ref[...]

    (residual,) = stage(root_sum, [(block, order)], going_up, partner, cost=medium)
    root_near, residual = after(root_near, residual)

    def way_down(residual_ref, root_ref, root_near_ref, hot_ref, base_ref, high_ref, low_ref, *out_refs):
        leaf, _, odd, far_bit, _ = place()
        top = squared(residual_ref[...], root_ref[...], root_near_ref[...])
        high, low = pieces_of(top)
        large = product(jnp.concatenate([high, low], 0), high_ref[...], 1, 0)
        small = large[block:] + product(high, low_ref[...], 1, 0)
        under = base_ref[...] + (large[:block] + small)
        solved = [under[:, level * order : (level + 1) * order] for level in range(depth - 1)]
        solved.append(top)
        even_solved = jnp.zeros_like(solved[0])
        for level in range(2, depth + 1):
            here = lax.rem(leaf - odd, 2**level) == 2 ** (level - 1)
            even_solved = jnp.where(here, solved[level - 1], even_solved)
        own_solved = by_bit(odd, even_solved, solved[0])
        other_solved = by_bit(odd, solved[0], even_solved)
        for flip, out_ref in enumerate(out_refs):
            rows_of = other_solved if flip >= 2 else own_solved
            out_ref[:, updates:] = by_bit(
                far_bit ^ (flip % 2), rows_of[:, : 2 * quarter], rows_of[:, 2 * quarter :]
            )
        for level in range(depth):
            picked = hot_dot(solved[level], hot_ref[level], 0)
            for flip, out_ref in enumerate(out_refs):
                side = flip // 2
                out_ref[:, level * capacity : (level + 1) * capacity] = picked[
                    :, side * capacity : (side + 1) * capacity
                ]

    stay, to_far, to_odd, to_both = stage(
        way_down,
        [(block, width)] * 4,
        residual,
        root,
        root_near,
        hots,
        base,
        taken_high,
        taken_low,
    )
    both = swap(to_both, 1, 2)
    beyond = swap(to_far, 0, 2)
    side = swap(to_odd, 1, 0)

    def last_left(own_ref, chip_ref, y_ref, far_ref, high_ref, low_ref, keep_ref, pass_ref, left_ref):
        near_bit = place()[4]
        left_ref[:rows, :updates] = -(own_ref[...] + far_ref[:, :updates])
        left_ref[:rows, updates:] = jnp.zeros((rows, 2 * quarter), f32)
        row = lax.broadcasted_iota(jnp.int32, (quarter, width), 0)
        lane = lax.broadcasted_iota(jnp.int32, (quarter, width), 1)
        left_ref[rows:] = jnp.where(lane == updates + near_bit * quarter + row, 1.0, 0.0)
        high_ref[...], low_ref[...] = pieces_of(left_ref[...])
        turned_y = dot3(chip_ref[...], y_ref[...], 0, 0)
        first = turned_y[:rows] + far_ref[:, updates : updates + half]
        second = turned_y[rows:] + far_ref[:, updates + half :]
        keep_ref[...] = by_bit(near_bit, first, second)
        pass_ref[...] = by_bit(near_bit, second, first)

    from_far, stay = after(from_far, stay)
    left_pieces = jax.ShapeDtypeStruct((rows + quarter, width), bf16)
    left, left_low, base_keep, base_pass = stage(
        last_left, [left_pieces, left_pieces, (rows, half), (rows, half)], own_sum, inverse_chip, leaf_y, from_far, scratch=[(rows + quarter, width)]
    )
    both, beyond, side, left = after(both, beyond, side, left)

    def grouped(*refs):
        _, _, odd, far_bit, _ = place()
        out_ref = refs[-1]
        for flip, ref in enumerate(refs[:-1]):
            out_ref[at((2 * odd + far_bit) ^ flip, block)] = ref[...]

    (group,) = stage(grouped, [(half, width)], stay, beyond, side, both)
    base_near = swap(base_pass, 0, 1)
    group_near = swap(group, 0, 1)

    def last_product(high_ref, low_ref, group_ref):
        high, low = pieces_of(group_ref[...])
        small = product(high_ref[...], low, 1, 1) + product(low_ref[...], high, 1, 1)
        return product(high_ref[...], high, 1, 1) + small

    def own_columns(high_ref, low_ref, group_ref, out_ref):
        out_ref[...] = last_product(high_ref, low_ref, group_ref)

    (ours,) = stage(own_columns, [(rows + quarter, half)], left, left_low, group)
    group_near, ours = after(group_near, ours)

    def finish(high_ref, low_ref, group_ref, ours_ref, base_ref, base_near_ref, leaf_ref, rows_ref):
        near_bit = place()[4]
        ours = ours_ref[...]
        theirs = last_product(high_ref, low_ref, group_ref)
        ours_x, theirs_x = base_ref[...] + ours[:rows], base_near_ref[...] + theirs[:rows]
        leaf_ref[:, :half] = by_bit(near_bit, ours_x, theirs_x)
        leaf_ref[:, half:] = by_bit(near_bit, theirs_x, ours_x)
        rows_ref[:, :half] = by_bit(near_bit, ours[rows:], theirs[rows:])
        rows_ref[:, half:] = by_bit(near_bit, theirs[rows:], ours[rows:])

    leaf_x, separator_rows = stage(
        finish,
        [(rows, columns), (quarter, columns)],
        left,
        left_low,
        group_near,
        ours,
        base_keep,
        base_near,
    )
    return (leaf_x[None], separator_rows[None])


def solution(mesh):
    placed = (
        P("leaf", "sep", None),
        P("leaf", "sep", None),
        P("leaf", None, "sep"),
        P("leaf", None),
        P("leaf", None),
        P("leaf", "sep", None),
        P("leaf", None, None),
        P("leaf", None, None),
    )
    return jax.shard_map(
        per_device,
        mesh=mesh,
        in_specs=placed,
        out_specs=(P("leaf", "sep", None), P("leaf", "sep", None)),
        check_vma=False,
    )
```
